32 devices in a mesh: dp: 8 (over z, x), mp: 4 (over y, core).
Axes of the slice: x: 2, y: 2, z: 4, core: 2. Of those that a mesh axis runs over, the one named last changes fastest.
Arguments:
- tokens: bfloat16 [16384, 512], P('dp'), may hold values from -6 to 6
- cotangent: bfloat16 [16384, 512], P('dp'), may hold values from -6 to 6
- memory_init: bfloat16 [20, 512], P(None, ('dp', 'mp')), may hold values from -6 to 6
- query_weight: bfloat16 [512, 512], P(('dp', 'mp')), may hold values from -0.25 to 0.25
- key_weight: bfloat16 [512, 512], P(('dp', 'mp')), may hold values from -0.25 to 0.25
- value_weight: bfloat16 [512, 512], P(('dp', 'mp')), may hold values from -0.25 to 0.25
- output_weight: bfloat16 [512, 512], P(('dp', 'mp')), may hold values from -2 to 2
- first_gain: bfloat16 [512], P(('dp', 'mp')), may hold values from 0.5 to 1.5
- first_bias: bfloat16 [512], P(('dp', 'mp')), may hold values from -2 to 2
- inner_weight: bfloat16 [512, 2048], P(None, 'mp'), may hold values from -0.25 to 0.25
- inner_bias: bfloat16 [2048], P('mp'), may hold values from -3 to 3
- outer_weight: bfloat16 [2048, 512], P('mp'), may hold values from -0.125 to 0.125
- outer_bias: bfloat16 [512], P(('dp', 'mp')), may hold values from -3 to 3
- second_gain: bfloat16 [512], P(('dp', 'mp')), may hold values from 0.5 to 1.5
- second_bias: bfloat16 [512], P(('dp', 'mp')), may hold values from -2 to 2
Outputs:
- layer_out: bfloat16 [16384, 512], P('dp')
- grad_tokens: bfloat16 [16384, 512], P('dp')
- grad_memory: float32 [20, 512], P(None, ('dp', 'mp'))
- grad_query: float32 [512, 512], P(('dp', 'mp'))
- grad_key: float32 [512, 512], P(('dp', 'mp'))
- grad_value: float32 [512, 512], P(('dp', 'mp'))
- grad_output: float32 [512, 512], P(('dp', 'mp'))
- grad_first_gain: float32 [512], P(('dp', 'mp'))
- grad_first_bias: float32 [512], P(('dp', 'mp'))
- grad_inner: float32 [512, 2048], P(None, 'mp')
- grad_inner_bias: float32 [2048], P('mp')
- grad_outer: float32 [2048, 512], P('mp')
- grad_outer_bias: float32 [512], P(('dp', 'mp'))
- grad_second_gain: float32 [512], P(('dp', 'mp'))
- grad_second_bias: float32 [512], P(('dp', 'mp'))
The draws below stay inside these ranges and needn't reach their ends.
All inputs are finite; a program needn't handle non-finite values.
Results may differ from the reference program's by a relative error of at most 0.019.
Values may be sent and summed in bfloat16 or wider, within the bound.
No kernel may reach another device: no remote copies, remote signals or barrier semaphores. Data moves between devices by JAX's collectives and lax.ppermute only.
A program may use at most 192 MiB of HBM per device.

```python
import jax
import jax.numpy as jnp
from jax import lax

D = 512
HEADS = 8
HEAD = 64
FF = 2048
MEM = 20
SPAN = 512
SPANS = 2
TOKENS = 16384


def shard_levels(key, extent, shards, least, largest):
    factor_of, own = 1.0, jax.random.fold_in(key, 6)
    for position, parts in shards:
        draws = jnp.exp(jax.random.uniform(jax.random.fold_in(own, position), (parts,), jnp.float32, least / len(shards), largest / len(shards)))
        factor_of = factor_of * jnp.repeat(draws, extent[position] // parts).reshape([-1 if axis == position else 1 for axis in range(len(extent))])
    return factor_of


def gaussian(key, shape, deviation, limit, split=(), held_as=jnp.bfloat16):
    array = jax.random.normal(key, shape, jnp.float32) * deviation
    if len(split) > 0:
        array = shard_levels(key, shape, split, -0.22, 0.18) * array
    return jnp.clip(array, min=-limit, max=limit).astype(held_as)


def setup_inputs(seed: int = 0) -> dict:
    key_of = jax.random.split(jax.random.key(seed), 16)
    tokens = gaussian(key_of[0], (TOKENS, D), 1.0, 6.0, ((0, 8),))
    cotangent = gaussian(key_of[1], (TOKENS, D), 1.0, 6.0, ((0, 8),))
    memory_init = gaussian(key_of[2], (MEM, D), 1.0, 6.0, ((1, 32),))
    query_weight = gaussian(key_of[3], (D, D), D ** -0.5, 0.25, ((0, 32),))
    key_weight = gaussian(key_of[4], (D, D), D ** -0.5, 0.25, ((0, 32),))
    value_weight = gaussian(key_of[5], (D, D), D ** -0.5, 0.25, ((0, 32),))
    output_weight = gaussian(key_of[6], (D, D), (D // 64) ** -0.5, 2.0, ((0, 32),))
    first_gain = jnp.clip(1.0 + 0.1 * jax.random.normal(key_of[7], (D,), jnp.float32), 0.5, 1.5).astype(jnp.bfloat16)
    first_bias = gaussian(key_of[8], (D,), 0.3, 2.0, ((0, 32),))
    inner_weight = gaussian(key_of[9], (D, FF), D ** -0.5, 0.25, ((1, 4),))
    inner_bias = gaussian(key_of[10], (FF,), 0.5, 3.0, ((0, 4),))
    outer_weight = gaussian(key_of[11], (FF, D), FF ** -0.5, 0.125, ((0, 4),))
    outer_bias = gaussian(key_of[12], (D,), 0.5, 3.0, ((0, 32),))
    second_gain = jnp.clip(1.0 + 0.1 * jax.random.normal(key_of[13], (D,), jnp.float32), 0.5, 1.5).astype(jnp.bfloat16)
    second_bias = gaussian(key_of[14], (D,), 0.3, 2.0, ((0, 32),))
    return {"tokens": tokens, "cotangent": cotangent, "memory_init": memory_init, "query_weight": query_weight, "key_weight": key_weight, "value_weight": value_weight, "output_weight": output_weight, "first_gain": first_gain, "first_bias": first_bias, "inner_weight": inner_weight, "inner_bias": inner_bias, "outer_weight": outer_weight, "outer_bias": outer_bias, "second_gain": second_gain, "second_bias": second_bias}


@jax.custom_vjp
def low(v):
    return lax.optimization_barrier(v.astype(jnp.bfloat16)).astype(jnp.float32)

@jax.custom_vjp
def low_back(v):
    return v

def low_keep(v):
    return (low(v), None)

def low_pass(kept, grad):
    return (grad,)

def back_keep(v):
    return (v, None)

def back_low(kept, grad):
    return (low(grad),)
low.defvjp(low_keep, low_pass)
low_back.defvjp(back_keep, back_low)
highest = lax.Precision.HIGHEST
norm_eps = 1e-05

def matmul(operand, other):
    return jnp.dot(operand, other, precision=highest)

def layer_norm(values, scales, shifts):
    center = values - lax.optimization_barrier(jnp.mean(values, axis=-1, keepdims=True))
    spread = lax.optimization_barrier(jnp.mean(center * center, axis=-1, keepdims=True))
    return center * lax.rsqrt(spread + norm_eps) * scales + shifts

def span_forward(joined, params):
    query_weight, key_weight, value_weight, output_weight, first_gain, first_bias, inner_weight, inner_bias, outer_weight, outer_bias, second_gain, second_bias = params
    row_count = joined.shape[0]
    joined_low = low(joined)
    queries = low_back(low(matmul(joined_low, query_weight))).reshape(row_count, HEADS, HEAD)
    key_rows = low_back(low(matmul(joined_low, key_weight))).reshape(row_count, HEADS, HEAD)
    value_rows = low_back(low(matmul(joined_low, value_weight))).reshape(row_count, HEADS, HEAD)
    scores = low_back(jnp.einsum('qhd,khd->hqk', queries, key_rows, precision=highest)) * HEAD ** (-0.5)
    attend = low(low_back(jax.nn.softmax(scores, axis=-1)))
    mixed_heads = jnp.einsum('hqk,khd->qhd', attend, value_rows, precision=highest).reshape(row_count, D)
    mixed_heads = low_back(low(mixed_heads))
    branch = low_back(matmul(mixed_heads, output_weight))
    normed = layer_norm(joined + branch, first_gain, first_bias)
    inner_act = low_back(matmul(low(normed), inner_weight) + inner_bias)
    hidden = low(jax.nn.gelu(inner_act))
    outer_act = low_back(matmul(hidden, outer_weight)) + outer_bias
    return layer_norm(normed + outer_act, second_gain, second_bias)

def reference(tokens, cotangent, memory_init, query_weight, key_weight, value_weight, output_weight, first_gain, first_bias, inner_weight, inner_bias, outer_weight, outer_bias, second_gain, second_bias):
    params = tuple((weight.astype(jnp.float32) for weight in (query_weight, key_weight, value_weight, output_weight, first_gain, first_bias, inner_weight, inner_bias, outer_weight, outer_bias, second_gain, second_bias)))
    memory = memory_init.astype(jnp.float32)
    documents = tokens.astype(jnp.float32).reshape(-1, SPANS, SPAN, D)
    cotangents = cotangent.astype(jnp.float32).reshape(-1, SPANS, SPAN, D)

    def one_document(totals, document_pair):
        document_rows, document_cot = document_pair
        carried = []
        current = memory
        for span_index in range(SPANS):
            carried.append(current)
            joined = jnp.concatenate([current, document_rows[span_index]], axis=0)
            current = span_forward(joined, params)[:MEM]

        def forward(weights, start_memory, block_rows):
            outputs = []
            for span_index in range(SPANS):
                memory_rows = start_memory if span_index == 0 else carried[span_index]
                joined = jnp.concatenate([memory_rows, block_rows[span_index]], axis=0)
                outputs.append(span_forward(joined, weights)[MEM:])
            return jnp.stack(outputs)
        outputs, pullback = jax.vjp(forward, params, memory, document_rows)
        grad_weights, grad_start, grad_rows = pullback(document_cot)
        totals = jax.tree.map(lambda augend, addend: augend + addend, totals, (grad_weights, grad_start))
        return (totals, (outputs, grad_rows))
    initial = jax.tree.map(jnp.zeros_like, (params, memory))
    totals, (outputs, grad_rows) = lax.scan(one_document, initial, (documents, cotangents))
    grad_weights, grad_start = totals
    return (outputs.reshape(-1, D).astype(jnp.bfloat16), grad_rows.reshape(-1, D).astype(jnp.bfloat16), grad_start, grad_weights[0], grad_weights[1], grad_weights[2], grad_weights[3], grad_weights[4], grad_weights[5], grad_weights[6], grad_weights[7], grad_weights[8], grad_weights[9], grad_weights[10], grad_weights[11])
```

```python
import functools

import jax
import jax.numpy as jnp
from jax import lax
from jax.experimental import pallas as pl
from jax.experimental.pallas import tpu as pltpu
from jax.sharding import PartitionSpec as P

D = 512
HEADS = 8
HEAD = 64
MEM = 20
PAD = 32
SPAN = 512
SPANS = 2
EXTRA = 128
WIDE = 4 * D + EXTRA
EPS = 1e-05
GELU_A = 0.7978845608028654
GELU_B = 0.044715
LOW = jnp.bfloat16
F32 = jnp.float32
SCALE = HEAD ** (-0.5)
ALL = ("dp", "mp")

VMEM = pl.BlockSpec(memory_space=pltpu.VMEM)
SMEM = pl.BlockSpec(memory_space=pltpu.SMEM)
ANY = pl.BlockSpec(memory_space=pl.ANY)


def dg(a, b, ca, cb):
    return lax.dot_general(a, b, (((ca,), (cb,)), ((), ())), preferred_element_type=F32)


def iota(shape, dim):
    return lax.broadcasted_iota(jnp.int32, shape, dim)


def head_mask():
    return (iota((HEADS * PAD, D), 0) >> 5) == (iota((HEADS * PAD, D), 1) >> 6)


def block_diagonal(rows):
    tall = jnp.concatenate([rows] * HEADS, axis=0)
    return jnp.where(head_mask(), tall, 0.0).astype(LOW)


def diagonal_sum(tall):
    kept = jnp.where(head_mask(), tall, 0.0)
    total = kept[:PAD]
    for h in range(1, HEADS):
        total = total + kept[h * PAD : (h + 1) * PAD]
    return total


def normalize(values):
    mean = jnp.mean(values, axis=1, keepdims=True)
    center = values - mean
    spread = jnp.mean(center * center, axis=1, keepdims=True)
    inv = lax.rsqrt(spread + EPS)
    return center * inv, inv


def gelu_parts(a):
    sq = a * a
    t = jnp.tanh(a * (GELU_A + (GELU_A * GELU_B) * sq))
    half = 0.5 * (1.0 + t)
    return half, t, sq


def gelu(a):
    half, _, _ = gelu_parts(a)
    return a * half


def call(kernel, out_shape, in_specs, out_specs, scratch=(), flops=0, bytes_=0):
    return pl.pallas_call(
        kernel,
        out_shape=out_shape,
        in_specs=in_specs,
        out_specs=out_specs,
        scratch_shapes=list(scratch),
        compiler_params=pltpu.CompilerParams(vmem_limit_bytes=56 * 2**20),
        cost_estimate=pl.CostEstimate(flops=flops, bytes_accessed=bytes_, transcendentals=0),
    )


def sds(shape, dtype):
    return jax.ShapeDtypeStruct(shape, dtype)


def pack_kernel(q_ref, k_ref, v_ref, o_ref, mem_ref, g1_ref, b1_ref, ob_ref, g2_ref, b2_ref, out_ref, tall):
    rows = q_ref.shape[0]
    for i, ref in enumerate((q_ref, k_ref, v_ref, o_ref)):
        out_ref[:, i * D : (i + 1) * D] = ref[...]
    tall[...] = jnp.zeros(tall.shape, F32)
    tall[:MEM, :rows] = mem_ref[...].astype(F32)
    for i, ref in enumerate((g1_ref, b1_ref, ob_ref, g2_ref, b2_ref)):
        tall[MEM + i : MEM + i + 1, :rows] = ref[...].astype(F32)
    out_ref[:, 4 * D :] = tall[...].T[:rows].astype(LOW)


def attend_kernel(bits, at_ref, *refs):
    n = len(bits)
    pieces = refs[:n]
    x_ref, x1_ref, w_ref, small_ref, nm_ref, qkv_ref, p_hbm, o_ref, m_ref, l_ref, wext, p_ref, sems = refs[n:]
    me = at_ref[0]
    for piece, offsets in zip(pieces, bits, strict=True):
        if offsets is None:
            wext[...] = piece[...]
            continue
        size = piece.shape[0] // len(offsets)
        for j, offset in enumerate(offsets):
            start = pl.multiple_of((me ^ offset) * size, size)
            wext[pl.ds(start, size), :] = piece[j * size : (j + 1) * size, :]
    w_ref[...] = wext[:, : 4 * D]
    small = wext[:, 4 * D :].T.astype(F32)[:PAD]
    small_ref[...] = small
    x_t = x_ref[...].T
    qkv_ref[:D] = (dg(wext[:, :D], x_t, 0, 0).astype(LOW).astype(F32) * SCALE).astype(LOW)
    qkv_ref[D : 3 * D] = dg(wext[:, D : 3 * D], x_t, 0, 0).astype(LOW)

    def scores(h):
        at = h * HEAD
        return dg(qkv_ref[D + at : D + at + HEAD], qkv_ref[at : at + HEAD], 0, 0)

    s_next = scores(0)
    copies = []
    for h in range(HEADS):
        s = s_next
        if h + 1 < HEADS:
            s_next = scores(h + 1)
        at = h * HEAD
        m = jnp.max(s, axis=0, keepdims=True)
        p = jnp.exp(s - m)
        m_ref[h : h + 1] = m
        l_ref[h : h + 1] = jnp.sum(p, axis=0, keepdims=True)
        p_ref[h] = p.astype(LOW)
        copy = pltpu.make_async_copy(p_ref.at[h], p_hbm.at[h], sems.at[h])
        copy.start()
        copies.append(copy)
        o_ref[at : at + HEAD] = dg(qkv_ref[2 * D + at : 2 * D + at + HEAD], p_ref[h], 1, 0)

    mem = jnp.where(iota((PAD, D), 0) < MEM, small, 0.0)
    packed = dg(mem.astype(LOW), wext[:, : 3 * D], 1, 0).astype(LOW)
    q_tall = block_diagonal(packed[:, :D].astype(F32) * SCALE)
    s_mem = dg(q_tall, packed[:, D : 2 * D], 1, 1)
    s_mem = jnp.where(iota(s_mem.shape, 1) < MEM, s_mem, -1e30)
    kv = dg(x1_ref[...], wext[:, D : 3 * D], 1, 0).astype(LOW)
    s = dg(q_tall, kv[:, :D], 1, 1)
    m = jnp.maximum(jnp.max(s, axis=1, keepdims=True), jnp.max(s_mem, axis=1, keepdims=True))
    p = jnp.exp(s - m)
    p_mem = jnp.exp(s_mem - m)
    total = jnp.sum(p, axis=1, keepdims=True) + jnp.sum(p_mem, axis=1, keepdims=True)
    o = dg(p.astype(LOW), kv[:, D:], 1, 0) + dg(p_mem.astype(LOW), packed[:, 2 * D :], 1, 0)
    mixed = diagonal_sum(o / total).astype(LOW)
    xhat, _ = normalize(mem + dg(mixed, wext[:, 3 * D : 4 * D], 1, 0))
    nm_ref[...] = xhat * small[20:21] + small[21:22]
    for copy in copies:
        copy.wait()


def forward_kernel(
    at_ref, nm_ref, small_ref, x_ref, w_ref, qkv_ref, o_ref, m_ref, l_ref,
    wi0, wi1, wi2, wi3, wo0, wo1, wo2, wo3, bi_ref, cot_ref,
    out_ref, keep_ref, send_ref, slope_ref, nl_ref, gl_ref, gs_ref, xhat_ref, inv_ref,
    mixed_ref, mem_ref, pm_ref, c_ref, cm_ref, vec_ref, hid,
):
    wis, wos = (wi0, wi1, wi2, wi3), (wo0, wo1, wo2, wo3)
    small = small_ref[...]
    gain1, bias1, outer_b, gain2, bias2 = (small[MEM + i : MEM + i + 1] for i in range(5))
    later, first = at_ref[2], at_ref[5]
    nm = nm_ref[...]
    nm_low = nm.astype(LOW)
    value = nm + outer_b
    for k in range(4):
        inner = dg(nm_low, wis[k][...], 1, 0) + bi_ref[k : k + 1]
        value = value + dg(gelu(inner).astype(LOW), wos[k][...], 1, 0)
    carried, _ = normalize(value)
    carried = carried * gain2 + bias2
    mem = jnp.where(later == 1, carried, small)
    mem = jnp.where(iota((PAD, D), 0) < MEM, mem, 0.0)
    mem_ref[...] = mem
    kv_mem = dg(mem.astype(LOW), w_ref[:, D : 3 * D], 1, 0).astype(LOW).astype(F32)
    k_tall = block_diagonal(kv_mem[:, :D])
    v_tall = block_diagonal(kv_mem[:, D:])
    s_all = dg(k_tall, qkv_ref[:D], 1, 0)
    s_all = jnp.where((iota(s_all.shape, 0) & (PAD - 1)) < MEM, s_all, -1e30)
    alphas, invs = [], []
    for h in range(HEADS):
        s = s_all[h * PAD : (h + 1) * PAD]
        m_old = m_ref[h : h + 1]
        m = jnp.maximum(m_old, jnp.max(s, axis=0, keepdims=True))
        alpha = jnp.exp(m_old - m)
        p = jnp.exp(s - m)
        inv = 1.0 / (l_ref[h : h + 1] * alpha + jnp.sum(p, axis=0, keepdims=True))
        pm_ref[h * PAD : (h + 1) * PAD] = p.astype(LOW)
        c_ref[h : h + 1] = alpha * inv
        cm_ref[h : h + 1] = inv
        alphas.append(alpha * inv)
        invs.append(inv)
    o_mem = dg(v_tall, pm_ref[...], 0, 0)
    for h in range(HEADS):
        at = h * HEAD
        mixed_ref[at : at + HEAD] = (
            o_ref[at : at + HEAD] * alphas[h] + o_mem[at : at + HEAD] * invs[h]
        ).astype(LOW)
    xhat1, inv1 = normalize(
        x_ref[...].astype(F32) + dg(mixed_ref[...], w_ref[:, 3 * D : 4 * D], 0, 0)
    )
    xhat_ref[...] = xhat1
    inv_ref[...] = inv1
    normed = xhat1 * gain1 + bias1
    normed_low = normed.astype(LOW)
    nl_ref[...] = normed_low
    total = normed + outer_b
    for k in range(4):
        a = dg(normed_low, wis[k][...], 1, 0) + bi_ref[k : k + 1]
        half, t, sq = gelu_parts(a)
        hid[k] = (a * half).astype(LOW)
        slope = half + (0.5 * a) * (1.0 - t * t) * (GELU_A + (3.0 * GELU_A * GELU_B) * sq)
        slope_ref[k] = slope.astype(LOW)
        total = total + dg(hid[k], wos[k][...], 1, 0)
    xhat2, inv2 = normalize(total)
    out_ref[...] = (xhat2 * gain2 + bias2).astype(LOW)
    cot = cot_ref[...].astype(F32)
    pull = cot * gain2
    grad_sum = inv2 * (
        pull
        - jnp.mean(pull, axis=1, keepdims=True)
        - xhat2 * jnp.mean(pull * xhat2, axis=1, keepdims=True)
    )
    vec_ref[2:3] = jnp.sum(grad_sum, axis=0, keepdims=True)
    vec_ref[3:4] = jnp.sum(cot * xhat2, axis=0, keepdims=True)
    vec_ref[4:5] = jnp.sum(cot, axis=0, keepdims=True)
    gs_ref[...] = grad_sum
    grad_low = grad_sum.astype(LOW)
    gl_ref[...] = grad_low
    for k in (1, 3, 0, 2):
        give(send_ref if k % 2 else keep_ref, k // 2, dg(hid[k], grad_low, 0, 0), first)


def give(ref, k, rows, first):
    size = rows.shape[0] // 4
    for i in range(4):
        ref[k, first ^ i] = rows[i * size : (i + 1) * size].astype(LOW)


def middle_kernel(
    at_ref, small_ref, w_ref, wi0, wi1, wi2, wi3, wo0, wo1, wo2, wo3, slope_ref, nl_ref, gl_ref, gs_ref, xhat_ref, inv_ref,
    mixed_ref, keep_ref, send_ref, resid_ref, dwo_ref, gmix_ref, vec_ref,
):
    wis, wos = (wi0, wi1, wi2, wi3), (wo0, wo1, wo2, wo3)
    first = at_ref[5]
    back = gs_ref[...]
    grad_low = gl_ref[...]
    extra = jnp.zeros((PAD - 8, D), F32)
    for k in (1, 3, 0, 2):
        gi = slope_ref[k].astype(F32) * dg(grad_low, wos[k][...], 1, 1)
        gi_low = gi.astype(LOW)
        bias = jnp.sum(gi_low.astype(F32), axis=0, keepdims=True)
        bias = jnp.where(iota((8, D), 0) == 0, bias, 0.0)
        rows = jnp.concatenate([dg(nl_ref[...], gi_low, 0, 0), bias, extra], axis=0)
        give(send_ref if k % 2 else keep_ref, k // 2, rows, first)
        back = back + dg(gi_low, wis[k][...], 1, 1)
    xhat1 = xhat_ref[...]
    vec_ref[0:1] = jnp.sum(back * xhat1, axis=0, keepdims=True)
    vec_ref[1:2] = jnp.sum(back, axis=0, keepdims=True)
    pull = back * small_ref[MEM : MEM + 1]
    resid = inv_ref[...] * (
        pull
        - jnp.mean(pull, axis=1, keepdims=True)
        - xhat1 * jnp.mean(pull * xhat1, axis=1, keepdims=True)
    )
    resid_ref[...] = resid
    resid_low = resid.astype(LOW)
    dwo_ref[...] = dg(mixed_ref[...], resid_low, 1, 0).astype(LOW)
    gmix_ref[...] = dg(w_ref[:, 3 * D : 4 * D], resid_low, 1, 1).astype(LOW)


def backward_kernel(
    bits, at_ref, x_ref, w_ref, qkv_ref, p_hbm, pm_ref, mixed_ref, c_ref, cm_ref, gmix_ref, mem_ref, resid_ref,
    dwo_ref, vec_ref, vec1_ref, *rest,
):
    g_refs, (tok_ref, p_ref, sems, gp, do_m, ds_m, wext) = rest[: len(bits)], rest[len(bits) :]
    me = at_ref[0]
    copies = [pltpu.make_async_copy(p_hbm.at[h], p_ref.at[h], sems.at[h]) for h in range(HEADS)]
    for copy in copies:
        copy.start()
    mem_low = mem_ref[...].astype(LOW)
    kv_mem = dg(mem_low, w_ref[:, D : 3 * D], 1, 0).astype(LOW).astype(F32)
    k_tall = block_diagonal(kv_mem[:, :D])
    v_tall = block_diagonal(kv_mem[:, D:])
    deltas = []
    for h in range(HEADS):
        at = h * HEAD
        do = gmix_ref[at : at + HEAD].astype(F32)
        deltas.append(
            jnp.sum(do * mixed_ref[at : at + HEAD].astype(F32), axis=0, keepdims=True)
        )
        do_m[at : at + HEAD] = (do * cm_ref[h : h + 1]).astype(LOW)
    da_m = dg(v_tall, do_m[...], 1, 0)
    for h in range(HEADS):
        rows = slice(h * PAD, (h + 1) * PAD)
        ds_m[rows] = (
            pm_ref[rows].astype(F32) * (da_m[rows] - deltas[h] * cm_ref[h : h + 1])
        ).astype(LOW)
    dv_mem = diagonal_sum(dg(pm_ref[...], do_m[...], 1, 1))
    dk_mem = diagonal_sum(dg(ds_m[...], qkv_ref[:D], 1, 1))
    dq_mem = dg(k_tall, ds_m[...], 0, 0)
    for h in range(HEADS):
        at = h * HEAD
        c = c_ref[h : h + 1]
        do = (gmix_ref[at : at + HEAD].astype(F32) * c).astype(LOW)
        copies[h].wait()
        p = p_ref[h]
        da = dg(qkv_ref[2 * D + at : 2 * D + at + HEAD], do, 0, 0)
        ds = (p.astype(F32) * (da - deltas[h] * c)).astype(LOW)
        gp[2 * D + at : 2 * D + at + HEAD] = dg(do, p, 1, 1).astype(LOW)
        gp[D + at : D + at + HEAD] = dg(qkv_ref[at : at + HEAD], ds, 1, 1).astype(LOW)
        gp[at : at + HEAD] = (
            SCALE * (dg(qkv_ref[D + at : D + at + HEAD], ds, 1, 0) + dq_mem[at : at + HEAD])
        ).astype(LOW)
    gp_mem = jnp.concatenate([dk_mem, dv_mem], axis=1).astype(LOW)
    x_t = x_ref[...].T
    wext[:, :D] = dg(x_t, gp[:D], 1, 1).astype(LOW)
    wext[:, D : 3 * D] = (dg(x_t, gp[D:], 1, 1) + dg(mem_low, gp_mem, 0, 0)).astype(LOW)
    wext[:, 3 * D : 4 * D] = dwo_ref[...]
    g_mem = dg(gp_mem, w_ref[:, D : 3 * D], 1, 1)
    g_mem = jnp.where(at_ref[2] == 0, g_mem, 0.0)
    row = iota((EXTRA, D), 0)
    tall = jnp.concatenate([g_mem, jnp.zeros((EXTRA - PAD, D), F32)], axis=0)
    tall = jnp.where(row < MEM, tall, 0.0)
    for i in range(5):
        tall = jnp.where(row == MEM + i, (vec1_ref if i < 2 else vec_ref)[i : i + 1], tall)
    wext[:, 4 * D :] = tall.T.astype(LOW)
    for g_ref, offsets in zip(g_refs, bits, strict=True):
        if offsets is None:
            g_ref[...] = wext[...]
            continue
        size = g_ref.shape[0] // len(offsets)
        for j, offset in enumerate(offsets):
            start = pl.multiple_of((me ^ offset) * size, size)
            g_ref[j * size : (j + 1) * size] = wext[pl.ds(start, size), :]
    tok_ref[...] = (dg(w_ref[:, : 3 * D], gp[...], 1, 0).T + resid_ref[...]).astype(LOW)


def place_kernel(at_ref, r0, r1, r2, r3, out_ref, held, ins, outs):
    me = at_ref[3]
    refs = (r0, r1, r2, r3)
    ins = [pltpu.make_async_copy(refs[k], held.at[k], ins.at[k]) for k in range(4)]
    outs = [pltpu.make_async_copy(held.at[k], out_ref.at[me ^ k], outs.at[k]) for k in range(4)]
    for copy in ins:
        copy.start()
    for k in range(4):
        ins[k].wait()
        outs[k].start()
    for copy in outs:
        copy.wait()


def place(at, pieces):
    rows = call(
        place_kernel,
        sds((4,) + pieces[0].shape, pieces[0].dtype),
        [SMEM] + [ANY] * 4,
        ANY,
        [
            pltpu.VMEM((4,) + pieces[0].shape, pieces[0].dtype),
            pltpu.SemaphoreType.DMA((4,)),
            pltpu.SemaphoreType.DMA((4,)),
        ],
    )(at, *pieces)
    return rows.reshape(-1, D)


def finish_kernel(at_ref, own_ref, other_ref, out_ref, bias_ref, held):
    first = at_ref[5]
    size = own_ref.shape[1]
    for i, ref in enumerate((own_ref, other_ref)):
        for j in range(2):
            start = pl.multiple_of((first ^ (2 * i + j)) * size, size)
            held[pl.ds(start, size), :] = ref[j].astype(F32)
    out_ref[...] = held[:D]
    bias_ref[...] = held[held.shape[0] - PAD : held.shape[0] - PAD + 1]


def swap(value, axis, bit):
    n = lax.axis_size(axis)
    return lax.ppermute(value, axis, [(i, i ^ bit) for i in range(n)])


def add_low(*terms):
    return functools.reduce(jnp.add, [t.astype(F32) for t in terms]).astype(LOW)


def sum_over_dp(at, own, theirs):
    n_dp = lax.axis_size("dp")
    got = swap(theirs, "mp", 2)
    if n_dp != 8:
        total = lax.psum(own.astype(F32) + got.astype(F32), "dp").reshape(-1, D)
        return total[:D], total[-PAD]
    mine, give_x = add_low(own[:2], got[:2]), add_low(own[2:], got[2:])
    got = swap(give_x, "dp", 1)
    mine, give_z = add_low(mine[0], got[0]), add_low(mine[1], got[1])
    mine = add_low(mine, swap(give_z, "dp", 2))
    mine = add_low(mine, swap(mine, "dp", 4))
    pair = jnp.stack([mine, swap(mine, "dp", 2)])
    rows = 4 * own.shape[1]
    grad, bias = call(
        finish_kernel,
        [sds((D, D), F32), sds((1, D), F32)],
        [SMEM] + [VMEM] * 2,
        [VMEM] * 2,
        [pltpu.VMEM((rows, D), F32)],
        bytes_=2 * 2**20,
    )(at, pair, swap(pair, "dp", 1))
    return grad, bias[0]


def shards(
    tokens, cotangent, memory_init, query_weight, key_weight, value_weight, output_weight, first_gain,
    first_bias, inner_weight, inner_bias, outer_weight, outer_bias, second_gain, second_bias,
):
    n_dp, n_mp = lax.axis_size("dp"), lax.axis_size("mp")
    rows_each = query_weight.shape[0]
    by_bits = n_dp == 8 and n_mp == 4 and rows_each % 16 == 0
    me_mp, me_dp = lax.axis_index("mp"), lax.axis_index("dp")
    me = me_dp * n_mp + me_mp
    later = me_mp % SPANS
    first = ((me_dp & 1) * 2 + ((me_dp >> 1) & 1)) if by_bits else 0
    at = jnp.stack([me, me_mp // SPANS, later, me_mp, me_dp, first]).astype(jnp.int32)

    vectors = (first_gain, first_bias, outer_bias, second_gain, second_bias)
    local = call(
        pack_kernel,
        sds((rows_each, WIDE), LOW),
        [VMEM] * 10,
        VMEM,
        [pltpu.VMEM((EXTRA, EXTRA), F32)],
    )(query_weight, key_weight, value_weight, output_weight, memory_init, *[v.reshape(1, -1) for v in vectors])
    if by_bits:
        line = jnp.concatenate([local] + [swap(local, ALL, 8 * j) for j in range(1, 4)], axis=0)
        plane = [line] + [swap(line, ALL, 2 * b) for b in range(1, 4)]
        pieces = plane + [swap(piece, ALL, 1) for piece in plane]
        bits = [[2 * b + c + 8 * j for j in range(4)] for c in range(2) for b in range(4)]
    else:
        pieces = [lax.all_gather(local, ALL, axis=0, tiled=True)]
        bits = [None]

    wis, wos = [inner_weight], [outer_weight]
    bis = [inner_bias.reshape(1, -1)]
    for group in (wis, wos, bis):
        group += [swap(group[0], "mp", k) for k in range(1, 3)]
        group.append(swap(group[2], "mp", 1))
    inner_shift = jnp.concatenate(bis, axis=0).astype(F32)

    blocks = tokens.reshape(-1, SPAN, D)
    pick = lambda v, i: lax.dynamic_index_in_dim(v, i, 0, keepdims=False)
    own = pick(blocks, me_mp)
    start = pick(blocks, me_mp - later)
    cot = pick(cotangent.reshape(-1, SPAN, D), me_mp)

    w, small, nm, qkv, p, o, m, l = call(
        functools.partial(attend_kernel, bits),
        [
            sds((D, 4 * D), LOW),
            sds((PAD, D), F32),
            sds((PAD, D), F32),
            sds((3 * D, SPAN), LOW),
            sds((HEADS, SPAN, SPAN), LOW),
            sds((D, SPAN), F32),
            sds((HEADS, SPAN), F32),
            sds((HEADS, SPAN), F32),
        ],
        [SMEM] + [VMEM] * (len(pieces) + 2),
        [VMEM, VMEM, VMEM, VMEM, ANY, VMEM, VMEM, VMEM],
        [
            pltpu.VMEM((D, WIDE), LOW),
            pltpu.VMEM((HEADS, SPAN, SPAN), LOW),
            pltpu.SemaphoreType.DMA((HEADS,)),
        ],
        flops=10 * 10**9,
        bytes_=10 * 2**20,
    )(at, *pieces, own, start)

    outer_shape = sds((2, 4, D // 4, D), LOW)
    inner_shape = sds((2, 4, (D + PAD) // 4, D), LOW)
    square, square_low = sds((SPAN, D), F32), sds((SPAN, D), LOW)
    (out, outer_keep, outer_send, slope, normed, grad_low, grad_sum, xhat, inv, mixed, mem, p_mem, c, c_mem, vecs) = call(
        forward_kernel,
        [
            square_low,
            outer_shape,
            outer_shape,
            sds((4, SPAN, D), LOW),
            square_low,
            square_low,
            square,
            square,
            sds((SPAN, 1), F32),
            sds((D, SPAN), LOW),
            sds((PAD, D), F32),
            sds((HEADS * PAD, SPAN), LOW),
            sds((HEADS, SPAN), F32),
            sds((HEADS, SPAN), F32),
            sds((8, D), F32),
        ],
        [SMEM] + [VMEM] * 18,
        [VMEM] * 15,
        [pltpu.VMEM((4, SPAN, D), LOW)],
        flops=10 * 10**9,
        bytes_=14 * 2**20,
    )(at, nm, small, own, w, qkv, o, m, l, *wis, *wos, inner_shift, cot)

    theirs = swap(outer_send, "mp", 1)
    grad_outer, _ = sum_over_dp(at, add_low(outer_keep[0], theirs[0]), add_low(outer_keep[1], theirs[1]))

    across = swap(out, "mp", 2)
    layer_out = place(at, [out, swap(out, "mp", 1), across, swap(across, "mp", 1)])

    inner_keep, inner_send, resid, d_mix, g_mixed, vecs1 = call(
        middle_kernel,
        [
            inner_shape,
            inner_shape,
            square,
            sds((D, D), LOW),
            sds((D, SPAN), LOW),
            sds((8, D), F32),
        ],
        [SMEM] + [VMEM] * 17,
        [VMEM] * 6,
        flops=8 * 10**9,
        bytes_=14 * 2**20,
    )(at, small, w, *wis, *wos, slope, normed, grad_low, grad_sum, xhat, inv, mixed)
    theirs = swap(inner_send, "mp", 1)
    grad_inner, grad_inner_bias = sum_over_dp(
        at, add_low(inner_keep[0], theirs[0]), add_low(inner_keep[1], theirs[1])
    )

    if by_bits:
        out_bits = [[2 * b + c + 8 * j for b in range(4) for j in range(4)] for c in range(2)]
    else:
        out_bits = [None]
    *grads, grad_rows = call(
        functools.partial(backward_kernel, out_bits),
        [sds((D // len(out_bits), WIDE), LOW) for _ in out_bits] + [sds((SPAN, D), LOW)],
        [SMEM, VMEM, VMEM, VMEM, ANY] + [VMEM] * 10,
        [VMEM] * (len(out_bits) + 1),
        [
            pltpu.VMEM((HEADS, SPAN, SPAN), LOW),
            pltpu.SemaphoreType.DMA((HEADS,)),
            pltpu.VMEM((3 * D, SPAN), LOW),
            pltpu.VMEM((D, SPAN), LOW),
            pltpu.VMEM((HEADS * PAD, SPAN), LOW),
            pltpu.VMEM((D, WIDE), LOW),
        ],
        flops=12 * 10**9,
        bytes_=12 * 2**20,
    )(at, own, w, qkv, p, p_mem, mixed, c, c_mem, g_mixed, mem, resid, d_mix, vecs, vecs1)

    across = swap(grad_rows, "mp", 2)
    grad_tokens = place(at, [grad_rows, swap(grad_rows, "mp", 1), across, swap(across, "mp", 1)])

    if by_bits:
        chip = add_low(grads[0], swap(grads[1], ALL, 1)).reshape(4, 4 * rows_each, WIDE)
        line = add_low(chip[0], *[swap(chip[b], ALL, 2 * b) for b in range(1, 4)])
        line = line.reshape(4, rows_each, WIDE)
        terms = [line[0]] + [swap(line[j], ALL, 8 * j) for j in range(1, 4)]
        reduced = functools.reduce(jnp.add, [t.astype(F32) for t in terms])
    else:
        reduced = lax.psum_scatter(grads[0], ALL, scatter_dimension=0, tiled=True).astype(F32)
    vector = lambda i: reduced[:, 4 * D + MEM + i]
    return (
        layer_out,
        grad_tokens,
        reduced[:, 4 * D : 4 * D + MEM].T,
        reduced[:, :D],
        reduced[:, D : 2 * D],
        reduced[:, 2 * D : 3 * D],
        reduced[:, 3 * D : 4 * D],
        vector(0),
        vector(1),
        grad_inner,
        grad_inner_bias,
        grad_outer,
        vector(2),
        vector(3),
        vector(4),
    )


def solution(mesh):
    both = ("dp", "mp")
    in_specs = (
        P("dp", None),
        P("dp", None),
        P(None, both),
        P(both, None),
        P(both, None),
        P(both, None),
        P(both, None),
        P(both),
        P(both),
        P(None, "mp"),
        P("mp"),
        P("mp", None),
        P(both),
        P(both),
        P(both),
    )
    out_specs = (
        P("dp", None),
        P("dp", None),
        P(None, both),
        P(both, None),
        P(both, None),
        P(both, None),
        P(both, None),
        P(both),
        P(both),
        P(None, "mp"),
        P("mp"),
        P("mp", None),
        P(both),
        P(both),
        P(both),
    )
    return jax.shard_map(shards, mesh=mesh, in_specs=in_specs, out_specs=out_specs, check_vma=False)
```

```python
import functools

import jax
import jax.numpy as jnp
from jax import lax
from jax.experimental import pallas as pl
from jax.experimental.pallas import tpu as pltpu
from jax.sharding import PartitionSpec as P

D = 512
HEADS = 8
HEAD = 64
MEM = 20
PAD = 32
SPAN = 512
SPANS = 2
EXTRA = 128
WIDE = 4 * D + EXTRA
EPS = 1e-05
GELU_A = 0.7978845608028654
GELU_B = 0.044715
LOW = jnp.bfloat16
F32 = jnp.float32
SCALE = HEAD ** (-0.5)
ALL = ("dp", "mp")

VMEM = pl.BlockSpec(memory_space=pltpu.VMEM)
SMEM = pl.BlockSpec(memory_space=pltpu.SMEM)
ANY = pl.BlockSpec(memory_space=pl.ANY)


def dg(a, b, ca, cb):
    return lax.dot_general(a, b, (((ca,), (cb,)), ((), ())), preferred_element_type=F32)


def iota(shape, dim):
    return lax.broadcasted_iota(jnp.int32, shape, dim)


def head_mask(heads):
    shape = (heads * PAD, heads * HEAD)
    return (iota(shape, 0) >> 5) == (iota(shape, 1) >> 6)


def block_diagonal(rows):
    heads = rows.shape[1] // HEAD
    tall = jnp.concatenate([rows] * heads, axis=0)
    return jnp.where(head_mask(heads), tall, 0.0).astype(LOW)


def diagonal_sum(tall):
    heads = tall.shape[1] // HEAD
    kept = jnp.where(head_mask(heads), tall, 0.0)
    total = kept[:PAD]
    for h in range(1, heads):
        total = total + kept[h * PAD : (h + 1) * PAD]
    return total


def normalize(values):
    mean = jnp.mean(values, axis=1, keepdims=True)
    center = values - mean
    spread = jnp.mean(center * center, axis=1, keepdims=True)
    inv = lax.rsqrt(spread + EPS)
    return center * inv, inv


def gelu_parts(a):
    sq = a * a
    t = jnp.tanh(a * (GELU_A + (GELU_A * GELU_B) * sq))
    half = 0.5 * (1.0 + t)
    return half, t, sq


def gelu(a):
    half, _, _ = gelu_parts(a)
    return a * half


def call(kernel, out_shape, in_specs, out_specs, scratch=(), flops=1, bytes_=1, mib=32):
    return pl.pallas_call(
        kernel,
        out_shape=out_shape,
        in_specs=in_specs,
        out_specs=out_specs,
        scratch_shapes=list(scratch),
        compiler_params=pltpu.CompilerParams(vmem_limit_bytes=mib * 2**20),
        cost_estimate=pl.CostEstimate(flops=flops, bytes_accessed=bytes_, transcendentals=0),
    )


def sds(shape, dtype):
    return jax.ShapeDtypeStruct(shape, dtype)


def pack_kernel(q_ref, k_ref, v_ref, o_ref, mem_ref, g1_ref, b1_ref, ob_ref, g2_ref, b2_ref, out_ref, tall):
    rows = q_ref.shape[0]
    for i, ref in enumerate((q_ref, k_ref, v_ref, o_ref)):
        out_ref[:, i * D : (i + 1) * D] = ref[...]
    tall[...] = jnp.zeros(tall.shape, F32)
    for i, ref in enumerate((g1_ref, b1_ref, ob_ref, g2_ref, b2_ref)):
        tall[MEM + i : MEM + i + 1, :rows] = ref[...].astype(F32)
    out_ref[:, 4 * D :] = tall[...].T[:rows].astype(LOW)
    out_ref[:, 4 * D : 4 * D + MEM] = mem_ref[...]


def assemble(me, pieces, bits, out_ref):
    for piece, offsets in zip(pieces, bits, strict=True):
        if offsets is None:
            out_ref[...] = piece[...]
            continue
        size = piece.shape[0] // len(offsets)
        for j, offset in enumerate(offsets):
            start = pl.multiple_of((me ^ offset) * size, size)
            out_ref[pl.ds(start, size), :] = piece[j * size : (j + 1) * size, :]


def project_kernel(bits, at_ref, *refs):
    n = len(bits)
    x_ref, w_ref, qkv_ref = refs[n:]
    assemble(at_ref[0], refs[:n], bits, w_ref)
    x_t = x_ref[...].T
    qkv_ref[:D] = (dg(w_ref[:, :D], x_t, 0, 0).astype(LOW).astype(F32) * SCALE).astype(LOW)
    qkv_ref[D : 3 * D] = dg(w_ref[:, D : 3 * D], x_t, 0, 0).astype(LOW)


def attend_kernel(qkv_ref, p_ref, o_ref, m_ref, l_ref):
    def scores(h):
        at = h * HEAD
        return dg(qkv_ref[D + at : D + at + HEAD], qkv_ref[at : at + HEAD], 0, 0)

    s_next = scores(0)
    for h in range(HEADS):
        s = s_next
        if h + 1 < HEADS:
            s_next = scores(h + 1)
        at = h * HEAD
        m = jnp.max(s, axis=0, keepdims=True)
        p = jnp.exp(s - m)
        m_ref[h : h + 1] = m
        l_ref[h : h + 1] = jnp.sum(p, axis=0, keepdims=True)
        p_ref[h] = p.astype(LOW)
        o_ref[at : at + HEAD] = dg(qkv_ref[2 * D + at : 2 * D + at + HEAD], p_ref[h], 1, 0)


def memory_kernel(x1_ref, w_ref, nm_ref, small_ref):
    small = w_ref[:, 4 * D :].T.astype(F32)[:PAD]
    small_ref[...] = small
    mem = jnp.where(iota((PAD, D), 0) < MEM, small, 0.0)
    packed = dg(mem.astype(LOW), w_ref[:, : 3 * D], 1, 0).astype(LOW)
    q_tall = block_diagonal(packed[:, :D].astype(F32) * SCALE)
    s_mem = dg(q_tall, packed[:, D : 2 * D], 1, 1)
    s_mem = jnp.where(iota(s_mem.shape, 1) < MEM, s_mem, -1e30)
    kv = dg(x1_ref[...], w_ref[:, D : 3 * D], 1, 0).astype(LOW)
    s = dg(q_tall, kv[:, :D], 1, 1)
    m = jnp.maximum(jnp.max(s, axis=1, keepdims=True), jnp.max(s_mem, axis=1, keepdims=True))
    p = jnp.exp(s - m)
    p_mem = jnp.exp(s_mem - m)
    total = jnp.sum(p, axis=1, keepdims=True) + jnp.sum(p_mem, axis=1, keepdims=True)
    o = dg(p.astype(LOW), kv[:, D:], 1, 0) + dg(p_mem.astype(LOW), packed[:, 2 * D :], 1, 0)
    mixed = diagonal_sum(o / total).astype(LOW)
    xhat, _ = normalize(mem + dg(mixed, w_ref[:, 3 * D : 4 * D], 1, 0))
    nm_ref[...] = xhat * small[MEM : MEM + 1] + small[MEM + 1 : MEM + 2]


def forward_kernel(
    at_ref, nm_ref, small_ref, x_ref, w_ref, qkv_ref, o_ref, m_ref, l_ref,
    wi0, wi1, wi2, wi3, wo0, wo1, wo2, wo3, cot_ref,
    out_ref, keep_ref, send_ref, slope_ref, nl_ref, gl_ref, gs_ref, xhat_ref, inv_ref,
    mixed_ref, mem_ref, kv_ref, pm_ref, c_ref, cm_ref, vec_ref, hid,
):
    wis, wos = (wi0, wi1, wi2, wi3), (wo0, wo1, wo2, wo3)
    shifts = [ref[D : D + 1].astype(F32) for ref in wos]
    small = small_ref[...]
    gain1, bias1, outer_b, gain2, bias2 = (small[MEM + i : MEM + i + 1] for i in range(5))
    later, first = at_ref[2], at_ref[5]
    nm = nm_ref[...]
    nm_low = nm.astype(LOW)
    value = nm + outer_b
    for k in range(4):
        inner = dg(nm_low, wis[k][...], 1, 0) + shifts[k]
        value = value + dg(gelu(inner).astype(LOW), wos[k][:D], 1, 0)
    carried, _ = normalize(value)
    carried = carried * gain2 + bias2
    mem = jnp.where(later == 1, carried, small)
    mem = jnp.where(iota((PAD, D), 0) < MEM, mem, 0.0)
    mem_ref[...] = mem
    kv_mem = dg(mem.astype(LOW), w_ref[:, D : 3 * D], 1, 0).astype(LOW)
    kv_ref[...] = kv_mem
    k_tall = block_diagonal(kv_mem[:, :D].astype(F32))
    v_tall = block_diagonal(kv_mem[:, D:].astype(F32))
    s_all = dg(k_tall, qkv_ref[:D], 1, 0)
    s_all = jnp.where((iota(s_all.shape, 0) & (PAD - 1)) < MEM, s_all, -1e30)
    alphas, invs = [], []
    for h in range(HEADS):
        s = s_all[h * PAD : (h + 1) * PAD]
        m_old = m_ref[h : h + 1]
        m = jnp.maximum(m_old, jnp.max(s, axis=0, keepdims=True))
        alpha = jnp.exp(m_old - m)
        p = jnp.exp(s - m)
        inv = 1.0 / (l_ref[h : h + 1] * alpha + jnp.sum(p, axis=0, keepdims=True))
        pm_ref[h * PAD : (h + 1) * PAD] = p.astype(LOW)
        c_ref[h : h + 1] = alpha * inv
        cm_ref[h : h + 1] = inv
        alphas.append(alpha * inv)
        invs.append(inv)
    o_mem = dg(v_tall, pm_ref[...], 0, 0)
    for h in range(HEADS):
        at = h * HEAD
        mixed_ref[at : at + HEAD] = (
            o_ref[at : at + HEAD] * alphas[h] + o_mem[at : at + HEAD] * invs[h]
        ).astype(LOW)
    xhat1, inv1 = normalize(
        x_ref[...].astype(F32) + dg(mixed_ref[...], w_ref[:, 3 * D : 4 * D], 0, 0)
    )
    xhat_ref[...] = xhat1
    inv_ref[...] = inv1
    normed = xhat1 * gain1 + bias1
    normed_low = normed.astype(LOW)
    nl_ref[...] = normed_low
    total = normed + outer_b
    for k in range(4):
        a = dg(normed_low, wis[k][...], 1, 0) + shifts[k]
        half, t, sq = gelu_parts(a)
        hid[k] = (a * half).astype(LOW)
        slope = half + (0.5 * a) * (1.0 - t * t) * (GELU_A + (3.0 * GELU_A * GELU_B) * sq)
        slope_ref[k] = slope.astype(LOW)
        total = total + dg(hid[k], wos[k][:D], 1, 0)
    xhat2, inv2 = normalize(total)
    out_ref[...] = (xhat2 * gain2 + bias2).astype(LOW)
    cot = cot_ref[...].astype(F32)
    pull = cot * gain2
    grad_sum = inv2 * (
        pull
        - jnp.mean(pull, axis=1, keepdims=True)
        - xhat2 * jnp.mean(pull * xhat2, axis=1, keepdims=True)
    )
    vec_ref[2:3] = jnp.sum(grad_sum, axis=0, keepdims=True)
    vec_ref[3:4] = jnp.sum(cot * xhat2, axis=0, keepdims=True)
    vec_ref[4:5] = jnp.sum(cot, axis=0, keepdims=True)
    gs_ref[...] = grad_sum
    grad_low = grad_sum.astype(LOW)
    gl_ref[...] = grad_low
    for k in (1, 3, 0, 2):
        give(send_ref if k % 2 else keep_ref, k // 2, dg(hid[k], grad_low, 0, 0), first)


def give(ref, k, rows, first):
    size = rows.shape[0] // 4
    for i in range(4):
        ref[k, first ^ i] = rows[i * size : (i + 1) * size].astype(LOW)


def inner_terms(k, wi_ref, wo_ref, slope_ref, normed_low, grad_low, ref, first):
    gi = slope_ref[k].astype(F32) * dg(grad_low, wo_ref[:D], 1, 1)
    gi_low = gi.astype(LOW)
    bias = jnp.sum(gi_low.astype(F32), axis=0, keepdims=True)
    bias = jnp.where(iota((PAD, D), 0) == 0, bias, 0.0)
    rows = jnp.concatenate([dg(normed_low, gi_low, 0, 0), bias], axis=0)
    give(ref, k // 2, rows, first)
    return dg(gi_low, wi_ref[...], 1, 1)


def send_kernel(at_ref, wi1, wi3, wo1, wo3, slope_ref, nl_ref, gl_ref, gs_ref, send_ref, back_ref):
    first = at_ref[5]
    back = gs_ref[...]
    for k, wi_ref, wo_ref in ((1, wi1, wo1), (3, wi3, wo3)):
        back = back + inner_terms(k, wi_ref, wo_ref, slope_ref, nl_ref[...], gl_ref[...], send_ref, first)
    back_ref[...] = back


def keep_kernel(
    at_ref, after_ref, small_ref, w_ref, wi0, wi2, wo0, wo2, slope_ref, nl_ref, gl_ref, back_ref, xhat_ref, inv_ref, mixed_ref,
    keep_ref, resid_ref, dwo_ref, gmix_ref, vec_ref,
):
    first = at_ref[5]
    back = back_ref[...]
    for k, wi_ref, wo_ref in ((0, wi0, wo0), (2, wi2, wo2)):
        back = back + inner_terms(k, wi_ref, wo_ref, slope_ref, nl_ref[...], gl_ref[...], keep_ref, first)
    xhat1 = xhat_ref[...]
    vec_ref[0:1] = jnp.sum(back * xhat1, axis=0, keepdims=True)
    vec_ref[1:2] = jnp.sum(back, axis=0, keepdims=True)
    pull = back * small_ref[MEM : MEM + 1]
    resid = inv_ref[...] * (
        pull
        - jnp.mean(pull, axis=1, keepdims=True)
        - xhat1 * jnp.mean(pull * xhat1, axis=1, keepdims=True)
    )
    resid_ref[...] = resid
    resid_low = resid.astype(LOW)
    dwo_ref[...] = dg(mixed_ref[...], resid_low, 1, 0).astype(LOW)
    gmix_ref[...] = dg(w_ref[:, 3 * D : 4 * D], resid_low, 1, 1).astype(LOW)


def heads_kernel(
    low_h, high_h, after_ref, qkv_ref, p_ref, pm_ref, mixed_ref, c_ref, cm_ref, gmix_ref, kv_ref, gp_ref, gm_ref,
    do_m, ds_m,
):
    heads = range(low_h, high_h)
    f0, f1 = low_h * HEAD, high_h * HEAD
    m0, m1 = low_h * PAD, high_h * PAD
    k_tall = block_diagonal(kv_ref[:, f0:f1].astype(F32))
    v_tall = block_diagonal(kv_ref[:, D + f0 : D + f1].astype(F32))
    deltas = []
    for i, h in enumerate(heads):
        at = h * HEAD
        do = gmix_ref[at : at + HEAD].astype(F32)
        deltas.append(
            jnp.sum(do * mixed_ref[at : at + HEAD].astype(F32), axis=0, keepdims=True)
        )
        do_m[i * HEAD : (i + 1) * HEAD] = (do * cm_ref[h : h + 1]).astype(LOW)
    da_m = dg(v_tall, do_m[...], 1, 0)
    for i, h in enumerate(heads):
        rows = slice(i * PAD, (i + 1) * PAD)
        p = pm_ref[h * PAD : (h + 1) * PAD].astype(F32)
        ds_m[rows] = (p * (da_m[rows] - deltas[i] * cm_ref[h : h + 1])).astype(LOW)
    gm_ref[0] = diagonal_sum(dg(ds_m[...], qkv_ref[f0:f1], 1, 1))
    gm_ref[1] = diagonal_sum(dg(pm_ref[m0:m1], do_m[...], 1, 1))
    dq_mem = dg(k_tall, ds_m[...], 0, 0)
    for i, h in enumerate(heads):
        at = h * HEAD
        rows = slice(i * HEAD, (i + 1) * HEAD)
        c = c_ref[h : h + 1]
        do = (gmix_ref[at : at + HEAD].astype(F32) * c).astype(LOW)
        p = p_ref[h]
        da = dg(qkv_ref[2 * D + at : 2 * D + at + HEAD], do, 0, 0)
        ds = (p.astype(F32) * (da - deltas[i] * c)).astype(LOW)
        gp_ref[2, rows] = dg(do, p, 1, 1).astype(LOW)
        gp_ref[1, rows] = dg(qkv_ref[at : at + HEAD], ds, 1, 1).astype(LOW)
        gp_ref[0, rows] = (
            SCALE * (dg(qkv_ref[D + at : D + at + HEAD], ds, 1, 0) + dq_mem[rows])
        ).astype(LOW)


def weights_kernel(
    bits, after_ref, at_ref, x_ref, w_ref, mem_ref, gp0_ref, gp1_ref, gm0_ref, gm1_ref, dwo_ref, vec_ref, vec1_ref, *rest
):
    g_refs, wext = rest[: len(bits)], rest[len(bits)]
    me = at_ref[0]
    mem_low = mem_ref[...].astype(LOW)
    x_t = x_ref[...].T
    width = gp0_ref.shape[1]
    for part, (gp_ref, gm_ref) in enumerate(((gp0_ref, gm0_ref), (gp1_ref, gm1_ref))):
        for i in range(3):
            grad = dg(x_t, gp_ref[i], 1, 1)
            if i > 0:
                grad = grad + dg(mem_low, gm_ref[i - 1].astype(LOW), 0, 0)
            at = i * D + part * width
            wext[:, at : at + width] = grad.astype(LOW)
    wext[:, 3 * D : 4 * D] = dwo_ref[...]
    gp_mem = jnp.concatenate([gm0_ref[0], gm1_ref[0], gm0_ref[1], gm1_ref[1]], axis=1).astype(LOW)
    g_mem = dg(gp_mem, w_ref[:, D : 3 * D], 1, 1)
    g_mem = jnp.where(at_ref[2] == 0, g_mem, 0.0)
    row = iota((EXTRA, D), 0)
    tall = jnp.concatenate([g_mem, jnp.zeros((EXTRA - PAD, D), F32)], axis=0)
    tall = jnp.where(row < MEM, tall, 0.0)
    for i in range(5):
        tall = jnp.where(row == MEM + i, (vec1_ref if i < 2 else vec_ref)[i : i + 1], tall)
    wext[:, 4 * D :] = tall.T.astype(LOW)
    for g_ref, offsets in zip(g_refs, bits, strict=True):
        if offsets is None:
            g_ref[...] = wext[...]
            continue
        size = g_ref.shape[0] // len(offsets)
        for j, offset in enumerate(offsets):
            start = pl.multiple_of((me ^ offset) * size, size)
            g_ref[j * size : (j + 1) * size] = wext[pl.ds(start, size), :]


def tokens_kernel(after_ref, w_ref, gp0_ref, gp1_ref, resid_ref, tok_ref):
    width = gp0_ref.shape[1]
    total = jnp.zeros((D, SPAN), F32)
    for part, gp_ref in enumerate((gp0_ref, gp1_ref)):
        for i in range(3):
            at = i * D + part * width
            total = total + dg(w_ref[:, at : at + width], gp_ref[i], 1, 0)
    tok_ref[...] = (total.T + resid_ref[...]).astype(LOW)


def place_kernel(at_ref, r0, r1, r2, r3, out_ref, sems):
    me = at_ref[3]
    copies = [pltpu.make_async_copy(ref, out_ref.at[me ^ k], sems.at[k]) for k, ref in enumerate((r0, r1, r2, r3))]
    for copy in copies:
        copy.start()
    for copy in copies:
        copy.wait()


def place(at, pieces):
    rows = call(
        place_kernel,
        sds((4,) + pieces[0].shape, pieces[0].dtype),
        [SMEM] + [VMEM] * 4,
        ANY,
        [pltpu.SemaphoreType.DMA((4,))],
        mib=8,
    )(at, *pieces)
    return rows.reshape(-1, D)


def finish_kernel(at_ref, own_ref, other_ref, out_ref, bias_ref, held):
    first = at_ref[5]
    size = own_ref.shape[1]
    for i, ref in enumerate((own_ref, other_ref)):
        for j in range(2):
            start = pl.multiple_of((first ^ (2 * i + j)) * size, size)
            held[pl.ds(start, size), :] = ref[j].astype(F32)
    out_ref[...] = held[:D]
    bias_ref[...] = held[held.shape[0] - PAD : held.shape[0] - PAD + 1]


def swap(value, axis, bit):
    n = lax.axis_size(axis)
    return lax.ppermute(value, axis, [(i, i ^ bit) for i in range(n)])


def tie(*values):
    return lax.optimization_barrier(values)


def add_low(*terms):
    return functools.reduce(jnp.add, [t.astype(F32) for t in terms]).astype(LOW)


def finish(at, pair, other):
    grad, bias = call(
        finish_kernel,
        [sds((D, D), F32), sds((1, D), F32)],
        [SMEM] + [VMEM] * 2,
        [VMEM] * 2,
        [pltpu.VMEM((4 * pair.shape[1], D), F32)],
        bytes_=2 * 2**20,
    )(at, pair, other)
    return grad, bias[0]


def shards(
    tokens, cotangent, memory_init, query_weight, key_weight, value_weight, output_weight, first_gain,
    first_bias, inner_weight, inner_bias, outer_weight, outer_bias, second_gain, second_bias,
):
    n_dp, n_mp = lax.axis_size("dp"), lax.axis_size("mp")
    rows_each = query_weight.shape[0]
    by_bits = n_dp == 8 and n_mp == 4 and rows_each % 16 == 0
    me_mp, me_dp = lax.axis_index("mp"), lax.axis_index("dp")
    me = me_dp * n_mp + me_mp
    later = me_mp % SPANS
    x = (me_dp & 1) if by_bits else 0
    first = (x * 2 + ((me_dp >> 1) & 1)) if by_bits else 0
    at = jnp.stack([me, me_mp // SPANS, later, me_mp, me_dp, first, x]).astype(jnp.int32)

    vectors = (first_gain, first_bias, outer_bias, second_gain, second_bias)
    local = call(
        pack_kernel,
        sds((rows_each, WIDE), LOW),
        [VMEM] * 10,
        VMEM,
        [pltpu.VMEM((EXTRA, EXTRA), F32)],
        mib=56,
    )(query_weight, key_weight, value_weight, output_weight, memory_init.T, *[v.reshape(1, -1) for v in vectors])

    pick = lambda v, i: lax.dynamic_index_in_dim(v, i, 0, keepdims=False)
    outer_rows = jnp.concatenate([outer_weight, inner_bias.reshape(1, -1), jnp.zeros((15, D), LOW)], axis=0)
    wi2 = swap(inner_weight, "mp", 2)
    if by_bits:
        line = [local] + [swap(local, ALL, 8 * j) for j in range(1, 4)]
        *line, wi2 = tie(*line, wi2)
        line = jnp.concatenate(line, axis=0)
        plane = [line] + [swap(line, ALL, 2 * b) for b in range(1, 4)]
        *plane, outer_rows = tie(*plane, outer_rows)
        pieces = plane + [swap(piece, ALL, 1) for piece in plane]
        bits = [[2 * b + c + 8 * j for j in range(4)] for c in range(2) for b in range(4)]
    else:
        pieces = [lax.all_gather(local, ALL, axis=0, tiled=True)]
        bits = [None]
    wo2 = swap(outer_rows, "mp", 2)
    wi1, wo1, wi3 = swap(inner_weight, "mp", 1), swap(outer_rows, "mp", 1), swap(wi2, "mp", 1)
    blocks = tokens.reshape(-1, SPAN, D)
    own = pick(blocks, me_mp)
    start = pick(blocks, me_mp - later)
    cot = pick(cotangent.reshape(-1, SPAN, D), me_mp)

    w, qkv = call(
        functools.partial(project_kernel, bits),
        [sds((D, WIDE), LOW), sds((3 * D, SPAN), LOW)],
        [SMEM] + [VMEM] * (len(pieces) + 1),
        [VMEM] * 2,
        flops=2 * 10**9,
        bytes_=5 * 2**20,
    )(at, *pieces, own)
    p, o, m, l = call(
        attend_kernel,
        [
            sds((HEADS, SPAN, SPAN), LOW),
            sds((D, SPAN), F32),
            sds((HEADS, SPAN), F32),
            sds((HEADS, SPAN), F32),
        ],
        [VMEM],
        [VMEM] * 4,
        flops=5 * 10**9,
        bytes_=7 * 2**20,
    )(qkv)

    nm, small = call(
        memory_kernel,
        [sds((PAD, D), F32), sds((PAD, D), F32)],
        [VMEM] * 2,
        [VMEM] * 2,
        flops=3 * 10**9,
        bytes_=4 * 2**20,
        mib=16,
    )(start, w)
    nm, m, wo2 = tie(nm, m, wo2)
    wo3 = swap(wo2, "mp", 1)

    outer_shape = sds((2, 4, D // 4, D), LOW)
    inner_shape = sds((2, 4, (D + PAD) // 4, D), LOW)
    square, square_low = sds((SPAN, D), F32), sds((SPAN, D), LOW)
    (
        out, outer_keep, outer_send, slope, normed, grad_low, grad_sum, xhat, inv, mixed, mem, kv_mem, p_mem, c, c_mem, vecs,
    ) = call(
        forward_kernel,
        [
            square_low,
            outer_shape,
            outer_shape,
            sds((4, SPAN, D), LOW),
            square_low,
            square_low,
            square,
            square,
            sds((SPAN, 1), F32),
            sds((D, SPAN), LOW),
            sds((PAD, D), F32),
            sds((PAD, 2 * D), LOW),
            sds((HEADS * PAD, SPAN), LOW),
            sds((HEADS, SPAN), F32),
            sds((HEADS, SPAN), F32),
            sds((8, D), F32),
        ],
        [SMEM] + [VMEM] * 17,
        [VMEM] * 16,
        [pltpu.VMEM((4, SPAN, D), LOW)],
        flops=10 * 10**9,
        bytes_=14 * 2**20,
    )(
        at, nm, small, own, w, qkv, o, m, l, inner_weight, wi1, wi2, wi3, outer_rows, wo1, wo2, wo3, cot,
    )
    wis, wos = (inner_weight, wi1, wi2, wi3), (outer_rows, wo1, wo2, wo3)

    outer_got = swap(outer_send, "mp", 1)

    inner_send, back = call(
        send_kernel,
        [inner_shape, square],
        [SMEM] + [VMEM] * 8,
        [VMEM] * 2,
    )(at, wis[1], wis[3], wos[1], wos[3], slope, normed, grad_low, grad_sum)
    inner_got = swap(inner_send, "mp", 1)

    outer_mine, outer_give = add_low(outer_keep[0], outer_got[0]), add_low(outer_keep[1], outer_got[1])
    outer_y = swap(outer_give, "mp", 2)

    inner_keep, resid, d_mix, g_mixed, vecs1 = call(
        keep_kernel,
        [
            inner_shape,
            square,
            sds((D, D), LOW),
            sds((D, SPAN), LOW),
            sds((8, D), F32),
        ],
        [SMEM, ANY] + [VMEM] * 13,
        [VMEM] * 5,
    )(at, outer_give, small, w, wis[0], wis[2], wos[0], wos[2], slope, normed, grad_low, back, xhat, inv, mixed)

    half = HEADS // 2
    some = half * HEAD

    def heads_backward(low_h, gate):
        return call(
            functools.partial(heads_kernel, low_h, low_h + half),
            [sds((3, some, SPAN), LOW), sds((2, PAD, some), F32)],
            [ANY] + [VMEM] * 8,
            [VMEM] * 2,
            [
                pltpu.VMEM((some, SPAN), LOW),
                pltpu.VMEM((half * PAD, SPAN), LOW),
            ],
        )(gate, qkv, p, p_mem, mixed, c, c_mem, g_mixed, kv_mem)

    if by_bits:
        inner_give = add_low(inner_keep[:, 2:], inner_got[:, 2:])
        inner_mine = add_low(inner_keep[:, :2], inner_got[:, :2])
        inner_x = swap(inner_give, "dp", 1)
    else:
        inner_give = inner_got
    gp0, gm0 = heads_backward(0, inner_give)
    gp1, gm1 = heads_backward(half, inner_give)

    if by_bits:
        out_bits = [[2 * b + c + 8 * j for b in range(4) for j in (0, 2, 1, 3)] for c in range(2)]
    else:
        out_bits = [None]

    def weights_backward(gate):
        return call(
            functools.partial(weights_kernel, out_bits),
            [sds((D // len(out_bits), WIDE), LOW) for _ in out_bits],
            [ANY, SMEM] + [VMEM] * 10,
            [VMEM] * len(out_bits),
            [pltpu.VMEM((D, WIDE), LOW)],
        )(gate, at, own, w, mem, gp0, gp1, gm0, gm1, d_mix, vecs, vecs1)

    def tokens_backward(gate):
        return call(tokens_kernel, sds((SPAN, D), LOW), [ANY] + [VMEM] * 4, VMEM)(gate, w, gp0, gp1, resid)

    if by_bits:
        halves_of = lambda v: (v[: v.shape[0] // 2], v[v.shape[0] // 2 :])
        both = lambda mine, got: [add_low(u, v) for u, v in zip(halves_of(mine), halves_of(got), strict=True)]

        a_mine, a_give = [g.reshape(16, rows_each, WIDE) for g in weights_backward(inner_give)]
        a_got = swap(a_give, ALL, 1)
        grad_rows = tokens_backward(inner_give)

        rows_got = swap(grad_rows, "mp", 1)
        out_got, out_across = swap(out, "mp", 1), swap(out, "mp", 2)

        outer_y, out_across, grad_rows = tie(outer_y, out_across, grad_rows)
        q_mine, q_give = both(outer_mine, outer_y)
        q_got = swap(q_give, "dp", 1)

        inner_x, q_mine = tie(inner_x, q_mine)
        p_mine, p_give = add_low(inner_mine[0], inner_x[0]), add_low(inner_mine[1], inner_x[1])
        p_got = swap(p_give, "mp", 2)

        out_across, p_mine = tie(out_across, p_mine)
        out_last = swap(out_across, "mp", 1)
        layer_out = place(at, [out, out_got, out_across, out_last])

        q_got, layer_out = tie(q_got, layer_out)
        q_mine, q_give = [v[0] for v in both(q_mine, q_got)]
        q_got = swap(q_give, "dp", 2)

        p_got, q_mine = tie(p_got, q_mine)
        p_mine, p_give = [v[0] for v in both(p_mine, p_got)]
        p_got = swap(p_give, "dp", 2)

        a_got, p_mine = tie(a_got, p_mine)
        a_mine, a_give = both(a_mine, a_got)
        a_got = swap(a_give, ALL, 4)

        grad_rows, a_mine = tie(grad_rows, a_mine)
        rows_across = swap(grad_rows, "mp", 2)

        q_got, a_mine = tie(q_got, a_mine)
        q_mine = add_low(q_mine, q_got)
        q_got = swap(q_mine, "dp", 4)

        p_got, q_mine = tie(p_got, q_mine)
        p_mine = add_low(p_mine, p_got)
        p_got = swap(p_mine, "dp", 4)

        q_got, p_mine = tie(q_got, p_mine)
        q_mine = add_low(q_mine, q_got)
        q_got = swap(q_mine, "dp", 2)

        a_got, q_mine = tie(a_got, q_mine)
        a_mine, a_give = both(a_mine, a_got)
        a_got = swap(a_give, ALL, 2)

        p_got, a_mine = tie(p_got, a_mine)
        p_mine = add_low(p_mine, p_got)
        p_got = swap(p_mine, "dp", 2)

        rows_across, p_mine = tie(rows_across, p_mine)
        rows_last = swap(rows_across, "mp", 1)

        q_got, rows_across = tie(q_got, rows_across)
        q_pair = jnp.stack([q_mine, q_got])
        q_got = swap(q_pair, "dp", 1)

        a_got, q_pair = tie(a_got, q_pair)
        a_mine, a_give = both(a_mine, a_got)
        a_got = swap(a_give, ALL, 8)

        p_got, a_mine = tie(p_got, a_mine)
        p_pair = jnp.stack([p_mine, p_got])
        p_got = swap(p_pair, "dp", 1)

        rows_last, p_pair = tie(rows_last, p_pair)
        grad_tokens = place(at, [grad_rows, rows_got, rows_across, rows_last])

        a_got, grad_tokens = tie(a_got, grad_tokens)
        a_mine, a_give = both(a_mine, a_got)
        a_got = swap(a_give, ALL, 16)

        q_got, a_mine = tie(q_got, a_mine)
        grad_outer, _ = finish(at, q_pair, q_got)

        a_got, grad_outer = tie(a_got, grad_outer)
        reduced = a_mine.astype(F32) + a_got.astype(F32)

        p_got, reduced = tie(p_got, reduced)
        grad_inner, grad_inner_bias = finish(at, p_pair, p_got)
    else:
        grad_outer = lax.psum(outer_mine.astype(F32) + outer_y.astype(F32), "dp").reshape(-1, D)
        grad_rows = tokens_backward(inner_give)
        grads = weights_backward(inner_give)
        inner = add_low(inner_keep, inner_got)
        layer_out = lax.all_gather(out, "mp", axis=0, tiled=True)
        grad_tokens = lax.all_gather(grad_rows, "mp", axis=0, tiled=True)
        inner = lax.psum(inner[0].astype(F32) + swap(inner[1], "mp", 2).astype(F32), "dp").reshape(-1, D)
        grad_inner, grad_inner_bias = inner[:D], inner[D]
        reduced = lax.psum_scatter(grads[0], ALL, scatter_dimension=0, tiled=True).astype(F32)
    reduced = reduced.reshape(rows_each, WIDE)
    vector = lambda i: reduced[:, 4 * D + MEM + i]
    return (
        layer_out,
        grad_tokens,
        reduced[:, 4 * D : 4 * D + MEM].T,
        reduced[:, :D],
        reduced[:, D : 2 * D],
        reduced[:, 2 * D : 3 * D],
        reduced[:, 3 * D : 4 * D],
        vector(0),
        vector(1),
        grad_inner,
        grad_inner_bias,
        grad_outer,
        vector(2),
        vector(3),
        vector(4),
    )


def solution(mesh):
    both = ("dp", "mp")
    in_specs = (
        P("dp", None),
        P("dp", None),
        P(None, both),
        P(both, None),
        P(both, None),
        P(both, None),
        P(both, None),
        P(both),
        P(both),
        P(None, "mp"),
        P("mp"),
        P("mp", None),
        P(both),
        P(both),
        P(both),
    )
    out_specs = (
        P("dp", None),
        P("dp", None),
        P(None, both),
        P(both, None),
        P(both, None),
        P(both, None),
        P(both, None),
        P(both),
        P(both),
        P(None, "mp"),
        P("mp"),
        P("mp", None),
        P(both),
        P(both),
        P(both),
    )
    return jax.shard_map(shards, mesh=mesh, in_specs=in_specs, out_specs=out_specs, check_vma=False)
```

```python
import functools

import jax
import jax.numpy as jnp
from jax import lax
from jax.experimental import pallas as pl
from jax.experimental.pallas import tpu as pltpu
from jax.sharding import PartitionSpec as P

D = 512
HEADS = 8
HEAD = 64
MEM = 20
PAD = 32
SPAN = 512
SPANS = 2
EXTRA = 128
WIDE = 4 * D + EXTRA
EPS = 1e-05
GELU_A = 0.7978845608028654
GELU_B = 0.044715
LOW = jnp.bfloat16
F32 = jnp.float32
SCALE = HEAD ** (-0.5)
ALL = ("dp", "mp")

VMEM = pl.BlockSpec(memory_space=pltpu.VMEM)
SMEM = pl.BlockSpec(memory_space=pltpu.SMEM)
ANY = pl.BlockSpec(memory_space=pl.ANY)


def dg(a, b, ca, cb):
    return lax.dot_general(a, b, (((ca,), (cb,)), ((), ())), preferred_element_type=F32)


def iota(shape, dim):
    return lax.broadcasted_iota(jnp.int32, shape, dim)


def head_mask(heads):
    shape = (heads * PAD, heads * HEAD)
    return (iota(shape, 0) >> 5) == (iota(shape, 1) >> 6)


def block_diagonal(rows):
    heads = rows.shape[1] // HEAD
    tall = jnp.concatenate([rows] * heads, axis=0)
    return jnp.where(head_mask(heads), tall, 0.0).astype(LOW)


def diagonal_sum(tall):
    heads = tall.shape[1] // HEAD
    kept = jnp.where(head_mask(heads), tall, 0.0)
    total = kept[:PAD]
    for h in range(1, heads):
        total = total + kept[h * PAD : (h + 1) * PAD]
    return total


def normalize(values):
    mean = jnp.mean(values, axis=1, keepdims=True)
    center = values - mean
    spread = jnp.mean(center * center, axis=1, keepdims=True)
    inv = lax.rsqrt(spread + EPS)
    return center * inv, inv


def gelu_parts(a):
    sq = a * a
    t = jnp.tanh(a * (GELU_A + (GELU_A * GELU_B) * sq))
    half = 0.5 * (1.0 + t)
    return half, t, sq


def gelu(a):
    half, _, _ = gelu_parts(a)
    return a * half


def call(kernel, out_shape, in_specs, out_specs, scratch=(), flops=1, bytes_=1, mib=32):
    return pl.pallas_call(
        kernel,
        out_shape=out_shape,
        in_specs=in_specs,
        out_specs=out_specs,
        scratch_shapes=list(scratch),
        compiler_params=pltpu.CompilerParams(vmem_limit_bytes=mib * 2**20),
        cost_estimate=pl.CostEstimate(flops=flops, bytes_accessed=bytes_, transcendentals=0),
    )


def sds(shape, dtype):
    return jax.ShapeDtypeStruct(shape, dtype)


def pack_kernel(q_ref, k_ref, v_ref, o_ref, mem_ref, g1_ref, b1_ref, ob_ref, g2_ref, b2_ref, out_ref, tall):
    rows = q_ref.shape[0]
    for i, ref in enumerate((q_ref, k_ref, v_ref, o_ref)):
        out_ref[:, i * D : (i + 1) * D] = ref[...]
    tall[...] = jnp.zeros(tall.shape, F32)
    for i, ref in enumerate((g1_ref, b1_ref, ob_ref, g2_ref, b2_ref)):
        tall[MEM + i : MEM + i + 1, :rows] = ref[...].astype(F32)
    out_ref[:, 4 * D :] = tall[...].T[:rows].astype(LOW)
    out_ref[:, 4 * D : 4 * D + MEM] = mem_ref[...]


def assemble(me, pieces, bits, out_ref):
    for piece, offsets in zip(pieces, bits, strict=True):
        if offsets is None:
            out_ref[...] = piece[...]
            continue
        size = piece.shape[0] // len(offsets)
        for j, offset in enumerate(offsets):
            start = pl.multiple_of((me ^ offset) * size, size)
            out_ref[pl.ds(start, size), :] = piece[j * size : (j + 1) * size, :]


def project_kernel(bits, at_ref, *refs):
    n = len(bits)
    x_ref, w_ref, qkv_ref = refs[n:]
    assemble(at_ref[0], refs[:n], bits, w_ref)
    x_t = x_ref[...].T
    qkv_ref[:D] = (dg(w_ref[:, :D], x_t, 0, 0).astype(LOW).astype(F32) * SCALE).astype(LOW)
    qkv_ref[D : 3 * D] = dg(w_ref[:, D : 3 * D], x_t, 0, 0).astype(LOW)


def attend_kernel(qkv_ref, p_ref, o_ref, m_ref, l_ref):
    def scores(h):
        at = h * HEAD
        return dg(qkv_ref[D + at : D + at + HEAD], qkv_ref[at : at + HEAD], 0, 0)

    s_next = scores(0)
    for h in range(HEADS):
        s = s_next
        if h + 1 < HEADS:
            s_next = scores(h + 1)
        at = h * HEAD
        m = jnp.max(s, axis=0, keepdims=True)
        p = jnp.exp(s - m)
        m_ref[h : h + 1] = m
        l_ref[h : h + 1] = jnp.sum(p, axis=0, keepdims=True)
        p_ref[h] = p.astype(LOW)
        o_ref[at : at + HEAD] = dg(qkv_ref[2 * D + at : 2 * D + at + HEAD], p_ref[h], 1, 0)


def memory_kernel(x1_ref, w_ref, nm_ref, small_ref):
    small = w_ref[:, 4 * D :].T.astype(F32)[:PAD]
    small_ref[...] = small
    mem = jnp.where(iota((PAD, D), 0) < MEM, small, 0.0)
    packed = dg(mem.astype(LOW), w_ref[:, : 3 * D], 1, 0).astype(LOW)
    q_tall = block_diagonal(packed[:, :D].astype(F32) * SCALE)
    s_mem = dg(q_tall, packed[:, D : 2 * D], 1, 1)
    s_mem = jnp.where(iota(s_mem.shape, 1) < MEM, s_mem, -1e30)
    kv = dg(x1_ref[...], w_ref[:, D : 3 * D], 1, 0).astype(LOW)
    s = dg(q_tall, kv[:, :D], 1, 1)
    m = jnp.maximum(jnp.max(s, axis=1, keepdims=True), jnp.max(s_mem, axis=1, keepdims=True))
    p = jnp.exp(s - m)
    p_mem = jnp.exp(s_mem - m)
    total = jnp.sum(p, axis=1, keepdims=True) + jnp.sum(p_mem, axis=1, keepdims=True)
    o = dg(p.astype(LOW), kv[:, D:], 1, 0) + dg(p_mem.astype(LOW), packed[:, 2 * D :], 1, 0)
    mixed = diagonal_sum(o / total).astype(LOW)
    xhat, _ = normalize(mem + dg(mixed, w_ref[:, 3 * D : 4 * D], 1, 0))
    nm_ref[...] = xhat * small[MEM : MEM + 1] + small[MEM + 1 : MEM + 2]


def forward_kernel(
    at_ref, nm_ref, small_ref, x_ref, w_ref, qkv_ref, o_ref, m_ref, l_ref,
    wi0, wi1, wi2, wi3, wo0, wo1, wo2, wo3, cot_ref,
    out_ref, keep_ref, send_ref, slope_ref, nl_ref, gl_ref, gs_ref, xhat_ref, inv_ref,
    mixed_ref, mem_ref, kv_ref, pm_ref, c_ref, cm_ref, vec_ref, hid,
):
    wis, wos = (wi0, wi1, wi2, wi3), (wo0, wo1, wo2, wo3)
    shifts = [ref[D : D + 1].astype(F32) for ref in wos]
    small = small_ref[...]
    gain1, bias1, outer_b, gain2, bias2 = (small[MEM + i : MEM + i + 1] for i in range(5))
    later, first = at_ref[2], at_ref[5]
    nm = nm_ref[...]
    nm_low = nm.astype(LOW)
    value = nm + outer_b
    for k in range(4):
        inner = dg(nm_low, wis[k][...], 1, 0) + shifts[k]
        value = value + dg(gelu(inner).astype(LOW), wos[k][:D], 1, 0)
    carried, _ = normalize(value)
    carried = carried * gain2 + bias2
    mem = jnp.where(later == 1, carried, small)
    mem = jnp.where(iota((PAD, D), 0) < MEM, mem, 0.0)
    mem_ref[...] = mem
    kv_mem = dg(mem.astype(LOW), w_ref[:, D : 3 * D], 1, 0).astype(LOW)
    kv_ref[...] = kv_mem
    k_tall = block_diagonal(kv_mem[:, :D].astype(F32))
    v_tall = block_diagonal(kv_mem[:, D:].astype(F32))
    s_all = dg(k_tall, qkv_ref[:D], 1, 0)
    s_all = jnp.where((iota(s_all.shape, 0) & (PAD - 1)) < MEM, s_all, -1e30)
    alphas, invs = [], []
    for h in range(HEADS):
        s = s_all[h * PAD : (h + 1) * PAD]
        m_old = m_ref[h : h + 1]
        m = jnp.maximum(m_old, jnp.max(s, axis=0, keepdims=True))
        alpha = jnp.exp(m_old - m)
        p = jnp.exp(s - m)
        inv = 1.0 / (l_ref[h : h + 1] * alpha + jnp.sum(p, axis=0, keepdims=True))
        pm_ref[h * PAD : (h + 1) * PAD] = p.astype(LOW)
        c_ref[h : h + 1] = alpha * inv
        cm_ref[h : h + 1] = inv
        alphas.append(alpha * inv)
        invs.append(inv)
    o_mem = dg(v_tall, pm_ref[...], 0, 0)
    for h in range(HEADS):
        at = h * HEAD
        mixed_ref[at : at + HEAD] = (
            o_ref[at : at + HEAD] * alphas[h] + o_mem[at : at + HEAD] * invs[h]
        ).astype(LOW)
    xhat1, inv1 = normalize(
        x_ref[...].astype(F32) + dg(mixed_ref[...], w_ref[:, 3 * D : 4 * D], 0, 0)
    )
    xhat_ref[...] = xhat1
    inv_ref[...] = inv1
    normed = xhat1 * gain1 + bias1
    normed_low = normed.astype(LOW)
    nl_ref[...] = normed_low
    total = normed + outer_b
    for k in range(4):
        a = dg(normed_low, wis[k][...], 1, 0) + shifts[k]
        half, t, sq = gelu_parts(a)
        hid[k] = (a * half).astype(LOW)
        slope = half + (0.5 * a) * (1.0 - t * t) * (GELU_A + (3.0 * GELU_A * GELU_B) * sq)
        slope_ref[k] = slope.astype(LOW)
        total = total + dg(hid[k], wos[k][:D], 1, 0)
    xhat2, inv2 = normalize(total)
    out_ref[...] = (xhat2 * gain2 + bias2).astype(LOW)
    cot = cot_ref[...].astype(F32)
    pull = cot * gain2
    grad_sum = inv2 * (
        pull
        - jnp.mean(pull, axis=1, keepdims=True)
        - xhat2 * jnp.mean(pull * xhat2, axis=1, keepdims=True)
    )
    vec_ref[2:3] = jnp.sum(grad_sum, axis=0, keepdims=True)
    vec_ref[3:4] = jnp.sum(cot * xhat2, axis=0, keepdims=True)
    vec_ref[4:5] = jnp.sum(cot, axis=0, keepdims=True)
    gs_ref[...] = grad_sum
    grad_low = grad_sum.astype(LOW)
    gl_ref[...] = grad_low
    for k in (1, 3, 0, 2):
        give(send_ref if k % 2 else keep_ref, k // 2, dg(hid[k], grad_low, 0, 0), first)


def give(ref, k, rows, first):
    size = rows.shape[0] // 4
    for i in range(4):
        ref[k, first ^ i] = rows[i * size : (i + 1) * size].astype(LOW)


def inner_terms(k, wi_ref, wo_ref, slope_ref, normed_low, grad_low, ref, first):
    gi = slope_ref[k].astype(F32) * dg(grad_low, wo_ref[:D], 1, 1)
    gi_low = gi.astype(LOW)
    bias = jnp.sum(gi_low.astype(F32), axis=0, keepdims=True)
    bias = jnp.where(iota((PAD, D), 0) == 0, bias, 0.0)
    rows = jnp.concatenate([dg(normed_low, gi_low, 0, 0), bias], axis=0)
    give(ref, k // 2, rows, first)
    return dg(gi_low, wi_ref[...], 1, 1)


def send_kernel(at_ref, wi1, wi3, wo1, wo3, slope_ref, nl_ref, gl_ref, gs_ref, send_ref, back_ref):
    first = at_ref[5]
    back = gs_ref[...]
    for k, wi_ref, wo_ref in ((1, wi1, wo1), (3, wi3, wo3)):
        back = back + inner_terms(k, wi_ref, wo_ref, slope_ref, nl_ref[...], gl_ref[...], send_ref, first)
    back_ref[...] = back


def keep_kernel(
    at_ref, after_ref, small_ref, w_ref, wi0, wi2, wo0, wo2, slope_ref, nl_ref, gl_ref, back_ref, xhat_ref, inv_ref, mixed_ref,
    keep_ref, resid_ref, dwo_ref, gmix_ref, vec_ref,
):
    first = at_ref[5]
    back = back_ref[...]
    for k, wi_ref, wo_ref in ((0, wi0, wo0), (2, wi2, wo2)):
        back = back + inner_terms(k, wi_ref, wo_ref, slope_ref, nl_ref[...], gl_ref[...], keep_ref, first)
    xhat1 = xhat_ref[...]
    vec_ref[0:1] = jnp.sum(back * xhat1, axis=0, keepdims=True)
    vec_ref[1:2] = jnp.sum(back, axis=0, keepdims=True)
    pull = back * small_ref[MEM : MEM + 1]
    resid = inv_ref[...] * (
        pull
        - jnp.mean(pull, axis=1, keepdims=True)
        - xhat1 * jnp.mean(pull * xhat1, axis=1, keepdims=True)
    )
    resid_ref[...] = resid
    resid_low = resid.astype(LOW)
    dwo_ref[...] = dg(mixed_ref[...], resid_low, 1, 0).astype(LOW)
    gmix_ref[...] = dg(w_ref[:, 3 * D : 4 * D], resid_low, 1, 1).astype(LOW)


def heads_kernel(
    low_h, high_h, after_ref, qkv_ref, p_ref, pm_ref, mixed_ref, c_ref, cm_ref, gmix_ref, kv_ref, gp_ref, gm_ref,
    do_m, ds_m,
):
    heads = range(low_h, high_h)
    f0, f1 = low_h * HEAD, high_h * HEAD
    m0, m1 = low_h * PAD, high_h * PAD
    k_tall = block_diagonal(kv_ref[:, f0:f1].astype(F32))
    v_tall = block_diagonal(kv_ref[:, D + f0 : D + f1].astype(F32))
    deltas = []
    for i, h in enumerate(heads):
        at = h * HEAD
        do = gmix_ref[at : at + HEAD].astype(F32)
        deltas.append(
            jnp.sum(do * mixed_ref[at : at + HEAD].astype(F32), axis=0, keepdims=True)
        )
        do_m[i * HEAD : (i + 1) * HEAD] = (do * cm_ref[h : h + 1]).astype(LOW)
    da_m = dg(v_tall, do_m[...], 1, 0)
    for i, h in enumerate(heads):
        rows = slice(i * PAD, (i + 1) * PAD)
        p = pm_ref[h * PAD : (h + 1) * PAD].astype(F32)
        ds_m[rows] = (p * (da_m[rows] - deltas[i] * cm_ref[h : h + 1])).astype(LOW)
    gm_ref[0] = diagonal_sum(dg(ds_m[...], qkv_ref[f0:f1], 1, 1))
    gm_ref[1] = diagonal_sum(dg(pm_ref[m0:m1], do_m[...], 1, 1))
    dq_mem = dg(k_tall, ds_m[...], 0, 0)
    for i, h in enumerate(heads):
        at = h * HEAD
        rows = slice(i * HEAD, (i + 1) * HEAD)
        c = c_ref[h : h + 1]
        do = (gmix_ref[at : at + HEAD].astype(F32) * c).astype(LOW)
        p = p_ref[h]
        da = dg(qkv_ref[2 * D + at : 2 * D + at + HEAD], do, 0, 0)
        ds = (p.astype(F32) * (da - deltas[i] * c)).astype(LOW)
        gp_ref[2, rows] = dg(do, p, 1, 1).astype(LOW)
        gp_ref[1, rows] = dg(qkv_ref[at : at + HEAD], ds, 1, 1).astype(LOW)
        gp_ref[0, rows] = (
            SCALE * (dg(qkv_ref[D + at : D + at + HEAD], ds, 1, 0) + dq_mem[rows])
        ).astype(LOW)


def weights_kernel(
    bits, after_ref, at_ref, x_ref, w_ref, mem_ref, gp0_ref, gp1_ref, gm0_ref, gm1_ref, dwo_ref, vec_ref, vec1_ref, *rest
):
    g_refs, wext = rest[: len(bits)], rest[len(bits)]
    me = at_ref[0]
    mem_low = mem_ref[...].astype(LOW)
    x_t = x_ref[...].T
    width = gp0_ref.shape[1]
    for part, (gp_ref, gm_ref) in enumerate(((gp0_ref, gm0_ref), (gp1_ref, gm1_ref))):
        for i in range(3):
            grad = dg(x_t, gp_ref[i], 1, 1)
            if i > 0:
                grad = grad + dg(mem_low, gm_ref[i - 1].astype(LOW), 0, 0)
            at = i * D + part * width
            wext[:, at : at + width] = grad.astype(LOW)
    wext[:, 3 * D : 4 * D] = dwo_ref[...]
    gp_mem = jnp.concatenate([gm0_ref[0], gm1_ref[0], gm0_ref[1], gm1_ref[1]], axis=1).astype(LOW)
    g_mem = dg(gp_mem, w_ref[:, D : 3 * D], 1, 1)
    g_mem = jnp.where(at_ref[2] == 0, g_mem, 0.0)
    row = iota((EXTRA, D), 0)
    tall = jnp.concatenate([g_mem, jnp.zeros((EXTRA - PAD, D), F32)], axis=0)
    tall = jnp.where(row < MEM, tall, 0.0)
    for i in range(5):
        tall = jnp.where(row == MEM + i, (vec1_ref if i < 2 else vec_ref)[i : i + 1], tall)
    wext[:, 4 * D :] = tall.T.astype(LOW)
    for g_ref, offsets in zip(g_refs, bits, strict=True):
        if offsets is None:
            g_ref[...] = wext[...]
            continue
        size = g_ref.shape[0] // len(offsets)
        for j, offset in enumerate(offsets):
            start = pl.multiple_of((me ^ offset) * size, size)
            g_ref[j * size : (j + 1) * size] = wext[pl.ds(start, size), :]


def tokens_kernel(after_ref, w_ref, gp0_ref, gp1_ref, resid_ref, tok_ref):
    width = gp0_ref.shape[1]
    total = jnp.zeros((D, SPAN), F32)
    for part, gp_ref in enumerate((gp0_ref, gp1_ref)):
        for i in range(3):
            at = i * D + part * width
            total = total + dg(w_ref[:, at : at + width], gp_ref[i], 1, 0)
    tok_ref[...] = (total.T + resid_ref[...]).astype(LOW)


def place_kernel(at_ref, r0, r1, r2, r3, out_ref, sems):
    me = at_ref[3]
    copies = [pltpu.make_async_copy(ref, out_ref.at[me ^ k], sems.at[k]) for k, ref in enumerate((r0, r1, r2, r3))]
    for copy in copies:
        copy.start()
    for copy in copies:
        copy.wait()


def place(at, pieces):
    rows = call(
        place_kernel,
        sds((4,) + pieces[0].shape, pieces[0].dtype),
        [SMEM] + [VMEM] * 4,
        ANY,
        [pltpu.SemaphoreType.DMA((4,))],
        mib=8,
    )(at, *pieces)
    return rows.reshape(-1, D)


def finish_kernel(at_ref, own_ref, other_ref, out_ref, bias_ref, held):
    first = at_ref[5]
    size = own_ref.shape[1]
    for i, ref in enumerate((own_ref, other_ref)):
        for j in range(2):
            start = pl.multiple_of((first ^ (2 * i + j)) * size, size)
            held[pl.ds(start, size), :] = ref[j].astype(F32)
    out_ref[...] = held[:D]
    bias_ref[...] = held[held.shape[0] - PAD : held.shape[0] - PAD + 1]


def closing_kernel(at_ref, r0, r1, r2, r3, own_ref, other_ref, mine_ref, got_ref, rows_ref, out_ref, *rest):
    memory_ref, *square_refs, held, sems = rest
    squares, vectors = square_refs[:4], square_refs[4:]
    me, first = at_ref[3], at_ref[5]
    copies = [pltpu.make_async_copy(ref, rows_ref.at[me ^ k], sems.at[k]) for k, ref in enumerate((r0, r1, r2, r3))]
    for copy in copies:
        copy.start()
    size = own_ref.shape[1]
    for i, ref in enumerate((own_ref, other_ref)):
        for j in range(2):
            start = pl.multiple_of((first ^ (2 * i + j)) * size, size)
            out_ref[pl.ds(start, size), :] = ref[j].astype(F32)
    total = mine_ref[0].astype(F32) + got_ref[0].astype(F32)
    for i, ref in enumerate(squares):
        ref[...] = total[:, i * D : (i + 1) * D]
    memory_ref[...] = total[:, 4 * D : 4 * D + MEM]
    held[...] = jnp.zeros(held.shape, F32)
    held[: total.shape[0]] = total[:, 4 * D :]
    tall = held[...].T
    for i, ref in enumerate(vectors):
        ref[...] = tall[MEM + i : MEM + i + 1, : total.shape[0]]
    for copy in copies:
        copy.wait()


def closing(at, rows, pair, other, mine, got):
    n = mine.shape[1]
    shapes = [sds((4,) + rows[0].shape, LOW), sds((D, D), F32), sds((n, MEM), F32)]
    shapes += [sds((n, D), F32)] * 4 + [sds((1, n), F32)] * 5
    grad_tokens, grad_outer, grad_memory, *others = call(
        closing_kernel,
        shapes,
        [SMEM] + [VMEM] * 8,
        [ANY] + [VMEM] * (len(shapes) - 1),
        [pltpu.VMEM((EXTRA, EXTRA), F32), pltpu.SemaphoreType.DMA((4,))],
        mib=16,
    )(at, *rows, pair, other, mine, got)
    vectors = [v.reshape(-1) for v in others[4:]]
    return grad_tokens.reshape(-1, D), grad_outer, [grad_memory.T, *others[:4], *vectors]


def swap(value, axis, bit):
    n = lax.axis_size(axis)
    return lax.ppermute(value, axis, [(i, i ^ bit) for i in range(n)])


def tie(*values):
    return lax.optimization_barrier(values)


def add_low(*terms):
    return functools.reduce(jnp.add, [t.astype(F32) for t in terms]).astype(LOW)


def finish(at, pair, other):
    grad, bias = call(
        finish_kernel,
        [sds((D, D), F32), sds((1, D), F32)],
        [SMEM] + [VMEM] * 2,
        [VMEM] * 2,
        [pltpu.VMEM((4 * pair.shape[1], D), F32)],
        bytes_=2 * 2**20,
    )(at, pair, other)
    return grad, bias[0]


def split(reduced):
    reduced = reduced.reshape(-1, WIDE)
    squares = [reduced[:, i * D : (i + 1) * D] for i in range(4)]
    vectors = [reduced[:, 4 * D + MEM + i] for i in range(5)]
    return [reduced[:, 4 * D : 4 * D + MEM].T, *squares, *vectors]


def shards(
    tokens, cotangent, memory_init, query_weight, key_weight, value_weight, output_weight, first_gain,
    first_bias, inner_weight, inner_bias, outer_weight, outer_bias, second_gain, second_bias,
):
    n_dp, n_mp = lax.axis_size("dp"), lax.axis_size("mp")
    rows_each = query_weight.shape[0]
    by_bits = n_dp == 8 and n_mp == 4 and rows_each % 16 == 0
    me_mp, me_dp = lax.axis_index("mp"), lax.axis_index("dp")
    me = me_dp * n_mp + me_mp
    later = me_mp % SPANS
    x = (me_dp & 1) if by_bits else 0
    first = (x * 2 + ((me_dp >> 1) & 1)) if by_bits else 0
    at = jnp.stack([me, me_mp // SPANS, later, me_mp, me_dp, first, x]).astype(jnp.int32)

    pick = lambda v, i: lax.dynamic_index_in_dim(v, i, 0, keepdims=False)
    blocks = tokens.reshape(-1, SPAN, D)
    own = pick(blocks, me_mp)
    start = pick(blocks, me_mp - later)
    cot = pick(cotangent.reshape(-1, SPAN, D), me_mp)

    wi_halves = inner_weight.reshape(2, D // 2, D)
    wi_near = swap(pick(wi_halves, x), "mp", 2)
    outer_rows = jnp.concatenate([outer_weight, inner_bias.reshape(1, -1), jnp.zeros((15, D), LOW)], axis=0)

    vectors = (first_gain, first_bias, outer_bias, second_gain, second_bias)
    local = call(
        pack_kernel,
        sds((rows_each, WIDE), LOW),
        [VMEM] * 10,
        VMEM,
        [pltpu.VMEM((EXTRA, EXTRA), F32)],
        mib=56,
    )(query_weight, key_weight, value_weight, output_weight, memory_init.T, *[v.reshape(1, -1) for v in vectors])
    wo2 = swap(outer_rows, "mp", 2)
    if by_bits:
        line = [local] + [swap(local, ALL, 8 * j) for j in range(1, 4)]
        *line, wi_near = tie(*line, wi_near)
        wi_far = swap(wi_near, "dp", 1)
        line = jnp.concatenate(line, axis=0)
        plane = [line] + [swap(line, ALL, 2 * b) for b in range(1, 4)]
        wi2 = jnp.where(x == 0, jnp.concatenate([wi_near, wi_far]), jnp.concatenate([wi_far, wi_near]))
        plane[1], own, start, cot = tie(plane[1], own, start, cot)
        *plane, wo2, wi2 = tie(*plane, wo2, wi2)
        pieces = plane + [swap(piece, ALL, 1) for piece in plane]
        bits = [[2 * b + c + 8 * j for j in range(4)] for c in range(2) for b in range(4)]
    else:
        pieces = [lax.all_gather(local, ALL, axis=0, tiled=True)]
        bits = [None]
        wi2 = jnp.concatenate([wi_near, swap(wi_halves[1], "mp", 2)])
    wi1, wo1, wi3, wo3 = [swap(v, "mp", 1) for v in (inner_weight, outer_rows, wi2, wo2)]

    w, qkv = call(
        functools.partial(project_kernel, bits),
        [sds((D, WIDE), LOW), sds((3 * D, SPAN), LOW)],
        [SMEM] + [VMEM] * (len(pieces) + 1),
        [VMEM] * 2,
        flops=2 * 10**9,
        bytes_=5 * 2**20,
    )(at, *pieces, own)
    p, o, m, l = call(
        attend_kernel,
        [
            sds((HEADS, SPAN, SPAN), LOW),
            sds((D, SPAN), F32),
            sds((HEADS, SPAN), F32),
            sds((HEADS, SPAN), F32),
        ],
        [VMEM],
        [VMEM] * 4,
        flops=5 * 10**9,
        bytes_=7 * 2**20,
    )(qkv)

    nm, small = call(
        memory_kernel,
        [sds((PAD, D), F32), sds((PAD, D), F32)],
        [VMEM] * 2,
        [VMEM] * 2,
        flops=3 * 10**9,
        bytes_=4 * 2**20,
        mib=16,
    )(start, w)
    nm, m, wi1, wi3, wo1, wo3 = tie(nm, m, wi1, wi3, wo1, wo3)

    outer_shape = sds((2, 4, D // 4, D), LOW)
    inner_shape = sds((2, 4, (D + PAD) // 4, D), LOW)
    square, square_low = sds((SPAN, D), F32), sds((SPAN, D), LOW)
    (
        out, outer_keep, outer_send, slope, normed, grad_low, grad_sum, xhat, inv, mixed, mem, kv_mem, p_mem, c, c_mem, vecs,
    ) = call(
        forward_kernel,
        [
            square_low,
            outer_shape,
            outer_shape,
            sds((4, SPAN, D), LOW),
            square_low,
            square_low,
            square,
            square,
            sds((SPAN, 1), F32),
            sds((D, SPAN), LOW),
            sds((PAD, D), F32),
            sds((PAD, 2 * D), LOW),
            sds((HEADS * PAD, SPAN), LOW),
            sds((HEADS, SPAN), F32),
            sds((HEADS, SPAN), F32),
            sds((8, D), F32),
        ],
        [SMEM] + [VMEM] * 17,
        [VMEM] * 16,
        [pltpu.VMEM((4, SPAN, D), LOW)],
        flops=10 * 10**9,
        bytes_=14 * 2**20,
    )(
        at, nm, small, own, w, qkv, o, m, l, inner_weight, wi1, wi2, wi3, outer_rows, wo1, wo2, wo3, cot,
    )
    wis, wos = (inner_weight, wi1, wi2, wi3), (outer_rows, wo1, wo2, wo3)

    outer_got = swap(outer_send, "mp", 1)

    inner_send, back = call(
        send_kernel,
        [inner_shape, square],
        [SMEM] + [VMEM] * 8,
        [VMEM] * 2,
    )(at, wis[1], wis[3], wos[1], wos[3], slope, normed, grad_low, grad_sum)
    inner_got = swap(inner_send, "mp", 1)

    outer_mine, outer_give = add_low(outer_keep[0], outer_got[0]), add_low(outer_keep[1], outer_got[1])
    outer_y = swap(outer_give, "mp", 2)

    inner_keep, resid, d_mix, g_mixed, vecs1 = call(
        keep_kernel,
        [
            inner_shape,
            square,
            sds((D, D), LOW),
            sds((D, SPAN), LOW),
            sds((8, D), F32),
        ],
        [SMEM, ANY] + [VMEM] * 13,
        [VMEM] * 5,
    )(at, outer_give, small, w, wis[0], wis[2], wos[0], wos[2], slope, normed, grad_low, back, xhat, inv, mixed)

    half = HEADS // 2
    some = half * HEAD

    def heads_backward(low_h, gate):
        return call(
            functools.partial(heads_kernel, low_h, low_h + half),
            [sds((3, some, SPAN), LOW), sds((2, PAD, some), F32)],
            [ANY] + [VMEM] * 8,
            [VMEM] * 2,
            [
                pltpu.VMEM((some, SPAN), LOW),
                pltpu.VMEM((half * PAD, SPAN), LOW),
            ],
        )(gate, qkv, p, p_mem, mixed, c, c_mem, g_mixed, kv_mem)

    if by_bits:
        inner_give = add_low(inner_keep[:, 2:], inner_got[:, 2:])
        inner_mine = add_low(inner_keep[:, :2], inner_got[:, :2])
        inner_x = swap(inner_give, "dp", 1)
    else:
        inner_give = inner_got
    gp0, gm0 = heads_backward(0, inner_give)
    gp1, gm1 = heads_backward(half, inner_give)

    if by_bits:
        out_bits = [[[2 * b + c + 8 * j for j in (0, 2, 1, 3)] for b in range(4)] for c in range(2)]
        out_bits = [sum(out_bits[0], []), *out_bits[1]]
    else:
        out_bits = [None]

    def weights_backward(gate):
        return call(
            functools.partial(weights_kernel, out_bits),
            [sds((len(o) * rows_each if o else D, WIDE), LOW) for o in out_bits],
            [ANY, SMEM] + [VMEM] * 10,
            [VMEM] * len(out_bits),
            [pltpu.VMEM((D, WIDE), LOW)],
        )(gate, at, own, w, mem, gp0, gp1, gm0, gm1, d_mix, vecs, vecs1)

    def tokens_backward(gate):
        return call(tokens_kernel, sds((SPAN, D), LOW), [ANY] + [VMEM] * 4, VMEM)(gate, w, gp0, gp1, resid)

    if by_bits:
        halves_of = lambda v: (v[: v.shape[0] // 2], v[v.shape[0] // 2 :])
        both = lambda mine, got: [add_low(u, v) for u, v in zip(halves_of(mine), halves_of(got), strict=True)]

        a_mine, *a_give = [g.reshape(-1, rows_each, WIDE) for g in weights_backward(inner_give)]
        a_got = [swap(g, ALL, 1) for g in a_give]

        grad_rows = tokens_backward(inner_give)
        rows_got = swap(grad_rows, "mp", 1)

        outer_y, grad_rows, a_mine = tie(outer_y, grad_rows, a_mine)
        q_mine, q_give = both(outer_mine, outer_y)
        q_got = swap(q_give, "dp", 1)

        inner_x, q_mine = tie(inner_x, q_mine)
        p_mine, p_give = add_low(inner_mine[0], inner_x[0]), add_low(inner_mine[1], inner_x[1])
        p_got = swap(p_give, "mp", 2)

        *a_got, p_mine = tie(*a_got, p_mine)
        a_mine, a_give = both(a_mine, jnp.concatenate(a_got))
        a_got = swap(a_give, ALL, 4)

        q_got, a_mine = tie(q_got, a_mine)
        q_mine, q_give = [v[0] for v in both(q_mine, q_got)]
        q_got = swap(q_give, "dp", 2)

        grad_rows, q_mine = tie(grad_rows, q_mine)
        rows_across = swap(grad_rows, "mp", 2)

        p_got, grad_rows = tie(p_got, grad_rows)
        p_mine, p_give = [v[0] for v in both(p_mine, p_got)]
        p_got = swap(p_give, "dp", 2)

        q_got, p_mine = tie(q_got, p_mine)
        q_mine = add_low(q_mine, q_got)
        q_got = swap(q_mine, "dp", 4)

        out, q_mine = tie(out, q_mine)
        out_got, out_across = swap(out, "mp", 1), swap(out, "mp", 2)

        p_got, out = tie(p_got, out)
        p_mine = add_low(p_mine, p_got)
        p_got = swap(p_mine, "dp", 4)

        a_got, p_mine = tie(a_got, p_mine)
        a_mine, a_give = both(a_mine, a_got)
        a_got = swap(a_give, ALL, 2)

        q_got, a_mine = tie(q_got, a_mine)
        q_mine = add_low(q_mine, q_got)
        q_got = swap(q_mine, "dp", 2)

        rows_across, q_mine = tie(rows_across, q_mine)
        rows_last = swap(rows_across, "mp", 1)

        a_got, rows_across = tie(a_got, rows_across)
        a_mine, a_give = both(a_mine, a_got)
        a_got = swap(a_give, ALL, 8)

        p_got, a_mine = tie(p_got, a_mine)
        p_mine = add_low(p_mine, p_got)
        p_got = swap(p_mine, "dp", 2)

        q_got, p_mine = tie(q_got, p_mine)
        q_pair = jnp.stack([q_mine, q_got])
        q_got = swap(q_pair, "dp", 1)

        out_across, q_pair = tie(out_across, q_pair)
        out_last = swap(out_across, "mp", 1)

        p_got, out_across = tie(p_got, out_across)
        p_pair = jnp.stack([p_mine, p_got])
        p_got = swap(p_pair, "dp", 1)

        a_got, p_pair = tie(a_got, p_pair)
        a_mine, a_give = both(a_mine, a_got)
        a_got = swap(a_give, ALL, 16)

        out_last, a_mine = tie(out_last, a_mine)
        layer_out = place(at, [out, out_got, out_across, out_last])

        rows_last, q_got, a_got, layer_out = tie(rows_last, q_got, a_got, layer_out)
        rows = [grad_rows, rows_got, rows_across, rows_last]
        grad_tokens, grad_outer, outputs = closing(at, rows, q_pair, q_got, a_mine, a_got)

        p_got, grad_outer = tie(p_got, grad_outer)
        grad_inner, grad_inner_bias = finish(at, p_pair, p_got)
    else:
        grad_outer = lax.psum(outer_mine.astype(F32) + outer_y.astype(F32), "dp").reshape(-1, D)
        grad_rows = tokens_backward(inner_give)
        grads = weights_backward(inner_give)
        inner = add_low(inner_keep, inner_got)
        layer_out = lax.all_gather(out, "mp", axis=0, tiled=True)
        grad_tokens = lax.all_gather(grad_rows, "mp", axis=0, tiled=True)
        inner = lax.psum(inner[0].astype(F32) + swap(inner[1], "mp", 2).astype(F32), "dp").reshape(-1, D)
        grad_inner, grad_inner_bias = inner[:D], inner[D]
        outputs = split(lax.psum_scatter(grads[0], ALL, scatter_dimension=0, tiled=True).astype(F32))
    grad_memory, grad_query, grad_key, grad_value, grad_output, *grad_vectors = outputs
    return (
        layer_out,
        grad_tokens,
        grad_memory,
        grad_query,
        grad_key,
        grad_value,
        grad_output,
        grad_vectors[0],
        grad_vectors[1],
        grad_inner,
        grad_inner_bias,
        grad_outer,
        *grad_vectors[2:],
    )


def solution(mesh):
    both = ("dp", "mp")
    in_specs = (
        P("dp", None),
        P("dp", None),
        P(None, both),
        P(both, None),
        P(both, None),
        P(both, None),
        P(both, None),
        P(both),
        P(both),
        P(None, "mp"),
        P("mp"),
        P("mp", None),
        P(both),
        P(both),
        P(both),
    )
    out_specs = (
        P("dp", None),
        P("dp", None),
        P(None, both),
        P(both, None),
        P(both, None),
        P(both, None),
        P(both, None),
        P(both),
        P(both),
        P(None, "mp"),
        P("mp"),
        P("mp", None),
        P(both),
        P(both),
        P(both),
    )
    return jax.shard_map(shards, mesh=mesh, in_specs=in_specs, out_specs=out_specs, check_vma=False)
```

```python
import functools

import jax
import jax.numpy as jnp
from jax import lax
from jax.experimental import pallas as pl
from jax.experimental.pallas import tpu as pltpu
from jax.sharding import PartitionSpec as P

D = 512
HEADS = 8
HEAD = 64
MEM = 20
PAD = 32
SPAN = 512
SPANS = 2
EXTRA = 128
WIDE = 4 * D + EXTRA
EPS = 1e-05
GELU_A = 0.7978845608028654
GELU_B = 0.044715
LOW = jnp.bfloat16
F32 = jnp.float32
SCALE = HEAD ** (-0.5)
ALL = ("dp", "mp")

VMEM = pl.BlockSpec(memory_space=pltpu.VMEM)
SMEM = pl.BlockSpec(memory_space=pltpu.SMEM)
ANY = pl.BlockSpec(memory_space=pl.ANY)


def dg(a, b, ca, cb):
    return lax.dot_general(a, b, (((ca,), (cb,)), ((), ())), preferred_element_type=F32)


def iota(shape, dim):
    return lax.broadcasted_iota(jnp.int32, shape, dim)


def head_mask(heads):
    shape = (heads * PAD, heads * HEAD)
    return (iota(shape, 0) >> 5) == (iota(shape, 1) >> 6)


def block_diagonal(rows):
    heads = rows.shape[1] // HEAD
    tall = jnp.concatenate([rows] * heads, axis=0)
    return jnp.where(head_mask(heads), tall, 0.0).astype(LOW)


def diagonal_sum(tall):
    heads = tall.shape[1] // HEAD
    kept = jnp.where(head_mask(heads), tall, 0.0)
    total = kept[:PAD]
    for h in range(1, heads):
        total = total + kept[h * PAD : (h + 1) * PAD]
    return total


def normalize(values):
    mean = jnp.mean(values, axis=1, keepdims=True)
    center = values - mean
    spread = jnp.mean(center * center, axis=1, keepdims=True)
    inv = lax.rsqrt(spread + EPS)
    return center * inv, inv


def gelu_parts(a):
    sq = a * a
    t = jnp.tanh(a * (GELU_A + (GELU_A * GELU_B) * sq))
    half = 0.5 * (1.0 + t)
    return half, t, sq


def gelu(a):
    half, _, _ = gelu_parts(a)
    return a * half


def call(kernel, out_shape, in_specs, out_specs, scratch=(), flops=1, bytes_=1, mib=32):
    return pl.pallas_call(
        kernel,
        out_shape=out_shape,
        in_specs=in_specs,
        out_specs=out_specs,
        scratch_shapes=list(scratch),
        compiler_params=pltpu.CompilerParams(vmem_limit_bytes=mib * 2**20),
        cost_estimate=pl.CostEstimate(flops=flops, bytes_accessed=bytes_, transcendentals=0),
    )


def sds(shape, dtype):
    return jax.ShapeDtypeStruct(shape, dtype)


def pack_kernel(q_ref, k_ref, v_ref, o_ref, mem_ref, g1_ref, b1_ref, ob_ref, g2_ref, b2_ref, out_ref, tall):
    rows = q_ref.shape[0]
    for i, ref in enumerate((q_ref, k_ref, v_ref, o_ref)):
        out_ref[:, i * D : (i + 1) * D] = ref[...]
    tall[...] = jnp.zeros(tall.shape, F32)
    for i, ref in enumerate((g1_ref, b1_ref, ob_ref, g2_ref, b2_ref)):
        tall[MEM + i : MEM + i + 1, :rows] = ref[...].astype(F32)
    out_ref[:, 4 * D :] = tall[...].T[:rows].astype(LOW)
    out_ref[:, 4 * D : 4 * D + MEM] = mem_ref[...]


def assemble(me, pieces, bits, out_ref):
    for piece, offsets in zip(pieces, bits, strict=True):
        if offsets is None:
            out_ref[...] = piece[...]
            continue
        size = piece.shape[0] // len(offsets)
        for j, offset in enumerate(offsets):
            start = pl.multiple_of((me ^ offset) * size, size)
            out_ref[pl.ds(start, size), :] = piece[j * size : (j + 1) * size, :]


def project_kernel(bits, at_ref, *refs):
    n = len(bits)
    x_ref, w_ref, qkv_ref = refs[n:]
    assemble(at_ref[0], refs[:n], bits, w_ref)
    x_t = x_ref[...].T
    qkv_ref[:D] = (dg(w_ref[:, :D], x_t, 0, 0).astype(LOW).astype(F32) * SCALE).astype(LOW)
    qkv_ref[D : 3 * D] = dg(w_ref[:, D : 3 * D], x_t, 0, 0).astype(LOW)


def attend_kernel(qkv_ref, p_ref, o_ref, m_ref, l_ref):
    def scores(h):
        at = h * HEAD
        return dg(qkv_ref[D + at : D + at + HEAD], qkv_ref[at : at + HEAD], 0, 0)

    s_next = scores(0)
    for h in range(HEADS):
        s = s_next
        if h + 1 < HEADS:
            s_next = scores(h + 1)
        at = h * HEAD
        m = jnp.max(s, axis=0, keepdims=True)
        p = jnp.exp(s - m)
        m_ref[h : h + 1] = m
        l_ref[h : h + 1] = jnp.sum(p, axis=0, keepdims=True)
        p_ref[h] = p.astype(LOW)
        o_ref[at : at + HEAD] = dg(qkv_ref[2 * D + at : 2 * D + at + HEAD], p_ref[h], 1, 0)


def memory_kernel(x1_ref, w_ref, nm_ref, small_ref):
    small = w_ref[:, 4 * D :].T.astype(F32)[:PAD]
    small_ref[...] = small
    mem = jnp.where(iota((PAD, D), 0) < MEM, small, 0.0)
    packed = dg(mem.astype(LOW), w_ref[:, : 3 * D], 1, 0).astype(LOW)
    q_tall = block_diagonal(packed[:, :D].astype(F32) * SCALE)
    s_mem = dg(q_tall, packed[:, D : 2 * D], 1, 1)
    s_mem = jnp.where(iota(s_mem.shape, 1) < MEM, s_mem, -1e30)
    kv = dg(x1_ref[...], w_ref[:, D : 3 * D], 1, 0).astype(LOW)
    s = dg(q_tall, kv[:, :D], 1, 1)
    m = jnp.maximum(jnp.max(s, axis=1, keepdims=True), jnp.max(s_mem, axis=1, keepdims=True))
    p = jnp.exp(s - m)
    p_mem = jnp.exp(s_mem - m)
    total = jnp.sum(p, axis=1, keepdims=True) + jnp.sum(p_mem, axis=1, keepdims=True)
    o = dg(p.astype(LOW), kv[:, D:], 1, 0) + dg(p_mem.astype(LOW), packed[:, 2 * D :], 1, 0)
    mixed = diagonal_sum(o / total).astype(LOW)
    xhat, _ = normalize(mem + dg(mixed, w_ref[:, 3 * D : 4 * D], 1, 0))
    nm_ref[...] = xhat * small[MEM : MEM + 1] + small[MEM + 1 : MEM + 2]


def forward_kernel(
    at_ref, nm_ref, small_ref, x_ref, w_ref, qkv_ref, o_ref, m_ref, l_ref,
    wi0, wi1, wi2, wi3, wo0, wo1, wo2, wo3, cot_ref,
    out_ref, keep_ref, send_ref, slope_ref, nl_ref, gl_ref, gs_ref, xhat_ref, inv_ref,
    mixed_ref, mem_ref, kv_ref, pm_ref, c_ref, cm_ref, vec_ref, hid,
):
    wis, wos = (wi0, wi1, wi2, wi3), (wo0, wo1, wo2, wo3)
    shifts = [ref[D : D + 1].astype(F32) for ref in wos]
    small = small_ref[...]
    gain1, bias1, outer_b, gain2, bias2 = (small[MEM + i : MEM + i + 1] for i in range(5))
    later, first = at_ref[2], at_ref[5]
    nm = nm_ref[...]
    nm_low = nm.astype(LOW)
    value = nm + outer_b
    for k in range(4):
        inner = dg(nm_low, wis[k][...], 1, 0) + shifts[k]
        value = value + dg(gelu(inner).astype(LOW), wos[k][:D], 1, 0)
    carried, _ = normalize(value)
    carried = carried * gain2 + bias2
    mem = jnp.where(later == 1, carried, small)
    mem = jnp.where(iota((PAD, D), 0) < MEM, mem, 0.0)
    mem_ref[...] = mem
    kv_mem = dg(mem.astype(LOW), w_ref[:, D : 3 * D], 1, 0).astype(LOW)
    kv_ref[...] = kv_mem
    k_tall = block_diagonal(kv_mem[:, :D].astype(F32))
    v_tall = block_diagonal(kv_mem[:, D:].astype(F32))
    s_all = dg(k_tall, qkv_ref[:D], 1, 0)
    s_all = jnp.where((iota(s_all.shape, 0) & (PAD - 1)) < MEM, s_all, -1e30)
    alphas, invs = [], []
    for h in range(HEADS):
        s = s_all[h * PAD : (h + 1) * PAD]
        m_old = m_ref[h : h + 1]
        m = jnp.maximum(m_old, jnp.max(s, axis=0, keepdims=True))
        alpha = jnp.exp(m_old - m)
        p = jnp.exp(s - m)
        inv = 1.0 / (l_ref[h : h + 1] * alpha + jnp.sum(p, axis=0, keepdims=True))
        pm_ref[h * PAD : (h + 1) * PAD] = p.astype(LOW)
        c_ref[h : h + 1] = alpha * inv
        cm_ref[h : h + 1] = inv
        alphas.append(alpha * inv)
        invs.append(inv)
    o_mem = dg(v_tall, pm_ref[...], 0, 0)
    for h in range(HEADS):
        at = h * HEAD
        mixed_ref[at : at + HEAD] = (
            o_ref[at : at + HEAD] * alphas[h] + o_mem[at : at + HEAD] * invs[h]
        ).astype(LOW)
    xhat1, inv1 = normalize(
        x_ref[...].astype(F32) + dg(mixed_ref[...], w_ref[:, 3 * D : 4 * D], 0, 0)
    )
    xhat_ref[...] = xhat1
    inv_ref[...] = inv1
    normed = xhat1 * gain1 + bias1
    normed_low = normed.astype(LOW)
    nl_ref[...] = normed_low
    total = normed + outer_b
    for k in range(4):
        a = dg(normed_low, wis[k][...], 1, 0) + shifts[k]
        half, t, sq = gelu_parts(a)
        hid[k] = (a * half).astype(LOW)
        slope = half + (0.5 * a) * (1.0 - t * t) * (GELU_A + (3.0 * GELU_A * GELU_B) * sq)
        slope_ref[k] = slope.astype(LOW)
        total = total + dg(hid[k], wos[k][:D], 1, 0)
    xhat2, inv2 = normalize(total)
    out_ref[...] = (xhat2 * gain2 + bias2).astype(LOW)
    cot = cot_ref[...].astype(F32)
    pull = cot * gain2
    grad_sum = inv2 * (
        pull
        - jnp.mean(pull, axis=1, keepdims=True)
        - xhat2 * jnp.mean(pull * xhat2, axis=1, keepdims=True)
    )
    vec_ref[2:3] = jnp.sum(grad_sum, axis=0, keepdims=True)
    vec_ref[3:4] = jnp.sum(cot * xhat2, axis=0, keepdims=True)
    vec_ref[4:5] = jnp.sum(cot, axis=0, keepdims=True)
    gs_ref[...] = grad_sum
    grad_low = grad_sum.astype(LOW)
    gl_ref[...] = grad_low
    for k in (1, 3, 0, 2):
        give(send_ref if k % 2 else keep_ref, k // 2, dg(hid[k], grad_low, 0, 0), first)


def give(ref, k, rows, first):
    size = rows.shape[0] // 4
    for i in range(4):
        ref[k, first ^ i] = rows[i * size : (i + 1) * size].astype(LOW)


def inner_terms(k, wi_ref, wo_ref, slope_ref, normed_low, grad_low, ref, first):
    gi = slope_ref[k].astype(F32) * dg(grad_low, wo_ref[:D], 1, 1)
    gi_low = gi.astype(LOW)
    bias = jnp.sum(gi_low.astype(F32), axis=0, keepdims=True)
    bias = jnp.where(iota((PAD, D), 0) == 0, bias, 0.0)
    rows = jnp.concatenate([dg(normed_low, gi_low, 0, 0), bias], axis=0)
    give(ref, k // 2, rows, first)
    return dg(gi_low, wi_ref[...], 1, 1)


def send_kernel(at_ref, wi1, wi3, wo1, wo3, slope_ref, nl_ref, gl_ref, gs_ref, send_ref, back_ref):
    first = at_ref[5]
    back = gs_ref[...]
    for k, wi_ref, wo_ref in ((1, wi1, wo1), (3, wi3, wo3)):
        back = back + inner_terms(k, wi_ref, wo_ref, slope_ref, nl_ref[...], gl_ref[...], send_ref, first)
    back_ref[...] = back


def keep_kernel(
    at_ref, after_ref, small_ref, w_ref, wi0, wi2, wo0, wo2, slope_ref, nl_ref, gl_ref, back_ref, xhat_ref, inv_ref, mixed_ref,
    keep_ref, resid_ref, dwo_ref, gmix_ref, vec_ref,
):
    first = at_ref[5]
    back = back_ref[...]
    for k, wi_ref, wo_ref in ((0, wi0, wo0), (2, wi2, wo2)):
        back = back + inner_terms(k, wi_ref, wo_ref, slope_ref, nl_ref[...], gl_ref[...], keep_ref, first)
    xhat1 = xhat_ref[...]
    vec_ref[0:1] = jnp.sum(back * xhat1, axis=0, keepdims=True)
    vec_ref[1:2] = jnp.sum(back, axis=0, keepdims=True)
    pull = back * small_ref[MEM : MEM + 1]
    resid = inv_ref[...] * (
        pull
        - jnp.mean(pull, axis=1, keepdims=True)
        - xhat1 * jnp.mean(pull * xhat1, axis=1, keepdims=True)
    )
    resid_ref[...] = resid
    resid_low = resid.astype(LOW)
    dwo_ref[...] = dg(mixed_ref[...], resid_low, 1, 0).astype(LOW)
    gmix_ref[...] = dg(w_ref[:, 3 * D : 4 * D], resid_low, 1, 1).astype(LOW)


def heads_kernel(
    low_h, high_h, after_ref, qkv_ref, p_ref, pm_ref, mixed_ref, c_ref, cm_ref, gmix_ref, kv_ref, gp_ref, gm_ref,
    do_m, ds_m,
):
    heads = range(low_h, high_h)
    f0, f1 = low_h * HEAD, high_h * HEAD
    m0, m1 = low_h * PAD, high_h * PAD
    k_tall = block_diagonal(kv_ref[:, f0:f1].astype(F32))
    v_tall = block_diagonal(kv_ref[:, D + f0 : D + f1].astype(F32))
    deltas = []
    for i, h in enumerate(heads):
        at = h * HEAD
        do = gmix_ref[at : at + HEAD].astype(F32)
        deltas.append(
            jnp.sum(do * mixed_ref[at : at + HEAD].astype(F32), axis=0, keepdims=True)
        )
        do_m[i * HEAD : (i + 1) * HEAD] = (do * cm_ref[h : h + 1]).astype(LOW)
    da_m = dg(v_tall, do_m[...], 1, 0)
    for i, h in enumerate(heads):
        rows = slice(i * PAD, (i + 1) * PAD)
        p = pm_ref[h * PAD : (h + 1) * PAD].astype(F32)
        ds_m[rows] = (p * (da_m[rows] - deltas[i] * cm_ref[h : h + 1])).astype(LOW)
    gm_ref[0] = diagonal_sum(dg(ds_m[...], qkv_ref[f0:f1], 1, 1))
    gm_ref[1] = diagonal_sum(dg(pm_ref[m0:m1], do_m[...], 1, 1))
    dq_mem = dg(k_tall, ds_m[...], 0, 0)
    for i, h in enumerate(heads):
        at = h * HEAD
        rows = slice(i * HEAD, (i + 1) * HEAD)
        c = c_ref[h : h + 1]
        do = (gmix_ref[at : at + HEAD].astype(F32) * c).astype(LOW)
        p = p_ref[h]
        da = dg(qkv_ref[2 * D + at : 2 * D + at + HEAD], do, 0, 0)
        ds = (p.astype(F32) * (da - deltas[i] * c)).astype(LOW)
        gp_ref[2, rows] = dg(do, p, 1, 1).astype(LOW)
        gp_ref[1, rows] = dg(qkv_ref[at : at + HEAD], ds, 1, 1).astype(LOW)
        gp_ref[0, rows] = (
            SCALE * (dg(qkv_ref[D + at : D + at + HEAD], ds, 1, 0) + dq_mem[rows])
        ).astype(LOW)


def weights_kernel(
    bits, after_ref, at_ref, x_ref, w_ref, mem_ref, gp0_ref, gp1_ref, gm0_ref, gm1_ref, dwo_ref, vec_ref, vec1_ref, *rest
):
    g_refs, wext = rest[: len(bits)], rest[len(bits)]
    me = at_ref[0]
    mem_low = mem_ref[...].astype(LOW)
    x_t = x_ref[...].T
    width = gp0_ref.shape[1]
    for part, (gp_ref, gm_ref) in enumerate(((gp0_ref, gm0_ref), (gp1_ref, gm1_ref))):
        for i in range(3):
            grad = dg(x_t, gp_ref[i], 1, 1)
            if i > 0:
                grad = grad + dg(mem_low, gm_ref[i - 1].astype(LOW), 0, 0)
            at = i * D + part * width
            wext[:, at : at + width] = grad.astype(LOW)
    wext[:, 3 * D : 4 * D] = dwo_ref[...]
    gp_mem = jnp.concatenate([gm0_ref[0], gm1_ref[0], gm0_ref[1], gm1_ref[1]], axis=1).astype(LOW)
    g_mem = dg(gp_mem, w_ref[:, D : 3 * D], 1, 1)
    g_mem = jnp.where(at_ref[2] == 0, g_mem, 0.0)
    row = iota((EXTRA, D), 0)
    tall = jnp.concatenate([g_mem, jnp.zeros((EXTRA - PAD, D), F32)], axis=0)
    tall = jnp.where(row < MEM, tall, 0.0)
    for i in range(5):
        tall = jnp.where(row == MEM + i, (vec1_ref if i < 2 else vec_ref)[i : i + 1], tall)
    wext[:, 4 * D :] = tall.T.astype(LOW)
    for g_ref, offsets in zip(g_refs, bits, strict=True):
        if offsets is None:
            g_ref[...] = wext[...]
            continue
        size = g_ref.shape[0] // len(offsets)
        for j, offset in enumerate(offsets):
            start = pl.multiple_of((me ^ offset) * size, size)
            g_ref[j * size : (j + 1) * size] = wext[pl.ds(start, size), :]


def tokens_kernel(after_ref, w_ref, gp0_ref, gp1_ref, resid_ref, tok_ref):
    width = gp0_ref.shape[1]
    total = jnp.zeros((D, SPAN), F32)
    for part, gp_ref in enumerate((gp0_ref, gp1_ref)):
        for i in range(3):
            at = i * D + part * width
            total = total + dg(w_ref[:, at : at + width], gp_ref[i], 1, 0)
    tok_ref[...] = (total.T + resid_ref[...]).astype(LOW)


def place_kernel(at_ref, r0, r1, r2, r3, out_ref, sems):
    me = at_ref[3]
    copies = [pltpu.make_async_copy(ref, out_ref.at[me ^ k], sems.at[k]) for k, ref in enumerate((r0, r1, r2, r3))]
    for copy in copies:
        copy.start()
    for copy in copies:
        copy.wait()


def place(at, pieces):
    rows = call(
        place_kernel,
        sds((4,) + pieces[0].shape, pieces[0].dtype),
        [SMEM] + [VMEM] * 4,
        ANY,
        [pltpu.SemaphoreType.DMA((4,))],
        mib=8,
    )(at, *pieces)
    return rows.reshape(-1, D)


def finish_kernel(at_ref, own_ref, other_ref, out_ref, bias_ref, held):
    first = at_ref[5]
    size = own_ref.shape[1]
    for i, ref in enumerate((own_ref, other_ref)):
        for j in range(2):
            start = pl.multiple_of((first ^ (2 * i + j)) * size, size)
            held[pl.ds(start, size), :] = ref[j].astype(F32)
    out_ref[...] = held[:D]
    bias_ref[...] = held[held.shape[0] - PAD : held.shape[0] - PAD + 1]


def closing_kernel(at_ref, r0, r1, r2, r3, own_ref, other_ref, mine_ref, got_ref, rows_ref, out_ref, *rest):
    memory_ref, *square_refs, held, sems = rest
    squares, vectors = square_refs[:4], square_refs[4:]
    me, first = at_ref[3], at_ref[5]
    copies = [pltpu.make_async_copy(ref, rows_ref.at[me ^ k], sems.at[k]) for k, ref in enumerate((r0, r1, r2, r3))]
    for copy in copies:
        copy.start()
    size = own_ref.shape[1]
    for i, ref in enumerate((own_ref, other_ref)):
        for j in range(2):
            start = pl.multiple_of((first ^ (2 * i + j)) * size, size)
            out_ref[pl.ds(start, size), :] = ref[j].astype(F32)
    total = mine_ref[0].astype(F32) + got_ref[0].astype(F32)
    for i, ref in enumerate(squares):
        ref[...] = total[:, i * D : (i + 1) * D]
    memory_ref[...] = total[:, 4 * D : 4 * D + MEM]
    held[...] = jnp.zeros(held.shape, F32)
    held[: total.shape[0]] = total[:, 4 * D :]
    tall = held[...].T
    for i, ref in enumerate(vectors):
        ref[...] = tall[MEM + i : MEM + i + 1, : total.shape[0]]
    for copy in copies:
        copy.wait()


def closing(at, rows, pair, other, mine, got):
    n = mine.shape[1]
    shapes = [sds((4,) + rows[0].shape, LOW), sds((D, D), F32), sds((n, MEM), F32)]
    shapes += [sds((n, D), F32)] * 4 + [sds((1, n), F32)] * 5
    grad_tokens, grad_outer, grad_memory, *others = call(
        closing_kernel,
        shapes,
        [SMEM] + [VMEM] * 8,
        [ANY] + [VMEM] * (len(shapes) - 1),
        [pltpu.VMEM((EXTRA, EXTRA), F32), pltpu.SemaphoreType.DMA((4,))],
        mib=16,
    )(at, *rows, pair, other, mine, got)
    vectors = [v.reshape(-1) for v in others[4:]]
    return grad_tokens.reshape(-1, D), grad_outer, [grad_memory.T, *others[:4], *vectors]


def swap(value, axis, bit):
    n = lax.axis_size(axis)
    return lax.ppermute(value, axis, [(i, i ^ bit) for i in range(n)])


def tie(*values):
    return lax.optimization_barrier(values)


def add_low(*terms):
    return functools.reduce(jnp.add, [t.astype(F32) for t in terms]).astype(LOW)


def finish(at, pair, other):
    grad, bias = call(
        finish_kernel,
        [sds((D, D), F32), sds((1, D), F32)],
        [SMEM] + [VMEM] * 2,
        [VMEM] * 2,
        [pltpu.VMEM((4 * pair.shape[1], D), F32)],
        bytes_=2 * 2**20,
    )(at, pair, other)
    return grad, bias[0]


def split(reduced):
    reduced = reduced.reshape(-1, WIDE)
    squares = [reduced[:, i * D : (i + 1) * D] for i in range(4)]
    vectors = [reduced[:, 4 * D + MEM + i] for i in range(5)]
    return [reduced[:, 4 * D : 4 * D + MEM].T, *squares, *vectors]


def shards(
    tokens, cotangent, memory_init, query_weight, key_weight, value_weight, output_weight, first_gain,
    first_bias, inner_weight, inner_bias, outer_weight, outer_bias, second_gain, second_bias,
):
    n_dp, n_mp = lax.axis_size("dp"), lax.axis_size("mp")
    rows_each = query_weight.shape[0]
    by_bits = n_dp == 8 and n_mp == 4 and rows_each % 16 == 0
    me_mp, me_dp = lax.axis_index("mp"), lax.axis_index("dp")
    me = me_dp * n_mp + me_mp
    later = me_mp % SPANS
    x = (me_dp & 1) if by_bits else 0
    first = (x * 2 + ((me_dp >> 1) & 1)) if by_bits else 0
    at = jnp.stack([me, me_mp // SPANS, later, me_mp, me_dp, first, x]).astype(jnp.int32)

    pick = lambda v, i: lax.dynamic_index_in_dim(v, i, 0, keepdims=False)
    blocks = tokens.reshape(-1, SPAN, D)
    own = pick(blocks, me_mp)
    start = pick(blocks, me_mp - later)
    cot = pick(cotangent.reshape(-1, SPAN, D), me_mp)

    wi_halves = inner_weight.reshape(2, D // 2, D)
    z = ((me_dp >> 1) & 1) if by_bits else 0
    wi_near = swap(pick(wi_halves, z), "mp", 2)
    outer_rows = jnp.concatenate([outer_weight, inner_bias.reshape(1, -1), jnp.zeros((15, D), LOW)], axis=0)

    vectors = (first_gain, first_bias, outer_bias, second_gain, second_bias)
    local = call(
        pack_kernel,
        sds((rows_each, WIDE), LOW),
        [VMEM] * 10,
        VMEM,
        [pltpu.VMEM((EXTRA, EXTRA), F32)],
        mib=56,
    )(query_weight, key_weight, value_weight, output_weight, memory_init.T, *[v.reshape(1, -1) for v in vectors])
    z = ((me_dp >> 1) & 1) if by_bits else 0
    wo_halves = outer_weight.reshape(2, D // 2, D)
    wo_near = swap(jnp.concatenate([pick(wo_halves, z), outer_rows[D:]]), "mp", 2)
    if by_bits:
        line = [local] + [swap(local, ALL, 8 * j) for j in range(1, 4)]
        *line, wi_near = tie(*line, wi_near)
        wi_far = swap(wi_near, "dp", 2)
        line = jnp.concatenate(line, axis=0)
        plane = [line] + [swap(line, ALL, 2 * b) for b in range(1, 4)]
        wi2 = jnp.where(z == 0, jnp.concatenate([wi_near, wi_far]), jnp.concatenate([wi_far, wi_near]))
        wo_far = swap(wo_near, "dp", 2)
        top, bottom, biases = wo_near[: D // 2], wo_far[: D // 2], wo_near[D // 2 :]
        wo2 = jnp.where(z == 0, jnp.concatenate([top, bottom, biases]), jnp.concatenate([bottom, top, biases]))
        plane[1], own, start, cot = tie(plane[1], own, start, cot)
        *plane, wo2, wi2 = tie(*plane, wo2, wi2)
        pieces = plane + [swap(piece, ALL, 1) for piece in plane]
        bits = [[2 * b + c + 8 * j for j in range(4)] for c in range(2) for b in range(4)]
    else:
        pieces = [lax.all_gather(local, ALL, axis=0, tiled=True)]
        bits = [None]
        wi2 = jnp.concatenate([wi_near, swap(wi_halves[1], "mp", 2)])
        wo2 = jnp.concatenate([wo_near[: D // 2], swap(wo_halves[1], "mp", 2), wo_near[D // 2 :]])
    wi1, wo1, wi3, wo3 = [swap(v, "mp", 1) for v in (inner_weight, outer_rows, wi2, wo2)]

    w, qkv = call(
        functools.partial(project_kernel, bits),
        [sds((D, WIDE), LOW), sds((3 * D, SPAN), LOW)],
        [SMEM] + [VMEM] * (len(pieces) + 1),
        [VMEM] * 2,
        flops=2 * 10**9,
        bytes_=5 * 2**20,
    )(at, *pieces, own)
    p, o, m, l = call(
        attend_kernel,
        [
            sds((HEADS, SPAN, SPAN), LOW),
            sds((D, SPAN), F32),
            sds((HEADS, SPAN), F32),
            sds((HEADS, SPAN), F32),
        ],
        [VMEM],
        [VMEM] * 4,
        flops=5 * 10**9,
        bytes_=7 * 2**20,
    )(qkv)

    nm, small = call(
        memory_kernel,
        [sds((PAD, D), F32), sds((PAD, D), F32)],
        [VMEM] * 2,
        [VMEM] * 2,
        flops=3 * 10**9,
        bytes_=4 * 2**20,
        mib=16,
    )(start, w)
    nm, m, wi1, wi3, wo1, wo3 = tie(nm, m, wi1, wi3, wo1, wo3)

    outer_shape = sds((2, 4, D // 4, D), LOW)
    inner_shape = sds((2, 4, (D + PAD) // 4, D), LOW)
    square, square_low = sds((SPAN, D), F32), sds((SPAN, D), LOW)
    (
        out, outer_keep, outer_send, slope, normed, grad_low, grad_sum, xhat, inv, mixed, mem, kv_mem, p_mem, c, c_mem, vecs,
    ) = call(
        forward_kernel,
        [
            square_low,
            outer_shape,
            outer_shape,
            sds((4, SPAN, D), LOW),
            square_low,
            square_low,
            square,
            square,
            sds((SPAN, 1), F32),
            sds((D, SPAN), LOW),
            sds((PAD, D), F32),
            sds((PAD, 2 * D), LOW),
            sds((HEADS * PAD, SPAN), LOW),
            sds((HEADS, SPAN), F32),
            sds((HEADS, SPAN), F32),
            sds((8, D), F32),
        ],
        [SMEM] + [VMEM] * 17,
        [VMEM] * 16,
        [pltpu.VMEM((4, SPAN, D), LOW)],
        flops=10 * 10**9,
        bytes_=14 * 2**20,
    )(
        at, nm, small, own, w, qkv, o, m, l, inner_weight, wi1, wi2, wi3, outer_rows, wo1, wo2, wo3, cot,
    )
    wis, wos = (inner_weight, wi1, wi2, wi3), (outer_rows, wo1, wo2, wo3)

    outer_got = swap(outer_send, "mp", 1)

    inner_send, back = call(
        send_kernel,
        [inner_shape, square],
        [SMEM] + [VMEM] * 8,
        [VMEM] * 2,
    )(at, wis[1], wis[3], wos[1], wos[3], slope, normed, grad_low, grad_sum)
    inner_got = swap(inner_send, "mp", 1)

    outer_mine, outer_give = add_low(outer_keep[0], outer_got[0]), add_low(outer_keep[1], outer_got[1])
    outer_y = swap(outer_give, "mp", 2)

    inner_keep, resid, d_mix, g_mixed, vecs1 = call(
        keep_kernel,
        [
            inner_shape,
            square,
            sds((D, D), LOW),
            sds((D, SPAN), LOW),
            sds((8, D), F32),
        ],
        [SMEM, ANY] + [VMEM] * 13,
        [VMEM] * 5,
    )(at, outer_give, small, w, wis[0], wis[2], wos[0], wos[2], slope, normed, grad_low, back, xhat, inv, mixed)

    half = HEADS // 2
    some = half * HEAD

    def heads_backward(low_h, gate):
        return call(
            functools.partial(heads_kernel, low_h, low_h + half),
            [sds((3, some, SPAN), LOW), sds((2, PAD, some), F32)],
            [ANY] + [VMEM] * 8,
            [VMEM] * 2,
            [
                pltpu.VMEM((some, SPAN), LOW),
                pltpu.VMEM((half * PAD, SPAN), LOW),
            ],
        )(gate, qkv, p, p_mem, mixed, c, c_mem, g_mixed, kv_mem)

    if by_bits:
        inner_give = add_low(inner_keep[:, 2:], inner_got[:, 2:])
        inner_mine = add_low(inner_keep[:, :2], inner_got[:, :2])
        inner_x = swap(inner_give, "dp", 1)
    else:
        inner_give = inner_got
    gp0, gm0 = heads_backward(0, inner_give)
    gp1, gm1 = heads_backward(half, inner_give)

    if by_bits:
        out_bits = [[[2 * b + c + 8 * j for j in (0, 2, 1, 3)] for b in range(4)] for c in range(2)]
        out_bits = [sum(out_bits[0], []), *out_bits[1]]
    else:
        out_bits = [None]

    def weights_backward(gate):
        return call(
            functools.partial(weights_kernel, out_bits),
            [sds((len(o) * rows_each if o else D, WIDE), LOW) for o in out_bits],
            [ANY, SMEM] + [VMEM] * 10,
            [VMEM] * len(out_bits),
            [pltpu.VMEM((D, WIDE), LOW)],
        )(gate, at, own, w, mem, gp0, gp1, gm0, gm1, d_mix, vecs, vecs1)

    def tokens_backward(gate):
        return call(tokens_kernel, sds((SPAN, D), LOW), [ANY] + [VMEM] * 4, VMEM)(gate, w, gp0, gp1, resid)

    if by_bits:
        halves_of = lambda v: (v[: v.shape[0] // 2], v[v.shape[0] // 2 :])
        both = lambda mine, got: [add_low(u, v) for u, v in zip(halves_of(mine), halves_of(got), strict=True)]

        a_mine, *a_give = [g.reshape(-1, rows_each, WIDE) for g in weights_backward(inner_give)]
        a_got = [swap(g, ALL, 1) for g in a_give]

        grad_rows = tokens_backward(inner_give)
        rows_got = swap(grad_rows, "mp", 1)

        outer_y, grad_rows, a_mine = tie(outer_y, grad_rows, a_mine)
        q_mine, q_give = both(outer_mine, outer_y)
        q_got = swap(q_give, "dp", 1)

        inner_x, q_mine = tie(inner_x, q_mine)
        p_mine, p_give = add_low(inner_mine[0], inner_x[0]), add_low(inner_mine[1], inner_x[1])
        p_got = swap(p_give, "mp", 2)

        *a_got, p_mine = tie(*a_got, p_mine)
        a_mine, a_give = both(a_mine, jnp.concatenate(a_got))
        a_got = swap(a_give, ALL, 4)

        q_got, a_mine = tie(q_got, a_mine)
        q_mine, q_give = [v[0] for v in both(q_mine, q_got)]
        q_got = swap(q_give, "dp", 2)

        grad_rows, q_mine = tie(grad_rows, q_mine)
        rows_across = swap(grad_rows, "mp", 2)

        p_got, grad_rows = tie(p_got, grad_rows)
        p_mine, p_give = [v[0] for v in both(p_mine, p_got)]
        p_got = swap(p_give, "dp", 2)

        q_got, p_mine = tie(q_got, p_mine)
        q_mine = add_low(q_mine, q_got)
        q_got = swap(q_mine, "dp", 4)

        out, q_mine = tie(out, q_mine)
        out_got, out_across = swap(out, "mp", 1), swap(out, "mp", 2)

        p_got, out = tie(p_got, out)
        p_mine = add_low(p_mine, p_got)
        p_got = swap(p_mine, "dp", 4)

        a_got, p_mine = tie(a_got, p_mine)
        a_mine, a_give = both(a_mine, a_got)
        a_got = swap(a_give, ALL, 2)

        q_got, a_mine = tie(q_got, a_mine)
        q_mine = add_low(q_mine, q_got)
        q_got = swap(q_mine, "dp", 2)

        rows_across, q_mine = tie(rows_across, q_mine)
        rows_last = swap(rows_across, "mp", 1)

        a_got, rows_across = tie(a_got, rows_across)
        a_mine, a_give = both(a_mine, a_got)
        a_got = swap(a_give, ALL, 8)

        p_got, a_mine = tie(p_got, a_mine)
        p_mine = add_low(p_mine, p_got)
        p_got = swap(p_mine, "dp", 2)

        q_got, p_mine = tie(q_got, p_mine)
        q_pair = jnp.stack([q_mine, q_got])
        q_got = swap(q_pair, "dp", 1)

        out_across, q_pair = tie(out_across, q_pair)
        out_last = swap(out_across, "mp", 1)

        p_got, out_across = tie(p_got, out_across)
        p_pair = jnp.stack([p_mine, p_got])
        p_got = swap(p_pair, "dp", 1)

        a_got, p_pair = tie(a_got, p_pair)
        a_mine, a_give = both(a_mine, a_got)
        a_got = swap(a_give, ALL, 16)

        out_last, a_mine = tie(out_last, a_mine)
        layer_out = place(at, [out, out_got, out_across, out_last])

        rows_last, q_got, a_got, layer_out = tie(rows_last, q_got, a_got, layer_out)
        rows = [grad_rows, rows_got, rows_across, rows_last]
        grad_tokens, grad_outer, outputs = closing(at, rows, q_pair, q_got, a_mine, a_got)

        p_got, grad_outer = tie(p_got, grad_outer)
        grad_inner, grad_inner_bias = finish(at, p_pair, p_got)
    else:
        grad_outer = lax.psum(outer_mine.astype(F32) + outer_y.astype(F32), "dp").reshape(-1, D)
        grad_rows = tokens_backward(inner_give)
        grads = weights_backward(inner_give)
        inner = add_low(inner_keep, inner_got)
        layer_out = lax.all_gather(out, "mp", axis=0, tiled=True)
        grad_tokens = lax.all_gather(grad_rows, "mp", axis=0, tiled=True)
        inner = lax.psum(inner[0].astype(F32) + swap(inner[1], "mp", 2).astype(F32), "dp").reshape(-1, D)
        grad_inner, grad_inner_bias = inner[:D], inner[D]
        outputs = split(lax.psum_scatter(grads[0], ALL, scatter_dimension=0, tiled=True).astype(F32))
    grad_memory, grad_query, grad_key, grad_value, grad_output, *grad_vectors = outputs
    return (
        layer_out,
        grad_tokens,
        grad_memory,
        grad_query,
        grad_key,
        grad_value,
        grad_output,
        grad_vectors[0],
        grad_vectors[1],
        grad_inner,
        grad_inner_bias,
        grad_outer,
        *grad_vectors[2:],
    )


def solution(mesh):
    both = ("dp", "mp")
    in_specs = (
        P("dp", None),
        P("dp", None),
        P(None, both),
        P(both, None),
        P(both, None),
        P(both, None),
        P(both, None),
        P(both),
        P(both),
        P(None, "mp"),
        P("mp"),
        P("mp", None),
        P(both),
        P(both),
        P(both),
    )
    out_specs = (
        P("dp", None),
        P("dp", None),
        P(None, both),
        P(both, None),
        P(both, None),
        P(both, None),
        P(both, None),
        P(both),
        P(both),
        P(None, "mp"),
        P("mp"),
        P("mp", None),
        P(both),
        P(both),
        P(both),
    )
    return jax.shard_map(shards, mesh=mesh, in_specs=in_specs, out_specs=out_specs, check_vma=False)
```

```python
import functools

import jax
import jax.numpy as jnp
from jax import lax
from jax.experimental import pallas as pl
from jax.experimental.pallas import tpu as pltpu
from jax.sharding import PartitionSpec as P

D = 512
HEADS = 8
HEAD = 64
MEM = 20
PAD = 32
SPAN = 512
SPANS = 2
EXTRA = 128
WIDE = 4 * D + EXTRA
EPS = 1e-05
GELU_A = 0.7978845608028654
GELU_B = 0.044715
LOW = jnp.bfloat16
F32 = jnp.float32
SCALE = HEAD ** (-0.5)
ALL = ("dp", "mp")

VMEM = pl.BlockSpec(memory_space=pltpu.VMEM)
SMEM = pl.BlockSpec(memory_space=pltpu.SMEM)
ANY = pl.BlockSpec(memory_space=pl.ANY)


def dg(a, b, ca, cb):
    return lax.dot_general(a, b, (((ca,), (cb,)), ((), ())), preferred_element_type=F32)


def iota(shape, dim):
    return lax.broadcasted_iota(jnp.int32, shape, dim)


def head_mask(heads):
    shape = (heads * PAD, heads * HEAD)
    return (iota(shape, 0) >> 5) == (iota(shape, 1) >> 6)


def block_diagonal(rows):
    heads = rows.shape[1] // HEAD
    tall = jnp.concatenate([rows] * heads, axis=0)
    return jnp.where(head_mask(heads), tall, 0.0).astype(LOW)


def diagonal_sum(tall):
    heads = tall.shape[1] // HEAD
    kept = jnp.where(head_mask(heads), tall, 0.0)
    total = kept[:PAD]
    for h in range(1, heads):
        total = total + kept[h * PAD : (h + 1) * PAD]
    return total


def normalize(values):
    mean = jnp.mean(values, axis=1, keepdims=True)
    center = values - mean
    spread = jnp.mean(center * center, axis=1, keepdims=True)
    inv = lax.rsqrt(spread + EPS)
    return center * inv, inv


def gelu_parts(a):
    sq = a * a
    t = jnp.tanh(a * (GELU_A + (GELU_A * GELU_B) * sq))
    half = 0.5 * (1.0 + t)
    return half, t, sq


def gelu(a):
    half, _, _ = gelu_parts(a)
    return a * half


def call(kernel, out_shape, in_specs, out_specs, scratch=(), flops=1, bytes_=1, mib=32):
    return pl.pallas_call(
        kernel,
        out_shape=out_shape,
        in_specs=in_specs,
        out_specs=out_specs,
        scratch_shapes=list(scratch),
        compiler_params=pltpu.CompilerParams(vmem_limit_bytes=mib * 2**20),
        cost_estimate=pl.CostEstimate(flops=flops, bytes_accessed=bytes_, transcendentals=0),
    )


def sds(shape, dtype):
    return jax.ShapeDtypeStruct(shape, dtype)


def pack_kernel(q_ref, k_ref, v_ref, o_ref, mem_ref, g1_ref, b1_ref, ob_ref, g2_ref, b2_ref, out_ref, tall):
    rows = q_ref.shape[0]
    for i, ref in enumerate((q_ref, k_ref, v_ref, o_ref)):
        out_ref[:, i * D : (i + 1) * D] = ref[...]
    tall[...] = jnp.zeros(tall.shape, F32)
    for i, ref in enumerate((g1_ref, b1_ref, ob_ref, g2_ref, b2_ref)):
        tall[MEM + i : MEM + i + 1, :rows] = ref[...].astype(F32)
    out_ref[:, 4 * D :] = tall[...].T[:rows].astype(LOW)
    out_ref[:, 4 * D : 4 * D + MEM] = mem_ref[...]


def assemble(me, pieces, bits, out_ref):
    for piece, offsets in zip(pieces, bits, strict=True):
        if offsets is None:
            out_ref[...] = piece[...]
            continue
        size = piece.shape[0] // len(offsets)
        for j, offset in enumerate(offsets):
            start = pl.multiple_of((me ^ offset) * size, size)
            out_ref[pl.ds(start, size), :] = piece[j * size : (j + 1) * size, :]


def project_kernel(bits, at_ref, *refs):
    n = len(bits)
    x_ref, w_ref, qkv_ref = refs[n:]
    assemble(at_ref[0], refs[:n], bits, w_ref)
    x_t = x_ref[...].T
    qkv_ref[:D] = (dg(w_ref[:, :D], x_t, 0, 0).astype(LOW).astype(F32) * SCALE).astype(LOW)
    qkv_ref[D : 3 * D] = dg(w_ref[:, D : 3 * D], x_t, 0, 0).astype(LOW)


def attend_kernel(qkv_ref, p_ref, o_ref, m_ref, l_ref):
    def scores(h):
        at = h * HEAD
        return dg(qkv_ref[D + at : D + at + HEAD], qkv_ref[at : at + HEAD], 0, 0)

    s_next = scores(0)
    for h in range(HEADS):
        s = s_next
        if h + 1 < HEADS:
            s_next = scores(h + 1)
        at = h * HEAD
        m = jnp.max(s, axis=0, keepdims=True)
        p = jnp.exp(s - m)
        m_ref[h : h + 1] = m
        l_ref[h : h + 1] = jnp.sum(p, axis=0, keepdims=True)
        p_ref[h] = p.astype(LOW)
        o_ref[at : at + HEAD] = dg(qkv_ref[2 * D + at : 2 * D + at + HEAD], p_ref[h], 1, 0)


def memory_kernel(x1_ref, w_ref, nm_ref, small_ref):
    small = w_ref[:, 4 * D :].T.astype(F32)[:PAD]
    small_ref[...] = small
    mem = jnp.where(iota((PAD, D), 0) < MEM, small, 0.0)
    packed = dg(mem.astype(LOW), w_ref[:, : 3 * D], 1, 0).astype(LOW)
    q_tall = block_diagonal(packed[:, :D].astype(F32) * SCALE)
    s_mem = dg(q_tall, packed[:, D : 2 * D], 1, 1)
    s_mem = jnp.where(iota(s_mem.shape, 1) < MEM, s_mem, -1e30)
    kv = dg(x1_ref[...], w_ref[:, D : 3 * D], 1, 0).astype(LOW)
    s = dg(q_tall, kv[:, :D], 1, 1)
    m = jnp.maximum(jnp.max(s, axis=1, keepdims=True), jnp.max(s_mem, axis=1, keepdims=True))
    p = jnp.exp(s - m)
    p_mem = jnp.exp(s_mem - m)
    total = jnp.sum(p, axis=1, keepdims=True) + jnp.sum(p_mem, axis=1, keepdims=True)
    o = dg(p.astype(LOW), kv[:, D:], 1, 0) + dg(p_mem.astype(LOW), packed[:, 2 * D :], 1, 0)
    mixed = diagonal_sum(o / total).astype(LOW)
    xhat, _ = normalize(mem + dg(mixed, w_ref[:, 3 * D : 4 * D], 1, 0))
    nm_ref[...] = xhat * small[MEM : MEM + 1] + small[MEM + 1 : MEM + 2]


def forward_kernel(
    at_ref, nm_ref, small_ref, x_ref, w_ref, qkv_ref, o_ref, m_ref, l_ref,
    wi0, wi1, wi2, wi3, wo0, wo1, wo2, wo3, cot_ref,
    out_ref, keep_ref, send_ref, slope_ref, nl_ref, gl_ref, gs_ref, xhat_ref, inv_ref,
    mixed_ref, mem_ref, kv_ref, pm_ref, c_ref, cm_ref, vec_ref, hid,
):
    wis, wos = (wi0, wi1, wi2, wi3), (wo0, wo1, wo2, wo3)
    shifts = [ref[D : D + 1].astype(F32) for ref in wos]
    small = small_ref[...]
    gain1, bias1, outer_b, gain2, bias2 = (small[MEM + i : MEM + i + 1] for i in range(5))
    later, first = at_ref[2], at_ref[5]
    nm = nm_ref[...]
    nm_low = nm.astype(LOW)
    value = nm + outer_b
    for k in range(4):
        inner = dg(nm_low, wis[k][...], 1, 0) + shifts[k]
        value = value + dg(gelu(inner).astype(LOW), wos[k][:D], 1, 0)
    carried, _ = normalize(value)
    carried = carried * gain2 + bias2
    mem = jnp.where(later == 1, carried, small)
    mem = jnp.where(iota((PAD, D), 0) < MEM, mem, 0.0)
    mem_ref[...] = mem
    kv_mem = dg(mem.astype(LOW), w_ref[:, D : 3 * D], 1, 0).astype(LOW)
    kv_ref[...] = kv_mem
    k_tall = block_diagonal(kv_mem[:, :D].astype(F32))
    v_tall = block_diagonal(kv_mem[:, D:].astype(F32))
    s_all = dg(k_tall, qkv_ref[:D], 1, 0)
    s_all = jnp.where((iota(s_all.shape, 0) & (PAD - 1)) < MEM, s_all, -1e30)
    alphas, invs = [], []
    for h in range(HEADS):
        s = s_all[h * PAD : (h + 1) * PAD]
        m_old = m_ref[h : h + 1]
        m = jnp.maximum(m_old, jnp.max(s, axis=0, keepdims=True))
        alpha = jnp.exp(m_old - m)
        p = jnp.exp(s - m)
        inv = 1.0 / (l_ref[h : h + 1] * alpha + jnp.sum(p, axis=0, keepdims=True))
        pm_ref[h * PAD : (h + 1) * PAD] = p.astype(LOW)
        c_ref[h : h + 1] = alpha * inv
        cm_ref[h : h + 1] = inv
        alphas.append(alpha * inv)
        invs.append(inv)
    o_mem = dg(v_tall, pm_ref[...], 0, 0)
    for h in range(HEADS):
        at = h * HEAD
        mixed_ref[at : at + HEAD] = (
            o_ref[at : at + HEAD] * alphas[h] + o_mem[at : at + HEAD] * invs[h]
        ).astype(LOW)
    xhat1, inv1 = normalize(
        x_ref[...].astype(F32) + dg(mixed_ref[...], w_ref[:, 3 * D : 4 * D], 0, 0)
    )
    xhat_ref[...] = xhat1
    inv_ref[...] = inv1
    normed = xhat1 * gain1 + bias1
    normed_low = normed.astype(LOW)
    nl_ref[...] = normed_low
    total = normed + outer_b
    for k in range(4):
        a = dg(normed_low, wis[k][...], 1, 0) + shifts[k]
        half, t, sq = gelu_parts(a)
        hid[k] = (a * half).astype(LOW)
        slope = half + (0.5 * a) * (1.0 - t * t) * (GELU_A + (3.0 * GELU_A * GELU_B) * sq)
        slope_ref[k] = slope.astype(LOW)
        total = total + dg(hid[k], wos[k][:D], 1, 0)
    xhat2, inv2 = normalize(total)
    out_ref[...] = (xhat2 * gain2 + bias2).astype(LOW)
    cot = cot_ref[...].astype(F32)
    pull = cot * gain2
    grad_sum = inv2 * (
        pull
        - jnp.mean(pull, axis=1, keepdims=True)
        - xhat2 * jnp.mean(pull * xhat2, axis=1, keepdims=True)
    )
    vec_ref[2:3] = jnp.sum(grad_sum, axis=0, keepdims=True)
    vec_ref[3:4] = jnp.sum(cot * xhat2, axis=0, keepdims=True)
    vec_ref[4:5] = jnp.sum(cot, axis=0, keepdims=True)
    gs_ref[...] = grad_sum
    grad_low = grad_sum.astype(LOW)
    gl_ref[...] = grad_low
    for k in (1, 3, 0, 2):
        give(send_ref if k % 2 else keep_ref, k // 2, dg(hid[k], grad_low, 0, 0), first)


def give(ref, k, rows, first):
    size = rows.shape[0] // 4
    for i in range(4):
        ref[k, first ^ i] = rows[i * size : (i + 1) * size].astype(LOW)


def inner_terms(k, wi_ref, wo_ref, slope_ref, normed_low, grad_low, ref, first):
    gi = slope_ref[k].astype(F32) * dg(grad_low, wo_ref[:D], 1, 1)
    gi_low = gi.astype(LOW)
    bias = jnp.sum(gi_low.astype(F32), axis=0, keepdims=True)
    bias = jnp.where(iota((PAD, D), 0) == 0, bias, 0.0)
    rows = jnp.concatenate([dg(normed_low, gi_low, 0, 0), bias], axis=0)
    give(ref, k // 2, rows, first)
    return dg(gi_low, wi_ref[...], 1, 1)


def send_kernel(at_ref, wi1, wi3, wo1, wo3, slope_ref, nl_ref, gl_ref, gs_ref, send_ref, back_ref):
    first = at_ref[5]
    back = gs_ref[...]
    for k, wi_ref, wo_ref in ((1, wi1, wo1), (3, wi3, wo3)):
        back = back + inner_terms(k, wi_ref, wo_ref, slope_ref, nl_ref[...], gl_ref[...], send_ref, first)
    back_ref[...] = back


def keep_kernel(at_ref, after_ref, wi0, wi2, wo0, wo2, slope_ref, nl_ref, gl_ref, back_ref, keep_ref, sum_ref):
    first = at_ref[5]
    back = back_ref[...]
    for k, wi_ref, wo_ref in ((0, wi0, wo0), (2, wi2, wo2)):
        back = back + inner_terms(k, wi_ref, wo_ref, slope_ref, nl_ref[...], gl_ref[...], keep_ref, first)
    sum_ref[...] = back


def resid_kernel(back_ref, small_ref, w_ref, xhat_ref, inv_ref, mixed_ref, resid_ref, dwo_ref, gmix_ref, vec_ref):
    back = back_ref[...]
    xhat1 = xhat_ref[...]
    vec_ref[0:1] = jnp.sum(back * xhat1, axis=0, keepdims=True)
    vec_ref[1:2] = jnp.sum(back, axis=0, keepdims=True)
    pull = back * small_ref[MEM : MEM + 1]
    resid = inv_ref[...] * (
        pull
        - jnp.mean(pull, axis=1, keepdims=True)
        - xhat1 * jnp.mean(pull * xhat1, axis=1, keepdims=True)
    )
    resid_ref[...] = resid
    resid_low = resid.astype(LOW)
    dwo_ref[...] = dg(mixed_ref[...], resid_low, 1, 0).astype(LOW)
    gmix_ref[...] = dg(w_ref[:, 3 * D : 4 * D], resid_low, 1, 1).astype(LOW)


def heads_kernel(
    low_h, high_h, after_ref, qkv_ref, p_ref, pm_ref, mixed_ref, c_ref, cm_ref, gmix_ref, kv_ref, gp_ref, gm_ref,
    do_m, ds_m,
):
    heads = range(low_h, high_h)
    f0, f1 = low_h * HEAD, high_h * HEAD
    m0, m1 = low_h * PAD, high_h * PAD
    k_tall = block_diagonal(kv_ref[:, f0:f1].astype(F32))
    v_tall = block_diagonal(kv_ref[:, D + f0 : D + f1].astype(F32))
    deltas = []
    for i, h in enumerate(heads):
        at = h * HEAD
        do = gmix_ref[at : at + HEAD].astype(F32)
        deltas.append(
            jnp.sum(do * mixed_ref[at : at + HEAD].astype(F32), axis=0, keepdims=True)
        )
        do_m[i * HEAD : (i + 1) * HEAD] = (do * cm_ref[h : h + 1]).astype(LOW)
    da_m = dg(v_tall, do_m[...], 1, 0)
    for i, h in enumerate(heads):
        rows = slice(i * PAD, (i + 1) * PAD)
        p = pm_ref[h * PAD : (h + 1) * PAD].astype(F32)
        ds_m[rows] = (p * (da_m[rows] - deltas[i] * cm_ref[h : h + 1])).astype(LOW)
    gm_ref[0] = diagonal_sum(dg(ds_m[...], qkv_ref[f0:f1], 1, 1))
    gm_ref[1] = diagonal_sum(dg(pm_ref[m0:m1], do_m[...], 1, 1))
    dq_mem = dg(k_tall, ds_m[...], 0, 0)
    for i, h in enumerate(heads):
        at = h * HEAD
        rows = slice(i * HEAD, (i + 1) * HEAD)
        c = c_ref[h : h + 1]
        do = (gmix_ref[at : at + HEAD].astype(F32) * c).astype(LOW)
        p = p_ref[h]
        da = dg(qkv_ref[2 * D + at : 2 * D + at + HEAD], do, 0, 0)
        ds = (p.astype(F32) * (da - deltas[i] * c)).astype(LOW)
        gp_ref[2, rows] = dg(do, p, 1, 1).astype(LOW)
        gp_ref[1, rows] = dg(qkv_ref[at : at + HEAD], ds, 1, 1).astype(LOW)
        gp_ref[0, rows] = (
            SCALE * (dg(qkv_ref[D + at : D + at + HEAD], ds, 1, 0) + dq_mem[rows])
        ).astype(LOW)


def weights_kernel(
    bits, after_ref, at_ref, x_ref, w_ref, mem_ref, gp0_ref, gp1_ref, gm0_ref, gm1_ref, dwo_ref, vec_ref, vec1_ref, *rest
):
    g_refs, wext = rest[: len(bits)], rest[len(bits)]
    me = at_ref[0]
    mem_low = mem_ref[...].astype(LOW)
    x_t = x_ref[...].T
    width = gp0_ref.shape[1]
    for part, (gp_ref, gm_ref) in enumerate(((gp0_ref, gm0_ref), (gp1_ref, gm1_ref))):
        for i in range(3):
            grad = dg(x_t, gp_ref[i], 1, 1)
            if i > 0:
                grad = grad + dg(mem_low, gm_ref[i - 1].astype(LOW), 0, 0)
            at = i * D + part * width
            wext[:, at : at + width] = grad.astype(LOW)
    wext[:, 3 * D : 4 * D] = dwo_ref[...]
    gp_mem = jnp.concatenate([gm0_ref[0], gm1_ref[0], gm0_ref[1], gm1_ref[1]], axis=1).astype(LOW)
    g_mem = dg(gp_mem, w_ref[:, D : 3 * D], 1, 1)
    g_mem = jnp.where(at_ref[2] == 0, g_mem, 0.0)
    row = iota((EXTRA, D), 0)
    tall = jnp.concatenate([g_mem, jnp.zeros((EXTRA - PAD, D), F32)], axis=0)
    tall = jnp.where(row < MEM, tall, 0.0)
    for i in range(5):
        tall = jnp.where(row == MEM + i, (vec1_ref if i < 2 else vec_ref)[i : i + 1], tall)
    wext[:, 4 * D :] = tall.T.astype(LOW)
    for g_ref, offsets in zip(g_refs, bits, strict=True):
        if offsets is None:
            g_ref[...] = wext[...]
            continue
        size = g_ref.shape[0] // len(offsets)
        for j, offset in enumerate(offsets):
            start = pl.multiple_of((me ^ offset) * size, size)
            g_ref[j * size : (j + 1) * size] = wext[pl.ds(start, size), :]


def tokens_kernel(after_ref, w_ref, gp0_ref, gp1_ref, resid_ref, tok_ref):
    width = gp0_ref.shape[1]
    total = jnp.zeros((D, SPAN), F32)
    for part, gp_ref in enumerate((gp0_ref, gp1_ref)):
        for i in range(3):
            at = i * D + part * width
            total = total + dg(w_ref[:, at : at + width], gp_ref[i], 1, 0)
    tok_ref[...] = (total.T + resid_ref[...]).astype(LOW)


def place_kernel(at_ref, r0, r1, r2, r3, out_ref, sems):
    me = at_ref[3]
    copies = [pltpu.make_async_copy(ref, out_ref.at[me ^ k], sems.at[k]) for k, ref in enumerate((r0, r1, r2, r3))]
    for copy in copies:
        copy.start()
    for copy in copies:
        copy.wait()


def place(at, pieces):
    rows = call(
        place_kernel,
        sds((4,) + pieces[0].shape, pieces[0].dtype),
        [SMEM] + [VMEM] * 4,
        ANY,
        [pltpu.SemaphoreType.DMA((4,))],
        mib=8,
    )(at, *pieces)
    return rows.reshape(-1, D)


def finish_kernel(at_ref, own_ref, other_ref, out_ref, bias_ref, held):
    first = at_ref[5]
    size = own_ref.shape[1]
    for i, ref in enumerate((own_ref, other_ref)):
        for j in range(2):
            start = pl.multiple_of((first ^ (2 * i + j)) * size, size)
            held[pl.ds(start, size), :] = ref[j].astype(F32)
    out_ref[...] = held[:D]
    bias_ref[...] = held[held.shape[0] - PAD : held.shape[0] - PAD + 1]


def closing_kernel(at_ref, r0, r1, r2, r3, own_ref, other_ref, mine_ref, got_ref, rows_ref, out_ref, *rest):
    memory_ref, *square_refs, held, sems = rest
    squares, vectors = square_refs[:4], square_refs[4:]
    me, first = at_ref[3], at_ref[5]
    copies = [pltpu.make_async_copy(ref, rows_ref.at[me ^ k], sems.at[k]) for k, ref in enumerate((r0, r1, r2, r3))]
    for copy in copies:
        copy.start()
    size = own_ref.shape[1]
    for i, ref in enumerate((own_ref, other_ref)):
        for j in range(2):
            start = pl.multiple_of((first ^ (2 * i + j)) * size, size)
            out_ref[pl.ds(start, size), :] = ref[j].astype(F32)
    total = mine_ref[0].astype(F32) + got_ref[0].astype(F32)
    for i, ref in enumerate(squares):
        ref[...] = total[:, i * D : (i + 1) * D]
    memory_ref[...] = total[:, 4 * D : 4 * D + MEM]
    held[...] = jnp.zeros(held.shape, F32)
    held[: total.shape[0]] = total[:, 4 * D :]
    tall = held[...].T
    for i, ref in enumerate(vectors):
        ref[...] = tall[MEM + i : MEM + i + 1, : total.shape[0]]
    for copy in copies:
        copy.wait()


def closing(at, rows, pair, other, mine, got):
    n = mine.shape[1]
    shapes = [sds((4,) + rows[0].shape, LOW), sds((D, D), F32), sds((n, MEM), F32)]
    shapes += [sds((n, D), F32)] * 4 + [sds((1, n), F32)] * 5
    grad_tokens, grad_outer, grad_memory, *others = call(
        closing_kernel,
        shapes,
        [SMEM] + [VMEM] * 8,
        [ANY] + [VMEM] * (len(shapes) - 1),
        [pltpu.VMEM((EXTRA, EXTRA), F32), pltpu.SemaphoreType.DMA((4,))],
        mib=16,
    )(at, *rows, pair, other, mine, got)
    vectors = [v.reshape(-1) for v in others[4:]]
    return grad_tokens.reshape(-1, D), grad_outer, [grad_memory.T, *others[:4], *vectors]


def swap(value, axis, bit):
    n = lax.axis_size(axis)
    return lax.ppermute(value, axis, [(i, i ^ bit) for i in range(n)])


def tie(*values):
    return lax.optimization_barrier(values)


def add_low(*terms):
    return functools.reduce(jnp.add, [t.astype(F32) for t in terms]).astype(LOW)


def finish(at, pair, other):
    grad, bias = call(
        finish_kernel,
        [sds((D, D), F32), sds((1, D), F32)],
        [SMEM] + [VMEM] * 2,
        [VMEM] * 2,
        [pltpu.VMEM((4 * pair.shape[1], D), F32)],
        bytes_=2 * 2**20,
    )(at, pair, other)
    return grad, bias[0]


def split(reduced):
    reduced = reduced.reshape(-1, WIDE)
    squares = [reduced[:, i * D : (i + 1) * D] for i in range(4)]
    vectors = [reduced[:, 4 * D + MEM + i] for i in range(5)]
    return [reduced[:, 4 * D : 4 * D + MEM].T, *squares, *vectors]


def shards(
    tokens, cotangent, memory_init, query_weight, key_weight, value_weight, output_weight, first_gain,
    first_bias, inner_weight, inner_bias, outer_weight, outer_bias, second_gain, second_bias,
):
    n_dp, n_mp = lax.axis_size("dp"), lax.axis_size("mp")
    rows_each = query_weight.shape[0]
    by_bits = n_dp == 8 and n_mp == 4 and rows_each % 16 == 0
    me_mp, me_dp = lax.axis_index("mp"), lax.axis_index("dp")
    me = me_dp * n_mp + me_mp
    later = me_mp % SPANS
    x = (me_dp & 1) if by_bits else 0
    first = (x * 2 + ((me_dp >> 1) & 1)) if by_bits else 0
    at = jnp.stack([me, me_mp // SPANS, later, me_mp, me_dp, first, x]).astype(jnp.int32)

    pick = lambda v, i: lax.dynamic_index_in_dim(v, i, 0, keepdims=False)
    blocks = tokens.reshape(-1, SPAN, D)
    own = pick(blocks, me_mp)
    start = pick(blocks, me_mp - later)
    cot = pick(cotangent.reshape(-1, SPAN, D), me_mp)

    wi_halves = inner_weight.reshape(2, D // 2, D)
    z = ((me_dp >> 1) & 1) if by_bits else 0
    wi_near = swap(pick(wi_halves, z), "mp", 2)
    outer_rows = jnp.concatenate([outer_weight, inner_bias.reshape(1, -1), jnp.zeros((15, D), LOW)], axis=0)

    vectors = (first_gain, first_bias, outer_bias, second_gain, second_bias)
    local = call(
        pack_kernel,
        sds((rows_each, WIDE), LOW),
        [VMEM] * 10,
        VMEM,
        [pltpu.VMEM((EXTRA, EXTRA), F32)],
        mib=56,
    )(query_weight, key_weight, value_weight, output_weight, memory_init.T, *[v.reshape(1, -1) for v in vectors])
    z = ((me_dp >> 1) & 1) if by_bits else 0
    wo_halves = outer_weight.reshape(2, D // 2, D)
    wo_near = swap(jnp.concatenate([pick(wo_halves, z), outer_rows[D:]]), "mp", 2)
    if by_bits:
        line = [local] + [swap(local, ALL, 8 * j) for j in range(1, 4)]
        *line, wi_near = tie(*line, wi_near)
        wi_far = swap(wi_near, "dp", 2)
        line = jnp.concatenate(line, axis=0)
        plane = [line] + [swap(line, ALL, 2 * b) for b in range(1, 4)]
        wi2 = jnp.where(z == 0, jnp.concatenate([wi_near, wi_far]), jnp.concatenate([wi_far, wi_near]))
        wo_far = swap(wo_near, "dp", 2)
        top, bottom, biases = wo_near[: D // 2], wo_far[: D // 2], wo_near[D // 2 :]
        wo2 = jnp.where(z == 0, jnp.concatenate([top, bottom, biases]), jnp.concatenate([bottom, top, biases]))
        plane[2], own, start, cot = tie(plane[2], own, start, cot)
        *plane, wo2, wi2 = tie(*plane, wo2, wi2)
        pieces = plane + [swap(piece, ALL, 1) for piece in plane]
        bits = [[2 * b + c + 8 * j for j in range(4)] for c in range(2) for b in range(4)]
    else:
        pieces = [lax.all_gather(local, ALL, axis=0, tiled=True)]
        bits = [None]
        wi2 = jnp.concatenate([wi_near, swap(wi_halves[1], "mp", 2)])
        wo2 = jnp.concatenate([wo_near[: D // 2], swap(wo_halves[1], "mp", 2), wo_near[D // 2 :]])
    wi1, wo1, wi3, wo3 = [swap(v, "mp", 1) for v in (inner_weight, outer_rows, wi2, wo2)]

    w, qkv = call(
        functools.partial(project_kernel, bits),
        [sds((D, WIDE), LOW), sds((3 * D, SPAN), LOW)],
        [SMEM] + [VMEM] * (len(pieces) + 1),
        [VMEM] * 2,
        flops=2 * 10**9,
        bytes_=5 * 2**20,
    )(at, *pieces, own)
    p, o, m, l = call(
        attend_kernel,
        [
            sds((HEADS, SPAN, SPAN), LOW),
            sds((D, SPAN), F32),
            sds((HEADS, SPAN), F32),
            sds((HEADS, SPAN), F32),
        ],
        [VMEM],
        [VMEM] * 4,
        flops=5 * 10**9,
        bytes_=7 * 2**20,
    )(qkv)

    nm, small = call(
        memory_kernel,
        [sds((PAD, D), F32), sds((PAD, D), F32)],
        [VMEM] * 2,
        [VMEM] * 2,
        flops=3 * 10**9,
        bytes_=4 * 2**20,
        mib=16,
    )(start, w)
    nm, m, wi1, wi3, wo1, wo3 = tie(nm, m, wi1, wi3, wo1, wo3)

    outer_shape = sds((2, 4, D // 4, D), LOW)
    inner_shape = sds((2, 4, (D + PAD) // 4, D), LOW)
    square, square_low = sds((SPAN, D), F32), sds((SPAN, D), LOW)
    (
        out, outer_keep, outer_send, slope, normed, grad_low, grad_sum, xhat, inv, mixed, mem, kv_mem, p_mem, c, c_mem, vecs,
    ) = call(
        forward_kernel,
        [
            square_low,
            outer_shape,
            outer_shape,
            sds((4, SPAN, D), LOW),
            square_low,
            square_low,
            square,
            square,
            sds((SPAN, 1), F32),
            sds((D, SPAN), LOW),
            sds((PAD, D), F32),
            sds((PAD, 2 * D), LOW),
            sds((HEADS * PAD, SPAN), LOW),
            sds((HEADS, SPAN), F32),
            sds((HEADS, SPAN), F32),
            sds((8, D), F32),
        ],
        [SMEM] + [VMEM] * 17,
        [VMEM] * 16,
        [pltpu.VMEM((4, SPAN, D), LOW)],
        flops=10 * 10**9,
        bytes_=14 * 2**20,
    )(
        at, nm, small, own, w, qkv, o, m, l, inner_weight, wi1, wi2, wi3, outer_rows, wo1, wo2, wo3, cot,
    )
    wis, wos = (inner_weight, wi1, wi2, wi3), (outer_rows, wo1, wo2, wo3)

    outer_got = swap(outer_send, "mp", 1)

    inner_send, back = call(
        send_kernel,
        [inner_shape, square],
        [SMEM] + [VMEM] * 8,
        [VMEM] * 2,
    )(at, wis[1], wis[3], wos[1], wos[3], slope, normed, grad_low, grad_sum)
    inner_got = swap(inner_send, "mp", 1)

    outer_mine, outer_give = add_low(outer_keep[0], outer_got[0]), add_low(outer_keep[1], outer_got[1])
    outer_y = swap(outer_give, "mp", 2)

    inner_keep, back = call(
        keep_kernel,
        [inner_shape, square],
        [SMEM, ANY] + [VMEM] * 8,
        [VMEM] * 2,
    )(at, outer_give, wis[0], wis[2], wos[0], wos[2], slope, normed, grad_low, back)
    resid, d_mix, g_mixed, vecs1 = call(
        resid_kernel,
        [square, sds((D, D), LOW), sds((D, SPAN), LOW), sds((8, D), F32)],
        [VMEM] * 6,
        [VMEM] * 4,
    )(back, small, w, xhat, inv, mixed)

    half = HEADS // 2
    some = half * HEAD

    def heads_backward(low_h, gate):
        return call(
            functools.partial(heads_kernel, low_h, low_h + half),
            [sds((3, some, SPAN), LOW), sds((2, PAD, some), F32)],
            [ANY] + [VMEM] * 8,
            [VMEM] * 2,
            [
                pltpu.VMEM((some, SPAN), LOW),
                pltpu.VMEM((half * PAD, SPAN), LOW),
            ],
        )(gate, qkv, p, p_mem, mixed, c, c_mem, g_mixed, kv_mem)

    if by_bits:
        inner_give = add_low(inner_keep[:, 2:], inner_got[:, 2:])
        inner_mine = add_low(inner_keep[:, :2], inner_got[:, :2])
        inner_x = swap(inner_give, "dp", 1)
    else:
        inner_give = inner_got
    gp0, gm0 = heads_backward(0, inner_give)
    gp1, gm1 = heads_backward(half, inner_give)

    if by_bits:
        out_bits = [[[2 * b + c + 8 * j for j in (0, 2, 1, 3)] for b in range(4)] for c in range(2)]
        out_bits = [sum(out_bits[0], []), *out_bits[1]]
    else:
        out_bits = [None]

    def weights_backward(gate):
        return call(
            functools.partial(weights_kernel, out_bits),
            [sds((len(o) * rows_each if o else D, WIDE), LOW) for o in out_bits],
            [ANY, SMEM] + [VMEM] * 10,
            [VMEM] * len(out_bits),
            [pltpu.VMEM((D, WIDE), LOW)],
        )(gate, at, own, w, mem, gp0, gp1, gm0, gm1, d_mix, vecs, vecs1)

    def tokens_backward(gate):
        return call(tokens_kernel, sds((SPAN, D), LOW), [ANY] + [VMEM] * 4, VMEM)(gate, w, gp0, gp1, resid)

    if by_bits:
        halves_of = lambda v: (v[: v.shape[0] // 2], v[v.shape[0] // 2 :])
        both = lambda mine, got: [add_low(u, v) for u, v in zip(halves_of(mine), halves_of(got), strict=True)]

        grad_rows = tokens_backward(inner_give)
        rows_got = swap(grad_rows, "mp", 1)

        a_mine, *a_give = [g.reshape(-1, rows_each, WIDE) for g in weights_backward(inner_give)]
        a_got = [swap(g, ALL, 1) for g in a_give]

        outer_y, grad_rows, a_mine = tie(outer_y, grad_rows, a_mine)
        q_mine, q_give = both(outer_mine, outer_y)
        q_got = swap(q_give, "dp", 1)

        inner_x, q_mine = tie(inner_x, q_mine)
        p_mine, p_give = add_low(inner_mine[0], inner_x[0]), add_low(inner_mine[1], inner_x[1])
        p_got = swap(p_give, "mp", 2)

        *a_got, p_mine = tie(*a_got, p_mine)
        a_mine, a_give = both(a_mine, jnp.concatenate(a_got))
        a_got = swap(a_give, ALL, 4)

        q_got, a_mine = tie(q_got, a_mine)
        q_mine, q_give = [v[0] for v in both(q_mine, q_got)]
        q_got = swap(q_give, "dp", 2)

        grad_rows, q_mine = tie(grad_rows, q_mine)
        rows_across = swap(grad_rows, "mp", 2)

        p_got, grad_rows = tie(p_got, grad_rows)
        p_mine, p_give = [v[0] for v in both(p_mine, p_got)]
        p_got = swap(p_give, "dp", 2)

        q_got, p_mine = tie(q_got, p_mine)
        q_mine = add_low(q_mine, q_got)
        q_got = swap(q_mine, "dp", 4)

        out, q_mine = tie(out, q_mine)
        out_got, out_across = swap(out, "mp", 1), swap(out, "mp", 2)

        p_got, out = tie(p_got, out)
        p_mine = add_low(p_mine, p_got)
        p_got = swap(p_mine, "dp", 4)

        a_got, p_mine = tie(a_got, p_mine)
        a_mine, a_give = both(a_mine, a_got)
        a_got = swap(a_give, ALL, 2)

        q_got, a_mine = tie(q_got, a_mine)
        q_mine = add_low(q_mine, q_got)
        q_got = swap(q_mine, "dp", 2)

        rows_across, q_mine = tie(rows_across, q_mine)
        rows_last = swap(rows_across, "mp", 1)

        a_got, rows_across = tie(a_got, rows_across)
        a_mine, a_give = both(a_mine, a_got)
        a_got = swap(a_give, ALL, 8)

        p_got, a_mine = tie(p_got, a_mine)
        p_mine = add_low(p_mine, p_got)
        p_got = swap(p_mine, "dp", 2)

        q_got, p_mine = tie(q_got, p_mine)
        q_pair = jnp.stack([q_mine, q_got])
        q_got = swap(q_pair, "dp", 1)

        out_across, q_pair = tie(out_across, q_pair)
        out_last = swap(out_across, "mp", 1)

        p_got, out_across = tie(p_got, out_across)
        p_pair = jnp.stack([p_mine, p_got])
        p_got = swap(p_pair, "dp", 1)

        a_got, p_pair = tie(a_got, p_pair)
        a_mine, a_give = both(a_mine, a_got)
        a_got = swap(a_give, ALL, 16)

        out_last, a_mine = tie(out_last, a_mine)
        layer_out = place(at, [out, out_got, out_across, out_last])

        rows_last, q_got, a_got, layer_out = tie(rows_last, q_got, a_got, layer_out)
        rows = [grad_rows, rows_got, rows_across, rows_last]
        grad_tokens, grad_outer, outputs = closing(at, rows, q_pair, q_got, a_mine, a_got)

        p_got, grad_outer = tie(p_got, grad_outer)
        grad_inner, grad_inner_bias = finish(at, p_pair, p_got)
    else:
        grad_outer = lax.psum(outer_mine.astype(F32) + outer_y.astype(F32), "dp").reshape(-1, D)
        grad_rows = tokens_backward(inner_give)
        grads = weights_backward(inner_give)
        inner = add_low(inner_keep, inner_got)
        layer_out = lax.all_gather(out, "mp", axis=0, tiled=True)
        grad_tokens = lax.all_gather(grad_rows, "mp", axis=0, tiled=True)
        inner = lax.psum(inner[0].astype(F32) + swap(inner[1], "mp", 2).astype(F32), "dp").reshape(-1, D)
        grad_inner, grad_inner_bias = inner[:D], inner[D]
        outputs = split(lax.psum_scatter(grads[0], ALL, scatter_dimension=0, tiled=True).astype(F32))
    grad_memory, grad_query, grad_key, grad_value, grad_output, *grad_vectors = outputs
    return (
        layer_out,
        grad_tokens,
        grad_memory,
        grad_query,
        grad_key,
        grad_value,
        grad_output,
        grad_vectors[0],
        grad_vectors[1],
        grad_inner,
        grad_inner_bias,
        grad_outer,
        *grad_vectors[2:],
    )


def solution(mesh):
    both = ("dp", "mp")
    in_specs = (
        P("dp", None),
        P("dp", None),
        P(None, both),
        P(both, None),
        P(both, None),
        P(both, None),
        P(both, None),
        P(both),
        P(both),
        P(None, "mp"),
        P("mp"),
        P("mp", None),
        P(both),
        P(both),
        P(both),
    )
    out_specs = (
        P("dp", None),
        P("dp", None),
        P(None, both),
        P(both, None),
        P(both, None),
        P(both, None),
        P(both, None),
        P(both),
        P(both),
        P(None, "mp"),
        P("mp"),
        P("mp", None),
        P(both),
        P(both),
        P(both),
    )
    return jax.shard_map(shards, mesh=mesh, in_specs=in_specs, out_specs=out_specs, check_vma=False)
```

```python
import functools

import jax
import jax.numpy as jnp
from jax import lax
from jax.experimental import pallas as pl
from jax.experimental.pallas import tpu as pltpu
from jax.sharding import PartitionSpec as P

D = 512
HEADS = 8
HEAD = 64
MEM = 20
PAD = 32
SPAN = 512
SPANS = 2
EXTRA = 128
WIDE = 4 * D + EXTRA
EPS = 1e-05
GELU_A = 0.7978845608028654
GELU_B = 0.044715
LOW = jnp.bfloat16
F32 = jnp.float32
SCALE = HEAD ** (-0.5)
ALL = ("dp", "mp")

VMEM = pl.BlockSpec(memory_space=pltpu.VMEM)
SMEM = pl.BlockSpec(memory_space=pltpu.SMEM)
ANY = pl.BlockSpec(memory_space=pl.ANY)


def dg(a, b, ca, cb):
    return lax.dot_general(a, b, (((ca,), (cb,)), ((), ())), preferred_element_type=F32)


def iota(shape, dim):
    return lax.broadcasted_iota(jnp.int32, shape, dim)


def head_mask(heads):
    shape = (heads * PAD, heads * HEAD)
    return (iota(shape, 0) >> 5) == (iota(shape, 1) >> 6)


def block_diagonal(rows):
    heads = rows.shape[1] // HEAD
    tall = jnp.concatenate([rows] * heads, axis=0)
    return jnp.where(head_mask(heads), tall, 0.0).astype(LOW)


def diagonal_sum(tall):
    heads = tall.shape[1] // HEAD
    kept = jnp.where(head_mask(heads), tall, 0.0)
    total = kept[:PAD]
    for h in range(1, heads):
        total = total + kept[h * PAD : (h + 1) * PAD]
    return total


def normalize(values):
    mean = jnp.mean(values, axis=1, keepdims=True)
    center = values - mean
    spread = jnp.mean(center * center, axis=1, keepdims=True)
    inv = lax.rsqrt(spread + EPS)
    return center * inv, inv


def gelu_parts(a):
    sq = a * a
    t = jnp.tanh(a * (GELU_A + (GELU_A * GELU_B) * sq))
    half = 0.5 * (1.0 + t)
    return half, t, sq


def gelu(a):
    half, _, _ = gelu_parts(a)
    return a * half


def call(kernel, out_shape, in_specs, out_specs, scratch=(), flops=1, bytes_=1, mib=32):
    return pl.pallas_call(
        kernel,
        out_shape=out_shape,
        in_specs=in_specs,
        out_specs=out_specs,
        scratch_shapes=list(scratch),
        compiler_params=pltpu.CompilerParams(vmem_limit_bytes=mib * 2**20),
        cost_estimate=pl.CostEstimate(flops=flops, bytes_accessed=bytes_, transcendentals=0),
    )


def sds(shape, dtype):
    return jax.ShapeDtypeStruct(shape, dtype)


def pack_kernel(q_ref, k_ref, v_ref, o_ref, mem_ref, g1_ref, b1_ref, ob_ref, g2_ref, b2_ref, out_ref, tall):
    rows = q_ref.shape[0]
    for i, ref in enumerate((q_ref, k_ref, v_ref, o_ref)):
        out_ref[:, i * D : (i + 1) * D] = ref[...]
    tall[...] = jnp.zeros(tall.shape, F32)
    for i, ref in enumerate((g1_ref, b1_ref, ob_ref, g2_ref, b2_ref)):
        tall[MEM + i : MEM + i + 1, :rows] = ref[...].astype(F32)
    out_ref[:, 4 * D :] = tall[...].T[:rows].astype(LOW)
    out_ref[:, 4 * D : 4 * D + MEM] = mem_ref[...]


def assemble(me, pieces, bits, out_ref):
    for piece, offsets in zip(pieces, bits, strict=True):
        if offsets is None:
            out_ref[...] = piece[...]
            continue
        size = piece.shape[0] // len(offsets)
        for j, offset in enumerate(offsets):
            start = pl.multiple_of((me ^ offset) * size, size)
            out_ref[pl.ds(start, size), :] = piece[j * size : (j + 1) * size, :]


def project_kernel(bits, at_ref, *refs):
    n = len(bits)
    x_ref, w_ref, qkv_ref = refs[n:]
    assemble(at_ref[0], refs[:n], bits, w_ref)
    x_t = x_ref[...].T
    qkv_ref[:D] = (dg(w_ref[:, :D], x_t, 0, 0).astype(LOW).astype(F32) * SCALE).astype(LOW)
    qkv_ref[D : 3 * D] = dg(w_ref[:, D : 3 * D], x_t, 0, 0).astype(LOW)


def attend_kernel(qkv_ref, p_ref, o_ref, m_ref, l_ref):
    def scores(h):
        at = h * HEAD
        return dg(qkv_ref[D + at : D + at + HEAD], qkv_ref[at : at + HEAD], 0, 0)

    s_next = scores(0)
    for h in range(HEADS):
        s = s_next
        if h + 1 < HEADS:
            s_next = scores(h + 1)
        at = h * HEAD
        m = jnp.max(s, axis=0, keepdims=True)
        p = jnp.exp(s - m)
        m_ref[h : h + 1] = m
        l_ref[h : h + 1] = jnp.sum(p, axis=0, keepdims=True)
        p_ref[h] = p.astype(LOW)
        o_ref[at : at + HEAD] = dg(qkv_ref[2 * D + at : 2 * D + at + HEAD], p_ref[h], 1, 0)


def memory_kernel(x1_ref, w_ref, nm_ref, small_ref):
    small = w_ref[:, 4 * D :].T.astype(F32)[:PAD]
    small_ref[...] = small
    mem = jnp.where(iota((PAD, D), 0) < MEM, small, 0.0)
    packed = dg(mem.astype(LOW), w_ref[:, : 3 * D], 1, 0).astype(LOW)
    q_tall = block_diagonal(packed[:, :D].astype(F32) * SCALE)
    s_mem = dg(q_tall, packed[:, D : 2 * D], 1, 1)
    s_mem = jnp.where(iota(s_mem.shape, 1) < MEM, s_mem, -1e30)
    kv = dg(x1_ref[...], w_ref[:, D : 3 * D], 1, 0).astype(LOW)
    s = dg(q_tall, kv[:, :D], 1, 1)
    m = jnp.maximum(jnp.max(s, axis=1, keepdims=True), jnp.max(s_mem, axis=1, keepdims=True))
    p = jnp.exp(s - m)
    p_mem = jnp.exp(s_mem - m)
    total = jnp.sum(p, axis=1, keepdims=True) + jnp.sum(p_mem, axis=1, keepdims=True)
    o = dg(p.astype(LOW), kv[:, D:], 1, 0) + dg(p_mem.astype(LOW), packed[:, 2 * D :], 1, 0)
    mixed = diagonal_sum(o / total).astype(LOW)
    xhat, _ = normalize(mem + dg(mixed, w_ref[:, 3 * D : 4 * D], 1, 0))
    nm_ref[...] = xhat * small[MEM : MEM + 1] + small[MEM + 1 : MEM + 2]


def forward_kernel(
    at_ref, nm_ref, small_ref, x_ref, w_ref, qkv_ref, o_ref, m_ref, l_ref,
    wi0, wi1, wi2, wi3, wo0, wo1, wo2, wo3, cot_ref,
    out_ref, keep_ref, send_ref, slope_ref, nl_ref, gl_ref, gs_ref, xhat_ref, inv_ref,
    mixed_ref, mem_ref, kv_ref, pm_ref, c_ref, cm_ref, vec_ref, hid,
):
    wis, wos = (wi0, wi1, wi2, wi3), (wo0, wo1, wo2, wo3)
    shifts = [ref[D : D + 1].astype(F32) for ref in wos]
    small = small_ref[...]
    gain1, bias1, outer_b, gain2, bias2 = (small[MEM + i : MEM + i + 1] for i in range(5))
    later, first = at_ref[2], at_ref[5]
    nm = nm_ref[...]
    nm_low = nm.astype(LOW)
    value = nm + outer_b
    for k in range(4):
        inner = dg(nm_low, wis[k][...], 1, 0) + shifts[k]
        value = value + dg(gelu(inner).astype(LOW), wos[k][:D], 1, 0)
    carried, _ = normalize(value)
    carried = carried * gain2 + bias2
    mem = jnp.where(later == 1, carried, small)
    mem = jnp.where(iota((PAD, D), 0) < MEM, mem, 0.0)
    mem_ref[...] = mem
    kv_mem = dg(mem.astype(LOW), w_ref[:, D : 3 * D], 1, 0).astype(LOW)
    kv_ref[...] = kv_mem
    k_tall = block_diagonal(kv_mem[:, :D].astype(F32))
    v_tall = block_diagonal(kv_mem[:, D:].astype(F32))
    s_all = dg(k_tall, qkv_ref[:D], 1, 0)
    s_all = jnp.where((iota(s_all.shape, 0) & (PAD - 1)) < MEM, s_all, -1e30)
    alphas, invs = [], []
    for h in range(HEADS):
        s = s_all[h * PAD : (h + 1) * PAD]
        m_old = m_ref[h : h + 1]
        m = jnp.maximum(m_old, jnp.max(s, axis=0, keepdims=True))
        alpha = jnp.exp(m_old - m)
        p = jnp.exp(s - m)
        inv = 1.0 / (l_ref[h : h + 1] * alpha + jnp.sum(p, axis=0, keepdims=True))
        pm_ref[h * PAD : (h + 1) * PAD] = p.astype(LOW)
        c_ref[h : h + 1] = alpha * inv
        cm_ref[h : h + 1] = inv
        alphas.append(alpha * inv)
        invs.append(inv)
    o_mem = dg(v_tall, pm_ref[...], 0, 0)
    for h in range(HEADS):
        at = h * HEAD
        mixed_ref[at : at + HEAD] = (
            o_ref[at : at + HEAD] * alphas[h] + o_mem[at : at + HEAD] * invs[h]
        ).astype(LOW)
    xhat1, inv1 = normalize(
        x_ref[...].astype(F32) + dg(mixed_ref[...], w_ref[:, 3 * D : 4 * D], 0, 0)
    )
    xhat_ref[...] = xhat1
    inv_ref[...] = inv1
    normed = xhat1 * gain1 + bias1
    normed_low = normed.astype(LOW)
    nl_ref[...] = normed_low
    total = normed + outer_b
    for k in range(4):
        a = dg(normed_low, wis[k][...], 1, 0) + shifts[k]
        half, t, sq = gelu_parts(a)
        hid[k] = (a * half).astype(LOW)
        slope = half + (0.5 * a) * (1.0 - t * t) * (GELU_A + (3.0 * GELU_A * GELU_B) * sq)
        slope_ref[k] = slope.astype(LOW)
        total = total + dg(hid[k], wos[k][:D], 1, 0)
    xhat2, inv2 = normalize(total)
    out_ref[...] = (xhat2 * gain2 + bias2).astype(LOW)
    cot = cot_ref[...].astype(F32)
    pull = cot * gain2
    grad_sum = inv2 * (
        pull
        - jnp.mean(pull, axis=1, keepdims=True)
        - xhat2 * jnp.mean(pull * xhat2, axis=1, keepdims=True)
    )
    vec_ref[2:3] = jnp.sum(grad_sum, axis=0, keepdims=True)
    vec_ref[3:4] = jnp.sum(cot * xhat2, axis=0, keepdims=True)
    vec_ref[4:5] = jnp.sum(cot, axis=0, keepdims=True)
    gs_ref[...] = grad_sum
    grad_low = grad_sum.astype(LOW)
    gl_ref[...] = grad_low
    for k in (1, 3, 0, 2):
        give(send_ref if k % 2 else keep_ref, k // 2, dg(hid[k], grad_low, 0, 0), first)


def give(ref, k, rows, first):
    size = rows.shape[0] // 4
    for i in range(4):
        ref[k, first ^ i] = rows[i * size : (i + 1) * size].astype(LOW)


def inner_terms(k, wi_ref, wo_ref, slope_ref, normed_low, grad_low, ref, first):
    gi = slope_ref[k].astype(F32) * dg(grad_low, wo_ref[:D], 1, 1)
    gi_low = gi.astype(LOW)
    bias = jnp.sum(gi_low.astype(F32), axis=0, keepdims=True)
    bias = jnp.where(iota((PAD, D), 0) == 0, bias, 0.0)
    rows = jnp.concatenate([dg(normed_low, gi_low, 0, 0), bias], axis=0)
    give(ref, k // 2, rows, first)
    return dg(gi_low, wi_ref[...], 1, 1)


def send_kernel(at_ref, wi1, wi3, wo1, wo3, slope_ref, nl_ref, gl_ref, gs_ref, send_ref, back_ref):
    first = at_ref[5]
    back = gs_ref[...]
    for k, wi_ref, wo_ref in ((1, wi1, wo1), (3, wi3, wo3)):
        back = back + inner_terms(k, wi_ref, wo_ref, slope_ref, nl_ref[...], gl_ref[...], send_ref, first)
    back_ref[...] = back


def keep_kernel(at_ref, after_ref, wi0, wi2, wo0, wo2, slope_ref, nl_ref, gl_ref, back_ref, keep_ref, sum_ref):
    first = at_ref[5]
    back = back_ref[...]
    for k, wi_ref, wo_ref in ((0, wi0, wo0), (2, wi2, wo2)):
        back = back + inner_terms(k, wi_ref, wo_ref, slope_ref, nl_ref[...], gl_ref[...], keep_ref, first)
    sum_ref[...] = back


def resid_kernel(back_ref, small_ref, w_ref, xhat_ref, inv_ref, mixed_ref, resid_ref, dwo_ref, gmix_ref, vec_ref):
    back = back_ref[...]
    xhat1 = xhat_ref[...]
    vec_ref[0:1] = jnp.sum(back * xhat1, axis=0, keepdims=True)
    vec_ref[1:2] = jnp.sum(back, axis=0, keepdims=True)
    pull = back * small_ref[MEM : MEM + 1]
    resid = inv_ref[...] * (
        pull
        - jnp.mean(pull, axis=1, keepdims=True)
        - xhat1 * jnp.mean(pull * xhat1, axis=1, keepdims=True)
    )
    resid_ref[...] = resid
    resid_low = resid.astype(LOW)
    dwo_ref[...] = dg(mixed_ref[...], resid_low, 1, 0).astype(LOW)
    gmix_ref[...] = dg(w_ref[:, 3 * D : 4 * D], resid_low, 1, 1).astype(LOW)


def heads_kernel(
    low_h, high_h, after_ref, qkv_ref, p_ref, pm_ref, mixed_ref, c_ref, cm_ref, gmix_ref, kv_ref, gp_ref, gm_ref,
    do_m, ds_m,
):
    heads = range(low_h, high_h)
    f0, f1 = low_h * HEAD, high_h * HEAD
    m0, m1 = low_h * PAD, high_h * PAD
    k_tall = block_diagonal(kv_ref[:, f0:f1].astype(F32))
    v_tall = block_diagonal(kv_ref[:, D + f0 : D + f1].astype(F32))
    deltas = []
    for i, h in enumerate(heads):
        at = h * HEAD
        do = gmix_ref[at : at + HEAD].astype(F32)
        deltas.append(
            jnp.sum(do * mixed_ref[at : at + HEAD].astype(F32), axis=0, keepdims=True)
        )
        do_m[i * HEAD : (i + 1) * HEAD] = (do * cm_ref[h : h + 1]).astype(LOW)
    da_m = dg(v_tall, do_m[...], 1, 0)
    for i, h in enumerate(heads):
        rows = slice(i * PAD, (i + 1) * PAD)
        p = pm_ref[h * PAD : (h + 1) * PAD].astype(F32)
        ds_m[rows] = (p * (da_m[rows] - deltas[i] * cm_ref[h : h + 1])).astype(LOW)
    gm_ref[0] = diagonal_sum(dg(ds_m[...], qkv_ref[f0:f1], 1, 1))
    gm_ref[1] = diagonal_sum(dg(pm_ref[m0:m1], do_m[...], 1, 1))
    dq_mem = dg(k_tall, ds_m[...], 0, 0)
    for i, h in enumerate(heads):
        at = h * HEAD
        rows = slice(i * HEAD, (i + 1) * HEAD)
        c = c_ref[h : h + 1]
        do = (gmix_ref[at : at + HEAD].astype(F32) * c).astype(LOW)
        p = p_ref[h]
        da = dg(qkv_ref[2 * D + at : 2 * D + at + HEAD], do, 0, 0)
        ds = (p.astype(F32) * (da - deltas[i] * c)).astype(LOW)
        gp_ref[2, rows] = dg(do, p, 1, 1).astype(LOW)
        gp_ref[1, rows] = dg(qkv_ref[at : at + HEAD], ds, 1, 1).astype(LOW)
        gp_ref[0, rows] = (
            SCALE * (dg(qkv_ref[D + at : D + at + HEAD], ds, 1, 0) + dq_mem[rows])
        ).astype(LOW)


def weights_kernel(
    bits, after_ref, at_ref, x_ref, w_ref, mem_ref, gp0_ref, gp1_ref, gm0_ref, gm1_ref, dwo_ref, vec_ref, vec1_ref, *rest
):
    g_refs, wext = rest[: len(bits)], rest[len(bits)]
    me = at_ref[0]
    mem_low = mem_ref[...].astype(LOW)
    x_t = x_ref[...].T
    width = gp0_ref.shape[1]
    for part, (gp_ref, gm_ref) in enumerate(((gp0_ref, gm0_ref), (gp1_ref, gm1_ref))):
        for i in range(3):
            grad = dg(x_t, gp_ref[i], 1, 1)
            if i > 0:
                grad = grad + dg(mem_low, gm_ref[i - 1].astype(LOW), 0, 0)
            at = i * D + part * width
            wext[:, at : at + width] = grad.astype(LOW)
    wext[:, 3 * D : 4 * D] = dwo_ref[...]
    gp_mem = jnp.concatenate([gm0_ref[0], gm1_ref[0], gm0_ref[1], gm1_ref[1]], axis=1).astype(LOW)
    g_mem = dg(gp_mem, w_ref[:, D : 3 * D], 1, 1)
    g_mem = jnp.where(at_ref[2] == 0, g_mem, 0.0)
    row = iota((EXTRA, D), 0)
    tall = jnp.concatenate([g_mem, jnp.zeros((EXTRA - PAD, D), F32)], axis=0)
    tall = jnp.where(row < MEM, tall, 0.0)
    for i in range(5):
        tall = jnp.where(row == MEM + i, (vec1_ref if i < 2 else vec_ref)[i : i + 1], tall)
    wext[:, 4 * D :] = tall.T.astype(LOW)
    for g_ref, offsets in zip(g_refs, bits, strict=True):
        if offsets is None:
            g_ref[...] = wext[...]
            continue
        size = g_ref.shape[0] // len(offsets)
        for j, offset in enumerate(offsets):
            start = pl.multiple_of((me ^ offset) * size, size)
            g_ref[j * size : (j + 1) * size] = wext[pl.ds(start, size), :]


def tokens_kernel(after_ref, w_ref, gp0_ref, gp1_ref, resid_ref, tok_ref):
    width = gp0_ref.shape[1]
    total = jnp.zeros((D, SPAN), F32)
    for part, gp_ref in enumerate((gp0_ref, gp1_ref)):
        for i in range(3):
            at = i * D + part * width
            total = total + dg(w_ref[:, at : at + width], gp_ref[i], 1, 0)
    tok_ref[...] = (total.T + resid_ref[...]).astype(LOW)


def place_kernel(at_ref, r0, r1, r2, r3, out_ref, sems):
    me = at_ref[3]
    copies = [pltpu.make_async_copy(ref, out_ref.at[me ^ k], sems.at[k]) for k, ref in enumerate((r0, r1, r2, r3))]
    for copy in copies:
        copy.start()
    for copy in copies:
        copy.wait()


def place(at, pieces):
    rows = call(
        place_kernel,
        sds((4,) + pieces[0].shape, pieces[0].dtype),
        [SMEM] + [VMEM] * 4,
        ANY,
        [pltpu.SemaphoreType.DMA((4,))],
        mib=8,
    )(at, *pieces)
    return rows.reshape(-1, D)


def finish_kernel(at_ref, own_ref, other_ref, out_ref, bias_ref, held):
    first = at_ref[5]
    size = own_ref.shape[1]
    for i, ref in enumerate((own_ref, other_ref)):
        for j in range(2):
            start = pl.multiple_of((first ^ (2 * i + j)) * size, size)
            held[pl.ds(start, size), :] = ref[j].astype(F32)
    out_ref[...] = held[:D]
    bias_ref[...] = held[held.shape[0] - PAD : held.shape[0] - PAD + 1]


def closing_kernel(at_ref, r0, r1, r2, r3, own_ref, other_ref, mine_ref, got_ref, rows_ref, out_ref, *rest):
    memory_ref, *square_refs, held, sems = rest
    squares, vectors = square_refs[:4], square_refs[4:]
    me, first = at_ref[3], at_ref[5]
    copies = [pltpu.make_async_copy(ref, rows_ref.at[me ^ k], sems.at[k]) for k, ref in enumerate((r0, r1, r2, r3))]
    for copy in copies:
        copy.start()
    size = own_ref.shape[1]
    for i, ref in enumerate((own_ref, other_ref)):
        for j in range(2):
            start = pl.multiple_of((first ^ (2 * i + j)) * size, size)
            out_ref[pl.ds(start, size), :] = ref[j].astype(F32)
    total = mine_ref[0].astype(F32) + got_ref[0].astype(F32)
    for i, ref in enumerate(squares):
        ref[...] = total[:, i * D : (i + 1) * D]
    memory_ref[...] = total[:, 4 * D : 4 * D + MEM]
    held[...] = jnp.zeros(held.shape, F32)
    held[: total.shape[0]] = total[:, 4 * D :]
    tall = held[...].T
    for i, ref in enumerate(vectors):
        ref[...] = tall[MEM + i : MEM + i + 1, : total.shape[0]]
    for copy in copies:
        copy.wait()


def closing(at, rows, pair, other, mine, got):
    n = mine.shape[1]
    shapes = [sds((4,) + rows[0].shape, LOW), sds((D, D), F32), sds((n, MEM), F32)]
    shapes += [sds((n, D), F32)] * 4 + [sds((1, n), F32)] * 5
    grad_tokens, grad_outer, grad_memory, *others = call(
        closing_kernel,
        shapes,
        [SMEM] + [VMEM] * 8,
        [ANY] + [VMEM] * (len(shapes) - 1),
        [pltpu.VMEM((EXTRA, EXTRA), F32), pltpu.SemaphoreType.DMA((4,))],
        mib=16,
    )(at, *rows, pair, other, mine, got)
    vectors = [v.reshape(-1) for v in others[4:]]
    return grad_tokens.reshape(-1, D), grad_outer, [grad_memory.T, *others[:4], *vectors]


def swap(value, axis, bit):
    n = lax.axis_size(axis)
    return lax.ppermute(value, axis, [(i, i ^ bit) for i in range(n)])


def tie(*values):
    return lax.optimization_barrier(values)


def add_low(*terms):
    return functools.reduce(jnp.add, [t.astype(F32) for t in terms]).astype(LOW)


def finish(at, pair, other):
    grad, bias = call(
        finish_kernel,
        [sds((D, D), F32), sds((1, D), F32)],
        [SMEM] + [VMEM] * 2,
        [VMEM] * 2,
        [pltpu.VMEM((4 * pair.shape[1], D), F32)],
        bytes_=2 * 2**20,
    )(at, pair, other)
    return grad, bias[0]


def split(reduced):
    reduced = reduced.reshape(-1, WIDE)
    squares = [reduced[:, i * D : (i + 1) * D] for i in range(4)]
    vectors = [reduced[:, 4 * D + MEM + i] for i in range(5)]
    return [reduced[:, 4 * D : 4 * D + MEM].T, *squares, *vectors]


def shards(
    tokens, cotangent, memory_init, query_weight, key_weight, value_weight, output_weight, first_gain,
    first_bias, inner_weight, inner_bias, outer_weight, outer_bias, second_gain, second_bias,
):
    n_dp, n_mp = lax.axis_size("dp"), lax.axis_size("mp")
    rows_each = query_weight.shape[0]
    by_bits = n_dp == 8 and n_mp == 4 and rows_each % 16 == 0
    me_mp, me_dp = lax.axis_index("mp"), lax.axis_index("dp")
    me = me_dp * n_mp + me_mp
    later = me_mp % SPANS
    x = (me_dp & 1) if by_bits else 0
    first = (x * 2 + ((me_dp >> 1) & 1)) if by_bits else 0
    at = jnp.stack([me, me_mp // SPANS, later, me_mp, me_dp, first, x]).astype(jnp.int32)

    pick = lambda v, i: lax.dynamic_index_in_dim(v, i, 0, keepdims=False)
    blocks = tokens.reshape(-1, SPAN, D)
    own = pick(blocks, me_mp)
    start = pick(blocks, me_mp - later)
    cot = pick(cotangent.reshape(-1, SPAN, D), me_mp)

    wi_halves = inner_weight.reshape(2, D // 2, D)
    z = ((me_dp >> 1) & 1) if by_bits else 0
    wi_near = swap(pick(wi_halves, z), "mp", 2)
    outer_rows = jnp.concatenate([outer_weight, inner_bias.reshape(1, -1), jnp.zeros((15, D), LOW)], axis=0)

    vectors = (first_gain, first_bias, outer_bias, second_gain, second_bias)
    local = call(
        pack_kernel,
        sds((rows_each, WIDE), LOW),
        [VMEM] * 10,
        VMEM,
        [pltpu.VMEM((EXTRA, EXTRA), F32)],
        mib=56,
    )(query_weight, key_weight, value_weight, output_weight, memory_init.T, *[v.reshape(1, -1) for v in vectors])
    z = ((me_dp >> 1) & 1) if by_bits else 0
    wo_halves = outer_weight.reshape(2, D // 2, D)
    wo_near = swap(jnp.concatenate([pick(wo_halves, z), outer_rows[D:]]), "mp", 2)
    if by_bits:
        line = [local] + [swap(local, ALL, 8 * j) for j in (2, 1, 3)]
        *line, wi_near = tie(*line, wi_near)
        wi_far = swap(wi_near, "dp", 2)
        line = jnp.concatenate(line, axis=0)
        plane = [line] + [swap(line, ALL, 2 * b) for b in (1, 3, 2)]
        wi2 = jnp.where(z == 0, jnp.concatenate([wi_near, wi_far]), jnp.concatenate([wi_far, wi_near]))
        wo_far = swap(wo_near, "dp", 2)
        top, bottom, biases = wo_near[: D // 2], wo_far[: D // 2], wo_near[D // 2 :]
        wo2 = jnp.where(z == 0, jnp.concatenate([top, bottom, biases]), jnp.concatenate([bottom, top, biases]))
        plane[3], own, start, cot = tie(plane[3], own, start, cot)
        *plane, wo2, wi2 = tie(*plane, wo2, wi2)
        pieces = plane + [swap(piece, ALL, 1) for piece in plane]
        bits = [[2 * b + c + 8 * j for j in (0, 2, 1, 3)] for c in range(2) for b in (0, 1, 3, 2)]
    else:
        pieces = [lax.all_gather(local, ALL, axis=0, tiled=True)]
        bits = [None]
        wi2 = jnp.concatenate([wi_near, swap(wi_halves[1], "mp", 2)])
        wo2 = jnp.concatenate([wo_near[: D // 2], swap(wo_halves[1], "mp", 2), wo_near[D // 2 :]])
    wi1, wo1, wi3, wo3 = [swap(v, "mp", 1) for v in (inner_weight, outer_rows, wi2, wo2)]

    w, qkv = call(
        functools.partial(project_kernel, bits),
        [sds((D, WIDE), LOW), sds((3 * D, SPAN), LOW)],
        [SMEM] + [VMEM] * (len(pieces) + 1),
        [VMEM] * 2,
        flops=2 * 10**9,
        bytes_=5 * 2**20,
        mib=32,
    )(at, *pieces, own)
    p, o, m, l = call(
        attend_kernel,
        [
            sds((HEADS, SPAN, SPAN), LOW),
            sds((D, SPAN), F32),
            sds((HEADS, SPAN), F32),
            sds((HEADS, SPAN), F32),
        ],
        [VMEM],
        [VMEM] * 4,
        flops=9 * 10**9,
        bytes_=7 * 2**20,
    )(qkv)

    nm, small = call(
        memory_kernel,
        [sds((PAD, D), F32), sds((PAD, D), F32)],
        [VMEM] * 2,
        [VMEM] * 2,
        flops=1 * 10**9,
        bytes_=4 * 2**20,
        mib=16,
    )(start, w)
    nm, m, wi1, wi3, wo1, wo3 = tie(nm, m, wi1, wi3, wo1, wo3)

    outer_shape = sds((2, 4, D // 4, D), LOW)
    inner_shape = sds((2, 4, (D + PAD) // 4, D), LOW)
    square, square_low = sds((SPAN, D), F32), sds((SPAN, D), LOW)
    (
        out, outer_keep, outer_send, slope, normed, grad_low, grad_sum, xhat, inv, mixed, mem, kv_mem, p_mem, c, c_mem, vecs,
    ) = call(
        forward_kernel,
        [
            square_low,
            outer_shape,
            outer_shape,
            sds((4, SPAN, D), LOW),
            square_low,
            square_low,
            square,
            square,
            sds((SPAN, 1), F32),
            sds((D, SPAN), LOW),
            sds((PAD, D), F32),
            sds((PAD, 2 * D), LOW),
            sds((HEADS * PAD, SPAN), LOW),
            sds((HEADS, SPAN), F32),
            sds((HEADS, SPAN), F32),
            sds((8, D), F32),
        ],
        [SMEM] + [VMEM] * 17,
        [VMEM] * 16,
        [pltpu.VMEM((4, SPAN, D), LOW)],
        flops=5 * 10**9,
        mib=28,
        bytes_=14 * 2**20,
    )(
        at, nm, small, own, w, qkv, o, m, l, inner_weight, wi1, wi2, wi3, outer_rows, wo1, wo2, wo3, cot,
    )
    wis, wos = (inner_weight, wi1, wi2, wi3), (outer_rows, wo1, wo2, wo3)

    outer_got = swap(outer_send, "mp", 1)

    inner_send, back = call(
        send_kernel,
        [inner_shape, square],
        [SMEM] + [VMEM] * 8,
        [VMEM] * 2,
    )(at, wis[1], wis[3], wos[1], wos[3], slope, normed, grad_low, grad_sum)
    inner_got = swap(inner_send, "mp", 1)

    outer_mine, outer_give = add_low(outer_keep[0], outer_got[0]), add_low(outer_keep[1], outer_got[1])
    outer_y = swap(outer_give, "mp", 2)

    inner_keep, back = call(
        keep_kernel,
        [inner_shape, square],
        [SMEM, ANY] + [VMEM] * 8,
        [VMEM] * 2,
    )(at, outer_give, wis[0], wis[2], wos[0], wos[2], slope, normed, grad_low, back)
    resid, d_mix, g_mixed, vecs1 = call(
        resid_kernel,
        [square, sds((D, D), LOW), sds((D, SPAN), LOW), sds((8, D), F32)],
        [VMEM] * 6,
        [VMEM] * 4,
    )(back, small, w, xhat, inv, mixed)

    half = HEADS // 2
    some = half * HEAD

    def heads_backward(low_h, gate):
        return call(
            functools.partial(heads_kernel, low_h, low_h + half),
            [sds((3, some, SPAN), LOW), sds((2, PAD, some), F32)],
            [ANY] + [VMEM] * 8,
            [VMEM] * 2,
            [
                pltpu.VMEM((some, SPAN), LOW),
                pltpu.VMEM((half * PAD, SPAN), LOW),
            ],
        )(gate, qkv, p, p_mem, mixed, c, c_mem, g_mixed, kv_mem)

    if by_bits:
        inner_give = add_low(inner_keep[:, 2:], inner_got[:, 2:])
        inner_mine = add_low(inner_keep[:, :2], inner_got[:, :2])
        inner_x = swap(inner_give, "dp", 1)
    else:
        inner_give = inner_got
    gp0, gm0 = heads_backward(0, inner_give)
    gp1, gm1 = heads_backward(half, inner_give)

    if by_bits:
        out_bits = [[[2 * b + c + 8 * j for j in (0, 2, 1, 3)] for b in range(4)] for c in range(2)]
        out_bits = [sum(out_bits[0], []), *out_bits[1]]
    else:
        out_bits = [None]

    def weights_backward(gate):
        return call(
            functools.partial(weights_kernel, out_bits),
            [sds((len(o) * rows_each if o else D, WIDE), LOW) for o in out_bits],
            [ANY, SMEM] + [VMEM] * 10,
            [VMEM] * len(out_bits),
            [pltpu.VMEM((D, WIDE), LOW)],
        )(gate, at, own, w, mem, gp0, gp1, gm0, gm1, d_mix, vecs, vecs1)

    def tokens_backward(gate):
        return call(tokens_kernel, sds((SPAN, D), LOW), [ANY] + [VMEM] * 4, VMEM)(gate, w, gp0, gp1, resid)

    if by_bits:
        halves_of = lambda v: (v[: v.shape[0] // 2], v[v.shape[0] // 2 :])
        both = lambda mine, got: [add_low(u, v) for u, v in zip(halves_of(mine), halves_of(got), strict=True)]

        grad_rows = tokens_backward(inner_give)
        rows_got = swap(grad_rows, "mp", 1)

        a_mine, *a_give = [g.reshape(-1, rows_each, WIDE) for g in weights_backward(inner_give)]
        a_got = [swap(g, ALL, 1) for g in a_give]

        outer_y, grad_rows, a_mine = tie(outer_y, grad_rows, a_mine)
        q_mine, q_give = both(outer_mine, outer_y)
        q_got = swap(q_give, "dp", 1)

        inner_x, q_mine = tie(inner_x, q_mine)
        p_mine, p_give = add_low(inner_mine[0], inner_x[0]), add_low(inner_mine[1], inner_x[1])
        p_got = swap(p_give, "mp", 2)

        *a_got, p_mine = tie(*a_got, p_mine)
        a_mine, a_give = both(a_mine, jnp.concatenate(a_got))
        a_got = swap(a_give, ALL, 4)

        q_got, a_mine = tie(q_got, a_mine)
        q_mine, q_give = [v[0] for v in both(q_mine, q_got)]
        q_got = swap(q_give, "dp", 2)

        grad_rows, q_mine = tie(grad_rows, q_mine)
        rows_across = swap(grad_rows, "mp", 2)

        p_got, grad_rows = tie(p_got, grad_rows)
        p_mine, p_give = [v[0] for v in both(p_mine, p_got)]
        p_got = swap(p_give, "dp", 2)

        q_got, p_mine = tie(q_got, p_mine)
        q_mine = add_low(q_mine, q_got)
        q_got = swap(q_mine, "dp", 4)

        out, q_mine = tie(out, q_mine)
        out_got, out_across = swap(out, "mp", 1), swap(out, "mp", 2)

        p_got, out = tie(p_got, out)
        p_mine = add_low(p_mine, p_got)
        p_got = swap(p_mine, "dp", 4)

        a_got, p_mine = tie(a_got, p_mine)
        a_mine, a_give = both(a_mine, a_got)
        a_got = swap(a_give, ALL, 2)

        q_got, a_mine = tie(q_got, a_mine)
        q_mine = add_low(q_mine, q_got)
        q_got = swap(q_mine, "dp", 2)

        rows_across, q_mine = tie(rows_across, q_mine)
        rows_last = swap(rows_across, "mp", 1)

        a_got, rows_across = tie(a_got, rows_across)
        a_mine, a_give = both(a_mine, a_got)
        a_got = swap(a_give, ALL, 8)

        p_got, a_mine = tie(p_got, a_mine)
        p_mine = add_low(p_mine, p_got)
        p_got = swap(p_mine, "dp", 2)

        q_got, p_mine = tie(q_got, p_mine)
        q_pair = jnp.stack([q_mine, q_got])
        q_got = swap(q_pair, "dp", 1)

        out_across, q_pair = tie(out_across, q_pair)
        out_last = swap(out_across, "mp", 1)

        p_got, out_across = tie(p_got, out_across)
        p_pair = jnp.stack([p_mine, p_got])
        p_got = swap(p_pair, "dp", 1)

        a_got, p_pair = tie(a_got, p_pair)
        a_mine, a_give = both(a_mine, a_got)
        a_got = swap(a_give, ALL, 16)

        out_last, a_mine = tie(out_last, a_mine)
        layer_out = place(at, [out, out_got, out_across, out_last])

        rows_last, q_got, a_got, layer_out = tie(rows_last, q_got, a_got, layer_out)
        rows = [grad_rows, rows_got, rows_across, rows_last]
        grad_tokens, grad_outer, outputs = closing(at, rows, q_pair, q_got, a_mine, a_got)

        p_got, grad_outer = tie(p_got, grad_outer)
        grad_inner, grad_inner_bias = finish(at, p_pair, p_got)
    else:
        grad_outer = lax.psum(outer_mine.astype(F32) + outer_y.astype(F32), "dp").reshape(-1, D)
        grad_rows = tokens_backward(inner_give)
        grads = weights_backward(inner_give)
        inner = add_low(inner_keep, inner_got)
        layer_out = lax.all_gather(out, "mp", axis=0, tiled=True)
        grad_tokens = lax.all_gather(grad_rows, "mp", axis=0, tiled=True)
        inner = lax.psum(inner[0].astype(F32) + swap(inner[1], "mp", 2).astype(F32), "dp").reshape(-1, D)
        grad_inner, grad_inner_bias = inner[:D], inner[D]
        outputs = split(lax.psum_scatter(grads[0], ALL, scatter_dimension=0, tiled=True).astype(F32))
    grad_memory, grad_query, grad_key, grad_value, grad_output, *grad_vectors = outputs
    return (
        layer_out,
        grad_tokens,
        grad_memory,
        grad_query,
        grad_key,
        grad_value,
        grad_output,
        grad_vectors[0],
        grad_vectors[1],
        grad_inner,
        grad_inner_bias,
        grad_outer,
        *grad_vectors[2:],
    )


def solution(mesh):
    both = ("dp", "mp")
    in_specs = (
        P("dp", None),
        P("dp", None),
        P(None, both),
        P(both, None),
        P(both, None),
        P(both, None),
        P(both, None),
        P(both),
        P(both),
        P(None, "mp"),
        P("mp"),
        P("mp", None),
        P(both),
        P(both),
        P(both),
    )
    out_specs = (
        P("dp", None),
        P("dp", None),
        P(None, both),
        P(both, None),
        P(both, None),
        P(both, None),
        P(both, None),
        P(both),
        P(both),
        P(None, "mp"),
        P("mp"),
        P("mp", None),
        P(both),
        P(both),
        P(both),
    )
    return jax.shard_map(shards, mesh=mesh, in_specs=in_specs, out_specs=out_specs, check_vma=False)
```

```python
import functools

import jax
import jax.numpy as jnp
from jax import lax
from jax.experimental import pallas as pl
from jax.experimental.pallas import tpu as pltpu
from jax.sharding import PartitionSpec as P

D = 512
HEADS = 8
HEAD = 64
MEM = 20
PAD = 32
SPAN = 512
SPANS = 2
EXTRA = 128
WIDE = 4 * D + EXTRA
EPS = 1e-05
GELU_A = 0.7978845608028654
GELU_B = 0.044715
LOW = jnp.bfloat16
F32 = jnp.float32
SCALE = HEAD ** (-0.5)
ALL = ("dp", "mp")

VMEM = pl.BlockSpec(memory_space=pltpu.VMEM)
SMEM = pl.BlockSpec(memory_space=pltpu.SMEM)
ANY = pl.BlockSpec(memory_space=pl.ANY)


def dg(a, b, ca, cb):
    return lax.dot_general(a, b, (((ca,), (cb,)), ((), ())), preferred_element_type=F32)


def iota(shape, dim):
    return lax.broadcasted_iota(jnp.int32, shape, dim)


def head_mask(heads):
    shape = (heads * PAD, heads * HEAD)
    return (iota(shape, 0) >> 5) == (iota(shape, 1) >> 6)


def block_diagonal(rows):
    heads = rows.shape[1] // HEAD
    tall = jnp.concatenate([rows] * heads, axis=0)
    return jnp.where(head_mask(heads), tall, 0.0).astype(LOW)


def diagonal_sum(tall):
    heads = tall.shape[1] // HEAD
    kept = jnp.where(head_mask(heads), tall, 0.0)
    total = kept[:PAD]
    for h in range(1, heads):
        total = total + kept[h * PAD : (h + 1) * PAD]
    return total


def normalize(values):
    mean = jnp.mean(values, axis=1, keepdims=True)
    center = values - mean
    spread = jnp.mean(center * center, axis=1, keepdims=True)
    inv = lax.rsqrt(spread + EPS)
    return center * inv, inv


def gelu_parts(a):
    sq = a * a
    t = jnp.tanh(a * (GELU_A + (GELU_A * GELU_B) * sq))
    half = 0.5 * (1.0 + t)
    return half, t, sq


def gelu(a):
    half, _, _ = gelu_parts(a)
    return a * half


def call(kernel, out_shape, in_specs, out_specs, scratch=(), flops=1, bytes_=1, mib=32):
    return pl.pallas_call(
        kernel,
        out_shape=out_shape,
        in_specs=in_specs,
        out_specs=out_specs,
        scratch_shapes=list(scratch),
        compiler_params=pltpu.CompilerParams(vmem_limit_bytes=mib * 2**20),
        cost_estimate=pl.CostEstimate(flops=flops, bytes_accessed=bytes_, transcendentals=0),
    )


def sds(shape, dtype):
    return jax.ShapeDtypeStruct(shape, dtype)


def pack_kernel(q_ref, k_ref, v_ref, o_ref, mem_ref, g1_ref, b1_ref, ob_ref, g2_ref, b2_ref, out_ref, tall):
    rows = q_ref.shape[0]
    for i, ref in enumerate((q_ref, k_ref, v_ref, o_ref)):
        out_ref[:, i * D : (i + 1) * D] = ref[...]
    tall[...] = jnp.zeros(tall.shape, F32)
    for i, ref in enumerate((g1_ref, b1_ref, ob_ref, g2_ref, b2_ref)):
        tall[MEM + i : MEM + i + 1, :rows] = ref[...].astype(F32)
    out_ref[:, 4 * D :] = tall[...].T[:rows].astype(LOW)
    out_ref[:, 4 * D : 4 * D + MEM] = mem_ref[...]


def assemble(me, pieces, bits, out_ref):
    for piece, offsets in zip(pieces, bits, strict=True):
        if offsets is None:
            out_ref[...] = piece[...]
            continue
        size = piece.shape[0] // len(offsets)
        for j, offset in enumerate(offsets):
            start = pl.multiple_of((me ^ offset) * size, size)
            out_ref[pl.ds(start, size), :] = piece[j * size : (j + 1) * size, :]


def project_kernel(bits, at_ref, *refs):
    n = len(bits)
    x_ref, w_ref, qkv_ref = refs[n:]
    assemble(at_ref[0], refs[:n], bits, w_ref)
    x_t = x_ref[...].T
    qkv_ref[:D] = (dg(w_ref[:, :D], x_t, 0, 0).astype(LOW).astype(F32) * SCALE).astype(LOW)
    qkv_ref[D : 3 * D] = dg(w_ref[:, D : 3 * D], x_t, 0, 0).astype(LOW)


def attend_kernel(qkv_ref, p_ref, o_ref, m_ref, l_ref):
    def scores(h):
        at = h * HEAD
        return dg(qkv_ref[D + at : D + at + HEAD], qkv_ref[at : at + HEAD], 0, 0)

    s_next = scores(0)
    for h in range(HEADS):
        s = s_next
        if h + 1 < HEADS:
            s_next = scores(h + 1)
        at = h * HEAD
        m = jnp.max(s, axis=0, keepdims=True)
        p = jnp.exp(s - m)
        m_ref[h : h + 1] = m
        l_ref[h : h + 1] = jnp.sum(p, axis=0, keepdims=True)
        p_ref[h] = p.astype(LOW)
        o_ref[at : at + HEAD] = dg(qkv_ref[2 * D + at : 2 * D + at + HEAD], p_ref[h], 1, 0)


def memory_kernel(x1_ref, w_ref, nm_ref, small_ref):
    small = w_ref[:, 4 * D :].T.astype(F32)[:PAD]
    small_ref[...] = small
    mem = jnp.where(iota((PAD, D), 0) < MEM, small, 0.0)
    packed = dg(mem.astype(LOW), w_ref[:, : 3 * D], 1, 0).astype(LOW)
    q_tall = block_diagonal(packed[:, :D].astype(F32) * SCALE)
    s_mem = dg(q_tall, packed[:, D : 2 * D], 1, 1)
    s_mem = jnp.where(iota(s_mem.shape, 1) < MEM, s_mem, -1e30)
    kv = dg(x1_ref[...], w_ref[:, D : 3 * D], 1, 0).astype(LOW)
    s = dg(q_tall, kv[:, :D], 1, 1)
    m = jnp.maximum(jnp.max(s, axis=1, keepdims=True), jnp.max(s_mem, axis=1, keepdims=True))
    p = jnp.exp(s - m)
    p_mem = jnp.exp(s_mem - m)
    total = jnp.sum(p, axis=1, keepdims=True) + jnp.sum(p_mem, axis=1, keepdims=True)
    o = dg(p.astype(LOW), kv[:, D:], 1, 0) + dg(p_mem.astype(LOW), packed[:, 2 * D :], 1, 0)
    mixed = diagonal_sum(o / total).astype(LOW)
    xhat, _ = normalize(mem + dg(mixed, w_ref[:, 3 * D : 4 * D], 1, 0))
    nm_ref[...] = xhat * small[MEM : MEM + 1] + small[MEM + 1 : MEM + 2]


def forward_kernel(
    at_ref, nm_ref, small_ref, x_ref, w_ref, qkv_ref, o_ref, m_ref, l_ref,
    wi0, wi1, wi2, wi3, wo0, wo1, wo2, wo3, cot_ref,
    out_ref, keep_ref, send_ref, slope_ref, nl_ref, gl_ref, gs_ref, xhat_ref, inv_ref,
    mixed_ref, mem_ref, kv_ref, pm_ref, c_ref, cm_ref, vec_ref, hid,
):
    wis, wos = (wi0, wi1, wi2, wi3), (wo0, wo1, wo2, wo3)
    shifts = [ref[D : D + 1].astype(F32) for ref in wos]
    small = small_ref[...]
    gain1, bias1, outer_b, gain2, bias2 = (small[MEM + i : MEM + i + 1] for i in range(5))
    later, first = at_ref[2], at_ref[5]
    nm = nm_ref[...]
    nm_low = nm.astype(LOW)
    value = nm + outer_b
    for k in range(4):
        inner = dg(nm_low, wis[k][...], 1, 0) + shifts[k]
        value = value + dg(gelu(inner).astype(LOW), wos[k][:D], 1, 0)
    carried, _ = normalize(value)
    carried = carried * gain2 + bias2
    mem = jnp.where(later == 1, carried, small)
    mem = jnp.where(iota((PAD, D), 0) < MEM, mem, 0.0)
    mem_ref[...] = mem
    kv_mem = dg(mem.astype(LOW), w_ref[:, D : 3 * D], 1, 0).astype(LOW)
    kv_ref[...] = kv_mem
    k_tall = block_diagonal(kv_mem[:, :D].astype(F32))
    v_tall = block_diagonal(kv_mem[:, D:].astype(F32))
    s_all = dg(k_tall, qkv_ref[:D], 1, 0)
    s_all = jnp.where((iota(s_all.shape, 0) & (PAD - 1)) < MEM, s_all, -1e30)
    alphas, invs = [], []
    for h in range(HEADS):
        s = s_all[h * PAD : (h + 1) * PAD]
        m_old = m_ref[h : h + 1]
        m = jnp.maximum(m_old, jnp.max(s, axis=0, keepdims=True))
        alpha = jnp.exp(m_old - m)
        p = jnp.exp(s - m)
        inv = 1.0 / (l_ref[h : h + 1] * alpha + jnp.sum(p, axis=0, keepdims=True))
        pm_ref[h * PAD : (h + 1) * PAD] = p.astype(LOW)
        c_ref[h : h + 1] = alpha * inv
        cm_ref[h : h + 1] = inv
        alphas.append(alpha * inv)
        invs.append(inv)
    o_mem = dg(v_tall, pm_ref[...], 0, 0)
    for h in range(HEADS):
        at = h * HEAD
        mixed_ref[at : at + HEAD] = (
            o_ref[at : at + HEAD] * alphas[h] + o_mem[at : at + HEAD] * invs[h]
        ).astype(LOW)
    xhat1, inv1 = normalize(
        x_ref[...].astype(F32) + dg(mixed_ref[...], w_ref[:, 3 * D : 4 * D], 0, 0)
    )
    xhat_ref[...] = xhat1
    inv_ref[...] = inv1
    normed = xhat1 * gain1 + bias1
    normed_low = normed.astype(LOW)
    nl_ref[...] = normed_low
    total = normed + outer_b
    for k in range(4):
        a = dg(normed_low, wis[k][...], 1, 0) + shifts[k]
        half, t, sq = gelu_parts(a)
        hid[k] = (a * half).astype(LOW)
        slope = half + (0.5 * a) * (1.0 - t * t) * (GELU_A + (3.0 * GELU_A * GELU_B) * sq)
        slope_ref[k] = slope.astype(LOW)
        total = total + dg(hid[k], wos[k][:D], 1, 0)
    xhat2, inv2 = normalize(total)
    out_ref[...] = (xhat2 * gain2 + bias2).astype(LOW)
    cot = cot_ref[...].astype(F32)
    pull = cot * gain2
    grad_sum = inv2 * (
        pull
        - jnp.mean(pull, axis=1, keepdims=True)
        - xhat2 * jnp.mean(pull * xhat2, axis=1, keepdims=True)
    )
    vec_ref[2:3] = jnp.sum(grad_sum, axis=0, keepdims=True)
    vec_ref[3:4] = jnp.sum(cot * xhat2, axis=0, keepdims=True)
    vec_ref[4:5] = jnp.sum(cot, axis=0, keepdims=True)
    gs_ref[...] = grad_sum
    grad_low = grad_sum.astype(LOW)
    gl_ref[...] = grad_low
    for k in (1, 3, 0, 2):
        give(send_ref if k % 2 else keep_ref, k // 2, dg(hid[k], grad_low, 0, 0), first)


def give(ref, k, rows, first):
    size = rows.shape[0] // 4
    for i in range(4):
        ref[k, first ^ i] = rows[i * size : (i + 1) * size].astype(LOW)


def inner_terms(k, wi_ref, wo_ref, slope_ref, normed_low, grad_low, ref, first):
    gi = slope_ref[k].astype(F32) * dg(grad_low, wo_ref[:D], 1, 1)
    gi_low = gi.astype(LOW)
    bias = jnp.sum(gi_low.astype(F32), axis=0, keepdims=True)
    bias = jnp.where(iota((PAD, D), 0) == 0, bias, 0.0)
    rows = jnp.concatenate([dg(normed_low, gi_low, 0, 0), bias], axis=0)
    give(ref, k // 2, rows, first)
    return dg(gi_low, wi_ref[...], 1, 1)


def send_kernel(at_ref, wi1, wi3, wo1, wo3, slope_ref, nl_ref, gl_ref, gs_ref, send_ref, back_ref):
    first = at_ref[5]
    back = gs_ref[...]
    for k, wi_ref, wo_ref in ((1, wi1, wo1), (3, wi3, wo3)):
        back = back + inner_terms(k, wi_ref, wo_ref, slope_ref, nl_ref[...], gl_ref[...], send_ref, first)
    back_ref[...] = back


def keep_kernel(at_ref, after_ref, wi0, wi2, wo0, wo2, slope_ref, nl_ref, gl_ref, back_ref, keep_ref, sum_ref):
    first = at_ref[5]
    back = back_ref[...]
    for k, wi_ref, wo_ref in ((0, wi0, wo0), (2, wi2, wo2)):
        back = back + inner_terms(k, wi_ref, wo_ref, slope_ref, nl_ref[...], gl_ref[...], keep_ref, first)
    sum_ref[...] = back


def resid_kernel(back_ref, small_ref, w_ref, xhat_ref, inv_ref, mixed_ref, resid_ref, dwo_ref, gmix_ref, vec_ref):
    back = back_ref[...]
    xhat1 = xhat_ref[...]
    vec_ref[0:1] = jnp.sum(back * xhat1, axis=0, keepdims=True)
    vec_ref[1:2] = jnp.sum(back, axis=0, keepdims=True)
    pull = back * small_ref[MEM : MEM + 1]
    resid = inv_ref[...] * (
        pull
        - jnp.mean(pull, axis=1, keepdims=True)
        - xhat1 * jnp.mean(pull * xhat1, axis=1, keepdims=True)
    )
    resid_ref[...] = resid
    resid_low = resid.astype(LOW)
    dwo_ref[...] = dg(mixed_ref[...], resid_low, 1, 0).astype(LOW)
    gmix_ref[...] = dg(w_ref[:, 3 * D : 4 * D], resid_low, 1, 1).astype(LOW)


def heads_kernel(
    low_h, high_h, after_ref, qkv_ref, p_ref, pm_ref, mixed_ref, c_ref, cm_ref, gmix_ref, kv_ref, gp_ref, gm_ref,
    do_m, ds_m,
):
    heads = range(low_h, high_h)
    f0, f1 = low_h * HEAD, high_h * HEAD
    m0, m1 = low_h * PAD, high_h * PAD
    k_tall = block_diagonal(kv_ref[:, f0:f1].astype(F32))
    v_tall = block_diagonal(kv_ref[:, D + f0 : D + f1].astype(F32))
    deltas = []
    for i, h in enumerate(heads):
        at = h * HEAD
        do = gmix_ref[at : at + HEAD].astype(F32)
        deltas.append(
            jnp.sum(do * mixed_ref[at : at + HEAD].astype(F32), axis=0, keepdims=True)
        )
        do_m[i * HEAD : (i + 1) * HEAD] = (do * cm_ref[h : h + 1]).astype(LOW)
    da_m = dg(v_tall, do_m[...], 1, 0)
    for i, h in enumerate(heads):
        rows = slice(i * PAD, (i + 1) * PAD)
        p = pm_ref[h * PAD : (h + 1) * PAD].astype(F32)
        ds_m[rows] = (p * (da_m[rows] - deltas[i] * cm_ref[h : h + 1])).astype(LOW)
    gm_ref[0] = diagonal_sum(dg(ds_m[...], qkv_ref[f0:f1], 1, 1))
    gm_ref[1] = diagonal_sum(dg(pm_ref[m0:m1], do_m[...], 1, 1))
    dq_mem = dg(k_tall, ds_m[...], 0, 0)
    for i, h in enumerate(heads):
        at = h * HEAD
        rows = slice(i * HEAD, (i + 1) * HEAD)
        c = c_ref[h : h + 1]
        do = (gmix_ref[at : at + HEAD].astype(F32) * c).astype(LOW)
        p = p_ref[h]
        da = dg(qkv_ref[2 * D + at : 2 * D + at + HEAD], do, 0, 0)
        ds = (p.astype(F32) * (da - deltas[i] * c)).astype(LOW)
        gp_ref[2, rows] = dg(do, p, 1, 1).astype(LOW)
        gp_ref[1, rows] = dg(qkv_ref[at : at + HEAD], ds, 1, 1).astype(LOW)
        gp_ref[0, rows] = (
            SCALE * (dg(qkv_ref[D + at : D + at + HEAD], ds, 1, 0) + dq_mem[rows])
        ).astype(LOW)


def weights_kernel(
    bits, after_ref, at_ref, x_ref, w_ref, mem_ref, gp0_ref, gp1_ref, gm0_ref, gm1_ref, dwo_ref, vec_ref, vec1_ref, *rest
):
    g_refs, wext = rest[: len(bits)], rest[len(bits)]
    me = at_ref[0]
    mem_low = mem_ref[...].astype(LOW)
    x_t = x_ref[...].T
    width = gp0_ref.shape[1]
    for part, (gp_ref, gm_ref) in enumerate(((gp0_ref, gm0_ref), (gp1_ref, gm1_ref))):
        for i in range(3):
            grad = dg(x_t, gp_ref[i], 1, 1)
            if i > 0:
                grad = grad + dg(mem_low, gm_ref[i - 1].astype(LOW), 0, 0)
            at = i * D + part * width
            wext[:, at : at + width] = grad.astype(LOW)
    wext[:, 3 * D : 4 * D] = dwo_ref[...]
    gp_mem = jnp.concatenate([gm0_ref[0], gm1_ref[0], gm0_ref[1], gm1_ref[1]], axis=1).astype(LOW)
    g_mem = dg(gp_mem, w_ref[:, D : 3 * D], 1, 1)
    g_mem = jnp.where(at_ref[2] == 0, g_mem, 0.0)
    row = iota((EXTRA, D), 0)
    tall = jnp.concatenate([g_mem, jnp.zeros((EXTRA - PAD, D), F32)], axis=0)
    tall = jnp.where(row < MEM, tall, 0.0)
    for i in range(5):
        tall = jnp.where(row == MEM + i, (vec1_ref if i < 2 else vec_ref)[i : i + 1], tall)
    wext[:, 4 * D :] = tall.T.astype(LOW)
    for g_ref, offsets in zip(g_refs, bits, strict=True):
        if offsets is None:
            g_ref[...] = wext[...]
            continue
        size = g_ref.shape[0] // len(offsets)
        for j, offset in enumerate(offsets):
            start = pl.multiple_of((me ^ offset) * size, size)
            g_ref[j * size : (j + 1) * size] = wext[pl.ds(start, size), :]


def tokens_kernel(after_ref, w_ref, gp0_ref, gp1_ref, resid_ref, tok_ref):
    width = gp0_ref.shape[1]
    total = jnp.zeros((D, SPAN), F32)
    for part, gp_ref in enumerate((gp0_ref, gp1_ref)):
        for i in range(3):
            at = i * D + part * width
            total = total + dg(w_ref[:, at : at + width], gp_ref[i], 1, 0)
    tok_ref[...] = (total.T + resid_ref[...]).astype(LOW)


def place_kernel(at_ref, r0, r1, r2, r3, out_ref, sems):
    me = at_ref[3]
    copies = [pltpu.make_async_copy(ref, out_ref.at[me ^ k], sems.at[k]) for k, ref in enumerate((r0, r1, r2, r3))]
    for copy in copies:
        copy.start()
    for copy in copies:
        copy.wait()


def place(at, pieces):
    rows = call(
        place_kernel,
        sds((4,) + pieces[0].shape, pieces[0].dtype),
        [SMEM] + [VMEM] * 4,
        ANY,
        [pltpu.SemaphoreType.DMA((4,))],
        mib=8,
    )(at, *pieces)
    return rows.reshape(-1, D)


def finish_kernel(at_ref, own_ref, other_ref, out_ref, bias_ref, held):
    first = at_ref[5]
    size = own_ref.shape[1]
    for i, ref in enumerate((own_ref, other_ref)):
        for j in range(2):
            start = pl.multiple_of((first ^ (2 * i + j)) * size, size)
            held[pl.ds(start, size), :] = ref[j].astype(F32)
    out_ref[...] = held[:D]
    bias_ref[...] = held[held.shape[0] - PAD : held.shape[0] - PAD + 1]


def closing_kernel(at_ref, r0, r1, r2, r3, own_ref, other_ref, mine_ref, got_ref, rows_ref, out_ref, *rest):
    memory_ref, *square_refs, held, sems = rest
    squares, vectors = square_refs[:4], square_refs[4:]
    me, first = at_ref[3], at_ref[5]
    copies = [pltpu.make_async_copy(ref, rows_ref.at[me ^ k], sems.at[k]) for k, ref in enumerate((r0, r1, r2, r3))]
    for copy in copies:
        copy.start()
    size = own_ref.shape[1]
    for i, ref in enumerate((own_ref, other_ref)):
        for j in range(2):
            start = pl.multiple_of((first ^ (2 * i + j)) * size, size)
            out_ref[pl.ds(start, size), :] = ref[j].astype(F32)
    total = mine_ref[0].astype(F32) + got_ref[0].astype(F32)
    for i, ref in enumerate(squares):
        ref[...] = total[:, i * D : (i + 1) * D]
    memory_ref[...] = total[:, 4 * D : 4 * D + MEM]
    held[...] = jnp.zeros(held.shape, F32)
    held[: total.shape[0]] = total[:, 4 * D :]
    tall = held[...].T
    for i, ref in enumerate(vectors):
        ref[...] = tall[MEM + i : MEM + i + 1, : total.shape[0]]
    for copy in copies:
        copy.wait()


def closing(at, rows, pair, other, mine, got):
    n = mine.shape[1]
    shapes = [sds((4,) + rows[0].shape, LOW), sds((D, D), F32), sds((n, MEM), F32)]
    shapes += [sds((n, D), F32)] * 4 + [sds((1, n), F32)] * 5
    grad_tokens, grad_outer, grad_memory, *others = call(
        closing_kernel,
        shapes,
        [SMEM] + [VMEM] * 8,
        [ANY] + [VMEM] * (len(shapes) - 1),
        [pltpu.VMEM((EXTRA, EXTRA), F32), pltpu.SemaphoreType.DMA((4,))],
        mib=16,
    )(at, *rows, pair, other, mine, got)
    vectors = [v.reshape(-1) for v in others[4:]]
    return grad_tokens.reshape(-1, D), grad_outer, [grad_memory.T, *others[:4], *vectors]


def swap(value, axis, bit):
    n = lax.axis_size(axis)
    return lax.ppermute(value, axis, [(i, i ^ bit) for i in range(n)])


def tie(*values):
    return lax.optimization_barrier(values)


def add_low(*terms):
    return functools.reduce(jnp.add, [t.astype(F32) for t in terms]).astype(LOW)


def finish(at, pair, other):
    grad, bias = call(
        finish_kernel,
        [sds((D, D), F32), sds((1, D), F32)],
        [SMEM] + [VMEM] * 2,
        [VMEM] * 2,
        [pltpu.VMEM((4 * pair.shape[1], D), F32)],
        bytes_=2 * 2**20,
    )(at, pair, other)
    return grad, bias[0]


def split(reduced):
    reduced = reduced.reshape(-1, WIDE)
    squares = [reduced[:, i * D : (i + 1) * D] for i in range(4)]
    vectors = [reduced[:, 4 * D + MEM + i] for i in range(5)]
    return [reduced[:, 4 * D : 4 * D + MEM].T, *squares, *vectors]


def shards(
    tokens, cotangent, memory_init, query_weight, key_weight, value_weight, output_weight, first_gain,
    first_bias, inner_weight, inner_bias, outer_weight, outer_bias, second_gain, second_bias,
):
    n_dp, n_mp = lax.axis_size("dp"), lax.axis_size("mp")
    rows_each = query_weight.shape[0]
    by_bits = n_dp == 8 and n_mp == 4 and rows_each % 16 == 0
    me_mp, me_dp = lax.axis_index("mp"), lax.axis_index("dp")
    me = me_dp * n_mp + me_mp
    later = me_mp % SPANS
    x = (me_dp & 1) if by_bits else 0
    first = (x * 2 + ((me_dp >> 1) & 1)) if by_bits else 0
    at = jnp.stack([me, me_mp // SPANS, later, me_mp, me_dp, first, x]).astype(jnp.int32)

    pick = lambda v, i: lax.dynamic_index_in_dim(v, i, 0, keepdims=False)
    blocks = tokens.reshape(-1, SPAN, D)
    own = pick(blocks, me_mp)
    start = pick(blocks, me_mp - later)
    cot = pick(cotangent.reshape(-1, SPAN, D), me_mp)

    wi_halves = inner_weight.reshape(2, D // 2, D)
    z = ((me_dp >> 1) & 1) if by_bits else 0
    wi_near = swap(pick(wi_halves, z), "mp", 2)
    outer_rows = jnp.concatenate([outer_weight, inner_bias.reshape(1, -1), jnp.zeros((15, D), LOW)], axis=0)

    vectors = (first_gain, first_bias, outer_bias, second_gain, second_bias)
    local = call(
        pack_kernel,
        sds((rows_each, WIDE), LOW),
        [VMEM] * 10,
        VMEM,
        [pltpu.VMEM((EXTRA, EXTRA), F32)],
        mib=56,
    )(query_weight, key_weight, value_weight, output_weight, memory_init.T, *[v.reshape(1, -1) for v in vectors])
    z = ((me_dp >> 1) & 1) if by_bits else 0
    wo_halves = outer_weight.reshape(2, D // 2, D)
    wo_near = swap(jnp.concatenate([pick(wo_halves, z), outer_rows[D:]]), "mp", 2)
    if by_bits:
        line = [local] + [swap(local, ALL, 8 * j) for j in range(1, 4)]
        *line, wi_near = tie(*line, wi_near)
        wi_far = swap(wi_near, "dp", 2)
        line = jnp.concatenate(line, axis=0)
        plane = [line] + [swap(line, ALL, 2 * b) for b in range(1, 4)]
        wi2 = jnp.where(z == 0, jnp.concatenate([wi_near, wi_far]), jnp.concatenate([wi_far, wi_near]))
        wo_far = swap(wo_near, "dp", 2)
        top, bottom, biases = wo_near[: D // 2], wo_far[: D // 2], wo_near[D // 2 :]
        wo2 = jnp.where(z == 0, jnp.concatenate([top, bottom, biases]), jnp.concatenate([bottom, top, biases]))
        plane[2], own, start, cot = tie(plane[2], own, start, cot)
        *plane, wo2, wi2 = tie(*plane, wo2, wi2)
        pieces = plane + [swap(piece, ALL, 1) for piece in plane]
        bits = [[2 * b + c + 8 * j for j in range(4)] for c in range(2) for b in range(4)]
    else:
        pieces = [lax.all_gather(local, ALL, axis=0, tiled=True)]
        bits = [None]
        wi2 = jnp.concatenate([wi_near, swap(wi_halves[1], "mp", 2)])
        wo2 = jnp.concatenate([wo_near[: D // 2], swap(wo_halves[1], "mp", 2), wo_near[D // 2 :]])
    wi1, wo1, wi3, wo3 = [swap(v, "mp", 1) for v in (inner_weight, outer_rows, wi2, wo2)]

    w, qkv = call(
        functools.partial(project_kernel, bits),
        [sds((D, WIDE), LOW), sds((3 * D, SPAN), LOW)],
        [SMEM] + [VMEM] * (len(pieces) + 1),
        [VMEM] * 2,
        flops=2 * 10**9,
        bytes_=5 * 2**20,
    )(at, *pieces, own)
    p, o, m, l = call(
        attend_kernel,
        [
            sds((HEADS, SPAN, SPAN), LOW),
            sds((D, SPAN), F32),
            sds((HEADS, SPAN), F32),
            sds((HEADS, SPAN), F32),
        ],
        [VMEM],
        [VMEM] * 4,
        flops=5 * 10**9,
        bytes_=7 * 2**20,
    )(qkv)

    nm, small = call(
        memory_kernel,
        [sds((PAD, D), F32), sds((PAD, D), F32)],
        [VMEM] * 2,
        [VMEM] * 2,
        flops=3 * 10**9,
        bytes_=4 * 2**20,
        mib=16,
    )(start, w)
    nm, m, wi1, wi3, wo1, wo3 = tie(nm, m, wi1, wi3, wo1, wo3)

    outer_shape = sds((2, 4, D // 4, D), LOW)
    inner_shape = sds((2, 4, (D + PAD) // 4, D), LOW)
    square, square_low = sds((SPAN, D), F32), sds((SPAN, D), LOW)
    (
        out, outer_keep, outer_send, slope, normed, grad_low, grad_sum, xhat, inv, mixed, mem, kv_mem, p_mem, c, c_mem, vecs,
    ) = call(
        forward_kernel,
        [
            square_low,
            outer_shape,
            outer_shape,
            sds((4, SPAN, D), LOW),
            square_low,
            square_low,
            square,
            square,
            sds((SPAN, 1), F32),
            sds((D, SPAN), LOW),
            sds((PAD, D), F32),
            sds((PAD, 2 * D), LOW),
            sds((HEADS * PAD, SPAN), LOW),
            sds((HEADS, SPAN), F32),
            sds((HEADS, SPAN), F32),
            sds((8, D), F32),
        ],
        [SMEM] + [VMEM] * 17,
        [VMEM] * 16,
        [pltpu.VMEM((4, SPAN, D), LOW)],
        flops=10 * 10**9,
        bytes_=14 * 2**20,
    )(
        at, nm, small, own, w, qkv, o, m, l, inner_weight, wi1, wi2, wi3, outer_rows, wo1, wo2, wo3, cot,
    )
    wis, wos = (inner_weight, wi1, wi2, wi3), (outer_rows, wo1, wo2, wo3)

    outer_got = swap(outer_send, "mp", 1)

    inner_send, back = call(
        send_kernel,
        [inner_shape, square],
        [SMEM] + [VMEM] * 8,
        [VMEM] * 2,
    )(at, wis[1], wis[3], wos[1], wos[3], slope, normed, grad_low, grad_sum)
    inner_got = swap(inner_send, "mp", 1)

    outer_mine, outer_give = add_low(outer_keep[0], outer_got[0]), add_low(outer_keep[1], outer_got[1])
    outer_y = swap(outer_give, "mp", 2)

    inner_keep, back = call(
        keep_kernel,
        [inner_shape, square],
        [SMEM, ANY] + [VMEM] * 8,
        [VMEM] * 2,
    )(at, outer_give, wis[0], wis[2], wos[0], wos[2], slope, normed, grad_low, back)
    resid, d_mix, g_mixed, vecs1 = call(
        resid_kernel,
        [square, sds((D, D), LOW), sds((D, SPAN), LOW), sds((8, D), F32)],
        [VMEM] * 6,
        [VMEM] * 4,
    )(back, small, w, xhat, inv, mixed)

    half = HEADS // 2
    some = half * HEAD

    def heads_backward(low_h, gate):
        return call(
            functools.partial(heads_kernel, low_h, low_h + half),
            [sds((3, some, SPAN), LOW), sds((2, PAD, some), F32)],
            [ANY] + [VMEM] * 8,
            [VMEM] * 2,
            [
                pltpu.VMEM((some, SPAN), LOW),
                pltpu.VMEM((half * PAD, SPAN), LOW),
            ],
        )(gate, qkv, p, p_mem, mixed, c, c_mem, g_mixed, kv_mem)

    if by_bits:
        inner_give = add_low(inner_keep[:, 2:], inner_got[:, 2:])
        inner_mine = add_low(inner_keep[:, :2], inner_got[:, :2])
        inner_x = swap(inner_give, "dp", 1)
    else:
        inner_give = inner_got
    gp0, gm0 = heads_backward(0, inner_give)
    gp1, gm1 = heads_backward(half, inner_give)

    if by_bits:
        out_bits = [[[4 * (b >> 1) + 8 * (b & 1) + c + j for j in (0, 16, 2, 18)] for b in range(4)] for c in range(2)]
        out_bits = [sum(out_bits[0], []), *out_bits[1]]
    else:
        out_bits = [None]

    def weights_backward(gate):
        return call(
            functools.partial(weights_kernel, out_bits),
            [sds((len(o) * rows_each if o else D, WIDE), LOW) for o in out_bits],
            [ANY, SMEM] + [VMEM] * 10,
            [VMEM] * len(out_bits),
            [pltpu.VMEM((D, WIDE), LOW)],
        )(gate, at, own, w, mem, gp0, gp1, gm0, gm1, d_mix, vecs, vecs1)

    def tokens_backward(gate):
        return call(tokens_kernel, sds((SPAN, D), LOW), [ANY] + [VMEM] * 4, VMEM)(gate, w, gp0, gp1, resid)

    if by_bits:
        halves_of = lambda v: (v[: v.shape[0] // 2], v[v.shape[0] // 2 :])
        both = lambda mine, got: [add_low(u, v) for u, v in zip(halves_of(mine), halves_of(got), strict=True)]

        grad_rows = tokens_backward(inner_give)
        rows_got = swap(grad_rows, "mp", 1)

        a_mine, *a_give = [g.reshape(-1, rows_each, WIDE) for g in weights_backward(inner_give)]
        a_got = [swap(g, ALL, 1) for g in a_give]

        outer_y, grad_rows, a_mine = tie(outer_y, grad_rows, a_mine)
        q_mine, q_give = both(outer_mine, outer_y)
        q_got = swap(q_give, "dp", 1)

        inner_x, q_mine = tie(inner_x, q_mine)
        p_mine, p_give = add_low(inner_mine[0], inner_x[0]), add_low(inner_mine[1], inner_x[1])
        p_got = swap(p_give, "mp", 2)

        *a_got, p_mine = tie(*a_got, p_mine)
        a_mine, a_give = both(a_mine, jnp.concatenate(a_got))
        a_got = swap(a_give, ALL, 4)

        q_got, a_mine = tie(q_got, a_mine)
        q_mine, q_give = [v[0] for v in both(q_mine, q_got)]
        q_got = swap(q_give, "dp", 2)

        grad_rows, q_mine = tie(grad_rows, q_mine)
        rows_across = swap(grad_rows, "mp", 2)

        p_got, grad_rows = tie(p_got, grad_rows)
        p_mine, p_give = [v[0] for v in both(p_mine, p_got)]
        p_got = swap(p_give, "dp", 2)

        q_got, p_mine = tie(q_got, p_mine)
        q_mine = add_low(q_mine, q_got)
        q_got = swap(q_mine, "dp", 4)

        out, q_mine = tie(out, q_mine)
        out_got, out_across = swap(out, "mp", 1), swap(out, "mp", 2)

        p_got, out = tie(p_got, out)
        p_mine = add_low(p_mine, p_got)
        p_got = swap(p_mine, "dp", 4)

        a_got, p_mine = tie(a_got, p_mine)
        a_mine, a_give = both(a_mine, a_got)
        a_got = swap(a_give, ALL, 8)

        q_got, a_mine = tie(q_got, a_mine)
        q_mine = add_low(q_mine, q_got)
        q_got = swap(q_mine, "dp", 2)

        rows_across, q_mine = tie(rows_across, q_mine)
        rows_last = swap(rows_across, "mp", 1)

        a_got, rows_across = tie(a_got, rows_across)
        a_mine, a_give = both(a_mine, a_got)
        a_got = swap(a_give, ALL, 2)

        p_got, a_mine = tie(p_got, a_mine)
        p_mine = add_low(p_mine, p_got)
        p_got = swap(p_mine, "dp", 2)

        q_got, p_mine = tie(q_got, p_mine)
        q_pair = jnp.stack([q_mine, q_got])
        q_got = swap(q_pair, "dp", 1)

        out_across, q_pair = tie(out_across, q_pair)
        out_last = swap(out_across, "mp", 1)

        p_got, out_across = tie(p_got, out_across)
        p_pair = jnp.stack([p_mine, p_got])
        p_got = swap(p_pair, "dp", 1)

        a_got, p_pair = tie(a_got, p_pair)
        a_mine, a_give = both(a_mine, a_got)
        a_got = swap(a_give, ALL, 16)

        out_last, a_mine = tie(out_last, a_mine)
        layer_out = place(at, [out, out_got, out_across, out_last])

        rows_last, q_got, a_got, layer_out = tie(rows_last, q_got, a_got, layer_out)
        rows = [grad_rows, rows_got, rows_across, rows_last]
        grad_tokens, grad_outer, outputs = closing(at, rows, q_pair, q_got, a_mine, a_got)

        p_got, grad_outer = tie(p_got, grad_outer)
        grad_inner, grad_inner_bias = finish(at, p_pair, p_got)
    else:
        grad_outer = lax.psum(outer_mine.astype(F32) + outer_y.astype(F32), "dp").reshape(-1, D)
        grad_rows = tokens_backward(inner_give)
        grads = weights_backward(inner_give)
        inner = add_low(inner_keep, inner_got)
        layer_out = lax.all_gather(out, "mp", axis=0, tiled=True)
        grad_tokens = lax.all_gather(grad_rows, "mp", axis=0, tiled=True)
        inner = lax.psum(inner[0].astype(F32) + swap(inner[1], "mp", 2).astype(F32), "dp").reshape(-1, D)
        grad_inner, grad_inner_bias = inner[:D], inner[D]
        outputs = split(lax.psum_scatter(grads[0], ALL, scatter_dimension=0, tiled=True).astype(F32))
    grad_memory, grad_query, grad_key, grad_value, grad_output, *grad_vectors = outputs
    return (
        layer_out,
        grad_tokens,
        grad_memory,
        grad_query,
        grad_key,
        grad_value,
        grad_output,
        grad_vectors[0],
        grad_vectors[1],
        grad_inner,
        grad_inner_bias,
        grad_outer,
        *grad_vectors[2:],
    )


def solution(mesh):
    both = ("dp", "mp")
    in_specs = (
        P("dp", None),
        P("dp", None),
        P(None, both),
        P(both, None),
        P(both, None),
        P(both, None),
        P(both, None),
        P(both),
        P(both),
        P(None, "mp"),
        P("mp"),
        P("mp", None),
        P(both),
        P(both),
        P(both),
    )
    out_specs = (
        P("dp", None),
        P("dp", None),
        P(None, both),
        P(both, None),
        P(both, None),
        P(both, None),
        P(both, None),
        P(both),
        P(both),
        P(None, "mp"),
        P("mp"),
        P("mp", None),
        P(both),
        P(both),
        P(both),
    )
    return jax.shard_map(shards, mesh=mesh, in_specs=in_specs, out_specs=out_specs, check_vma=False)
```
